512 devices in a mesh: gx: 16 (over y, x), gy: 32 (over z, core).
Axes of the slice: x: 4, y: 4, z: 16, core: 2. Of those that a mesh axis runs over, the one named last changes fastest.
Arguments:
- probes: bfloat16 [32, 256, 32, 128], P('gx', 'gy'), may hold values from -6 to 6
- leaf_basis: bfloat16 [128, 64], replicated, may hold values from -0.5 to 0.5
- up_transfer: bfloat16 [7, 4, 64, 64], replicated, may hold values from -0.375 to 0.375
- down_transfer: bfloat16 [7, 4, 64, 64], replicated, may hold values from -0.75 to 0.75
- coupling: bfloat16 [8, 40, 64, 64], replicated, may hold values from -0.15625 to 0.15625
- far_ids: int32 [8, 4, 27], replicated, may hold values from 0 to 39
Outputs:
- product: bfloat16 [32, 256, 32, 128], P('gx', 'gy')
The draws below stay inside these ranges and needn't reach their ends.
Inputs may be any that keep to these rules, and one draw needn't show every extreme that they name: `far_ids`: each entry picks one of the 40 coupling matrices of its level.
All inputs are finite; a program needn't handle non-finite values.
Results may differ from the reference program's by a relative error of at most 0.012.
Values may be sent and summed in bfloat16 or wider, within the bound.
No kernel may reach another device: no remote copies, remote signals or barrier semaphores. Data moves between devices by JAX's collectives and lax.ppermute only.
A program may use at most 128 MiB of HBM per device.

```python
import jax
import jax.numpy as jnp
from jax import lax

LEAF_ROWS = 8
LEAF_COLS = 16
LEAF = 128
RANK = 64
PROBES = 32
LEVELS = 8
NCOUP = 40
SLOTS = 27
GX = 32
GY = 256


def set_ends(array, key, low, high):
    shape = array.shape
    spot = [jax.random.randint(jax.random.fold_in(key, axis), (), 0, shape[axis]) for axis in range(len(shape))]
    array = array.at[tuple(spot)].set(low)
    longest = shape.index(max(shape))
    spot[longest] = (spot[longest] + 1) % shape[longest]
    return array.at[tuple(spot)].set(high)


def shard_levels(key, extent, shards, smallest, top_value):
    loudness = 1.0
    for axis_at, shards_of in shards:
        heights = jax.random.uniform(jax.random.fold_in(jax.random.fold_in(key, 6), axis_at), (shards_of,), jnp.float32, smallest / len(shards), top_value / len(shards))
        loudness = loudness * jnp.repeat(jnp.exp(heights), extent[axis_at] // shards_of).reshape((-1,) + (1,) * (len(extent) - 1 - axis_at))
    return loudness


def scatter_about(key, extent, deviation, bound, shards=(), kind=jnp.bfloat16):
    array = deviation * jax.random.normal(key, extent, jnp.float32)
    if shards:
        array = array * shard_levels(key, extent, shards, -0.22, 0.18)
    return jnp.clip(array, -bound, bound).astype(kind)


def setup_inputs(seed: int = 0) -> dict:
    key_list = jax.random.split(jax.random.key(seed), 7)
    return {
        "probes": scatter_about(key_list[0], (GX, GY, PROBES, LEAF), 1.0, 6.0, ((0, 16), (1, 32))),
        "leaf_basis": scatter_about(key_list[1], (LEAF, RANK), LEAF ** -0.5, 0.5),
        "up_transfer": scatter_about(key_list[2], (LEVELS - 1, 4, RANK, RANK), (4 * RANK) ** -0.5, 0.375),
        "down_transfer": scatter_about(key_list[3], (LEVELS - 1, 4, RANK, RANK), RANK ** -0.5, 0.75),
        "coupling": scatter_about(key_list[4], (LEVELS, NCOUP, RANK, RANK), (SLOTS * RANK) ** -0.5, 0.15625),
        "far_ids": set_ends(jax.random.randint(key_list[5], (LEVELS, 4, SLOTS), 0, NCOUP), jax.random.fold_in(key_list[5], 1), 0, NCOUP - 1).astype(jnp.int32),
    }


length_scale = 1.5

def slot_offsets(type_row, type_col):
    offsets = []
    for off_row in range(-2 - type_row, 4 - type_row):
        for off_col in range(-2 - type_col, 4 - type_col):
            if max(abs(off_row), abs(off_col)) > 1:
                offsets.append((off_row, off_col))
    return offsets

def kernel_tables(rows_leaf, cols_leaf):
    points = jnp.arange(rows_leaf * cols_leaf, dtype=jnp.int32)
    point_row = (points // cols_leaf).astype(jnp.float32)
    point_col = (points % cols_leaf).astype(jnp.float32)
    tables = []
    for off_row in (-1, 0, 1):
        for off_col in (-1, 0, 1):
            apart_row = point_row[:, None] + off_row * rows_leaf - point_row[None, :]
            apart_col = point_col[:, None] + off_col * cols_leaf - point_col[None, :]
            scaled = jnp.sqrt(3.0 * (apart_row * apart_row + apart_col * apart_col)) / length_scale
            tables.append(((1.0 + scaled) * jnp.exp(-scaled)).astype(jnp.bfloat16))
    return jnp.stack(tables)

def upward(coeffs, transfer):
    rows_count, cols_count, count_p, rank_size = coeffs.shape
    padded = jnp.pad(coeffs, ((0, rows_count % 2), (0, cols_count % 2), (0, 0), (0, 0)))
    grouped = padded.reshape((rows_count + 1) // 2, 2, (cols_count + 1) // 2, 2, count_p, rank_size).astype(jnp.float32)
    parent_coef = jnp.einsum('iajbpr,abrq->ijpq', grouped, transfer.reshape(2, 2, rank_size, rank_size).astype(jnp.float32))
    return parent_coef.astype(jnp.bfloat16)

def far_field(coeffs, coupling_level, ids_level):
    rows_count, cols_count, count_p, rank_size = coeffs.shape
    padded = jnp.pad(coeffs, ((3, 3), (3, 3), (0, 0), (0, 0)))
    result = jnp.zeros((rows_count, cols_count, count_p, rank_size), jnp.float32)
    for type_row in (0, 1):
        for type_col in (0, 1):
            count_row = (rows_count - type_row + 1) // 2
            count_col = (cols_count - type_col + 1) // 2
            if count_row == 0 or count_col == 0:
                continue
            partial_value = jnp.zeros((count_row, count_col, count_p, rank_size), jnp.float32)
            for slot_index, (off_row, off_col) in enumerate(slot_offsets(type_row, type_col)):
                start_row = type_row + 3 + off_row
                start_col = type_col + 3 + off_col
                sliced = lax.slice(padded, (start_row, start_col, 0, 0), (start_row + 2 * count_row - 1, start_col + 2 * count_col - 1, count_p, rank_size), (2, 2, 1, 1))
                matrix = coupling_level[ids_level[2 * type_row + type_col, slot_index]]
                partial_value = partial_value + jnp.einsum('ijpr,rq->ijpq', sliced.astype(jnp.float32), matrix.astype(jnp.float32))
            result = result.at[type_row::2, type_col::2].set(partial_value)
    return result

def downward(parent, transfer, rows_count, cols_count):
    parent_rows, parent_cols, count_p, rank_size = parent.shape
    spread = jnp.einsum('ijpr,abrq->iajbpq', parent.astype(jnp.float32), transfer.reshape(2, 2, rank_size, rank_size).astype(jnp.float32))
    return spread.reshape(2 * parent_rows, 2 * parent_cols, count_p, rank_size)[:rows_count, :cols_count]

def reference(probes, leaf_basis, up_transfer, down_transfer, coupling, far_ids):
    grid_rows, grid_cols, count_p, leaf_size = probes.shape
    levels = coupling.shape[0]
    basis_wide = leaf_basis.astype(jnp.float32)
    first = jnp.einsum('abpq,qr->abpr', probes.astype(jnp.float32), basis_wide).astype(jnp.bfloat16)
    ladder = [first]
    for height in range(levels - 1):
        ladder.append(upward(ladder[-1], up_transfer[height]))
    carried = None
    for height in reversed(range(levels)):
        summed = far_field(ladder[height], coupling[height], far_ids[height])
        if carried is not None:
            summed = summed + downward(carried, down_transfer[height], ladder[height].shape[0], ladder[height].shape[1])
        carried = summed.astype(jnp.bfloat16)
    tables_wide = kernel_tables(LEAF_ROWS, LEAF_COLS).astype(jnp.float32)
    padded = jnp.pad(probes, ((1, 1), (1, 1), (0, 0), (0, 0)))

    def output_row(row_index):
        sliced = lax.dynamic_slice_in_dim(padded, row_index, 3, 0).astype(jnp.float32)
        summed = jnp.zeros((grid_cols, count_p, leaf_size), jnp.float32)
        for off_row in (-1, 0, 1):
            for off_col in (-1, 0, 1):
                neighbour = sliced[off_row + 1, off_col + 1:off_col + 1 + grid_cols]
                summed = summed + jnp.einsum('bpq,qr->bpr', neighbour, tables_wide[3 * (off_row + 1) + off_col + 1])
        local_row = lax.dynamic_index_in_dim(carried, row_index, 0, keepdims=False).astype(jnp.float32)
        summed = summed + jnp.einsum('bpr,qr->bpq', local_row, basis_wide)
        return summed.astype(jnp.bfloat16)
    return lax.map(output_row, jnp.arange(grid_rows, dtype=jnp.int32))
```

```python
import jax
import jax.numpy as jnp
from jax import lax
from jax.experimental import pallas as pl
from jax.experimental.pallas import tpu as pltpu
from jax.sharding import PartitionSpec as P

LEAF_ROWS = 8
LEAF_COLS = 16
RANK = 64
PROBES = 32
BF = jnp.bfloat16
F32 = jnp.float32

length_scale = 1.5


def dot(left, right):
    return jnp.dot(left, right, preferred_element_type=F32)


def lanes(parts):
    return jnp.concatenate(parts, axis=-1)


def block_slot(e, f, wr, wc):
    return 6 * wr + wc - 3 * min(max(wr - 1 - e, 0), 3) - (
        min(max(wc - 1 - f, 0), 3) if e + 1 <= wr <= e + 3 else 0
    )


def is_near(e, f, wr, wc):
    return e + 1 <= wr <= e + 3 and f + 1 <= wc <= f + 3


def places():
    row = lax.axis_index("gx")
    col = lax.axis_index("gy")
    return row, col, col // 2, col % 2


def prepare_kernel(ids, coupling, w0, w1, w2, w3, w4, w5, table):
    row, col, _, _ = places()

    def pair(level, e, wr, wc):
        halves = []
        for f in (0, 1):
            if is_near(e, f, wr, wc):
                halves.append(jnp.zeros((RANK, RANK), BF))
            else:
                halves.append(coupling[level, ids[level, 2 * e + f, block_slot(e, f, wr, wc)]])
        return lanes(halves)

    for wr in range(6):
        for wc in range(6):
            at = pl.ds((6 * wr + wc) * RANK, RANK)
            for e in (0, 1):
                w0[at, pl.ds(128 * e, 128)] = pair(0, e, wr, wc)

    for level, out, bit in ((1, w1, row % 2), (2, w2, (row // 2) % 2)):
        for e in (0, 1):

            @pl.when(bit == e)
            def _(level=level, out=out, e=e):
                for wr in range(6):
                    for wc in range(6):
                        out[pl.ds((6 * wr + wc) * RANK, RANK), :] = pair(level, e, wr, wc)

    def single(level, e, f, wr, wc):
        row_in = jnp.logical_and(wr >= e + 1, wr <= e + 3)
        col_in = jnp.logical_and(wc >= f + 1, wc <= f + 3)
        skipped = 3 * jnp.clip(wr - 1 - e, 0, 3) + jnp.where(row_in, jnp.clip(wc - 1 - f, 0, 3), 0)
        slot = jnp.clip(6 * wr + wc - skipped, 0, 26)
        keep = jnp.where(jnp.logical_and(row_in, col_in), 0.0, 1.0)
        block = coupling[level, ids[level, 2 * e + f, slot]]
        return block * jnp.full((RANK, RANK), keep, F32).astype(BF)

    e3, f3 = (row // 4) % 2, col % 2
    first3 = 2 - 2 * (row // 8)
    for r in range(4):
        for wc in range(6):
            w3[pl.ds((6 * r + wc) * RANK, RANK), :] = single(3, e3, f3, r + first3, wc)
    e4, f4 = row // 8, (col // 2) % 2
    for wc in range(6):
        for r in range(2):
            w4[pl.ds((2 * wc + r) * RANK, RANK), :] = single(4, e4, f4, jnp.int32(2 + r), wc)
    for level in (5, 6, 7):
        f = (col // (1 << (level - 3))) % 2
        for wc in range(6):
            w5[level - 5, pl.ds(wc * RANK, RANK), :] = single(
                level, jnp.int32(0), f, jnp.int32(2), wc
            )

    size = LEAF_ROWS * LEAF_COLS
    theirs = lax.broadcasted_iota(jnp.int32, (size, size), 0)
    ours = lax.broadcasted_iota(jnp.int32, (size, size), 1)
    rows_apart = (theirs // LEAF_COLS - ours // LEAF_COLS).astype(F32)
    cols_apart = (theirs % LEAF_COLS - ours % LEAF_COLS).astype(F32)
    for u in (-1, 0, 1):
        for v in (-1, 0, 1):
            apart_row = rows_apart + float(u * LEAF_ROWS)
            apart_col = cols_apart + float(v * LEAF_COLS)
            scaled = jnp.sqrt(3.0 * (apart_row * apart_row + apart_col * apart_col)) / length_scale
            value = (1.0 + scaled) * jnp.exp(-scaled)
            table[pl.ds((3 * (u + 1) + v + 1) * size, size), :] = value.astype(BF)


def vmem(shape, kind=BF):
    return jax.ShapeDtypeStruct(shape, kind)


def call(kernel, out_shape, scratch=(), flops=1 << 24, read=1 << 21, **specs):
    return pl.pallas_call(
        kernel,
        out_shape=out_shape,
        **specs,
        scratch_shapes=list(scratch),
        compiler_params=pltpu.CompilerParams(vmem_limit_bytes=48 << 20),
        cost_estimate=pl.CostEstimate(flops=flops, bytes_accessed=read, transcendentals=0),
    )


def pair_basis(basis):
    zero = jnp.zeros_like(basis)
    return jnp.concatenate([lanes([basis, zero]), lanes([zero, basis])], axis=0)


def leaf_coeffs(tile, wide_basis):
    rows = tile.shape[0]
    split = tile.reshape(rows, 4, 2, PROBES, 128)
    joined = lanes([split[:, :, 0], split[:, :, 1]]).reshape(-1, 256)
    return dot(joined, wide_basis).astype(BF).reshape(rows, 4, PROBES, 128)


def to_pairs(nodes):
    lead = nodes.shape[:-3]
    split = nodes.reshape(lead + (nodes.shape[-3] // 2, 2, PROBES, RANK))
    return lanes([split[..., 0, :, :], split[..., 1, :, :]])


def raise_pairs(pairs, transfer):
    rows, count = pairs.shape[:2]
    split = pairs.reshape(rows // 2, 2, count, PROBES, 128)
    joined = lanes([split[:, 0], split[:, 1]]).reshape(-1, 256)
    return dot(joined, transfer).astype(BF).reshape(rows // 2, count, PROBES, RANK)


def first_kernel(own, other, basis, up, sent, mine, others):
    _, _, _, core = places()
    wide = pair_basis(basis[...])
    transfer = up[0].reshape(4 * RANK, RANK)
    for which, tile, kept in ((core, own, mine), (1 - core, other, others)):
        coeffs = leaf_coeffs(tile[...], wide)
        kept[...] = coeffs
        pairs = to_pairs(raise_pairs(coeffs, transfer)[0])
        for peer in range(16):
            sent[peer, pl.ds(2 * which, 2)] = pairs


def second_kernel(
    gathered, own, mine, above, below, basis, up,
    far_out, side_out, third_out, mate_out, rim, level2, level3,
    padded1, padded2,
):
    row, _, _, core = places()
    wide = pair_basis(basis[...])
    pairs2 = to_pairs(raise_pairs(gathered[...], up[1].reshape(4 * RANK, RANK)))
    pairs3 = to_pairs(raise_pairs(pairs2, up[2].reshape(4 * RANK, RANK)))[:, 0]
    nodes4 = raise_pairs(pairs3[:, None], up[3].reshape(4 * RANK, RANK))
    far_out[...] = lanes([nodes4[0, 0], nodes4[1, 0]])
    level2[...] = pairs2
    level3[...] = pairs3
    third_out[...] = pairs3
    rim[pl.ds(0, 2)] = leaf_coeffs(above[...], wide)
    rim[pl.ds(2, 2)] = leaf_coeffs(below[...], wide)

    edge_pair = 3 * core
    edge_col = 7 * core
    nothing = jnp.zeros((2, PROBES, 128), BF)
    padded1[pl.ds(0, 2)] = nothing
    padded1[pl.ds(18, 2)] = nothing
    padded2[pl.ds(0, 2)] = nothing
    padded2[pl.ds(10, 2)] = nothing
    for r in range(16):
        padded1[r + 2] = gathered[r, edge_pair]
    for r in range(8):
        padded2[r + 2] = level2[r, core]
    side_out[0] = above[1, edge_col]
    side_out[1] = own[0, edge_col]
    side_out[2] = own[1, edge_col]
    side_out[3] = below[0, edge_col]
    side_out[4] = rim[0, edge_pair]
    side_out[5] = rim[1, edge_pair]
    side_out[6] = mine[0, edge_pair]
    side_out[7] = mine[1, edge_pair]
    side_out[8] = rim[2, edge_pair]
    side_out[9] = rim[3, edge_pair]
    side_out[pl.ds(10, 6)] = padded1[pl.ds(2 * (row // 2), 6)]
    side_out[pl.ds(16, 6)] = padded2[pl.ds(2 * (row // 4), 6)]
    side_out[pl.ds(22, 4)] = pairs3
    mate_out[0] = above[1, 7 - edge_col]
    mate_out[1] = below[0, 7 - edge_col]
    for r in range(4):
        mate_out[2 + r] = rim[r, 3 - edge_pair]


def third_kernel(
    own, other, above, below, mine, others, rim, gathered, level2, level3,
    side, third, mate, top, w0, w1, w2, w3, w4, w5, table, basis, up, down,
    out,
    near, window0, padded1, window1, padded2, window2, window3, padded4, padded5, padded6, padded7,
):
    row, col, chip, core = places()
    wide = pair_basis(basis[...])

    blank = jnp.zeros((2, PROBES, 128), BF)
    padded4[pl.ds(0, 2)] = blank
    padded4[pl.ds(18, 2)] = blank
    for c in range(16):
        padded4[c + 2] = top[(chip - c + 16) % 16]
    by_col = jnp.concatenate([up[4, 0], up[4, 2], up[4, 1], up[4, 3]], axis=0)
    all4 = padded4[pl.ds(2, 16)].reshape(8, 2, PROBES, 128)
    nodes5 = dot(lanes([all4[:, 0], all4[:, 1]]).reshape(-1, 256), by_col)
    nodes5 = nodes5.astype(BF).reshape(8, PROBES, RANK)

    def raise_row(nodes, level):
        pairs = to_pairs(nodes).reshape(-1, 128)
        both = jnp.concatenate([up[level, 0], up[level, 1]], axis=0)
        return dot(pairs, both).astype(BF).reshape(-1, PROBES, RANK)

    nodes6 = raise_row(nodes5, 5)
    nodes7 = raise_row(nodes6, 6)
    gap = jnp.zeros((2, PROBES, RANK), BF)
    for padded, nodes in ((padded5, nodes5), (padded6, nodes6), (padded7, nodes7)):
        count = nodes.shape[0]
        padded[pl.ds(0, 2)] = gap
        padded[pl.ds(2, count)] = nodes
        padded[pl.ds(2 + count, 2)] = gap

    def far_row(padded, level):
        start = 2 * (col // (1 << (level - 2)))
        return dot(lanes([padded[start + k] for k in range(6)]), w5[level - 5])

    def lowered(local, level):
        e = (row // (1 << (level - 1))) % 2
        f = (col // (1 << (level - 3))) % 2
        return dot(local, down[level, 2 * e + f])

    local = far_row(padded7, 7).astype(BF)
    local = (far_row(padded6, 6) + lowered(local, 6)).astype(BF)
    local = (far_row(padded5, 5) + lowered(local, 5)).astype(BF)
    start4 = 2 * (chip // 2)
    far4 = dot(lanes([padded4[start4 + k] for k in range(6)]), w4[...])
    local = (far4 + lowered(local, 4)).astype(BF)

    for r in range(4):
        window3[r, 2 * core] = side[22 + r]
        window3[r, 1] = level3[r]
        window3[r, 2 - 2 * core] = third[r]
    far3 = dot(lanes([window3[r, k] for r in range(4) for k in range(3)]), w3[...])
    local3 = (far3 + lowered(local, 3)).astype(BF)

    empty2 = jnp.zeros((2, 2, PROBES, 128), BF)
    padded2[pl.ds(0, 2)] = empty2
    padded2[pl.ds(2, 8)] = level2[...]
    padded2[pl.ds(10, 2)] = empty2
    for w in range(6):
        for k in range(2):
            window2[w, k + 1 - core] = padded2[2 * (row // 4) + w, k]
        window2[w, 2 * core] = side[16 + w]
    far2 = dot(lanes([window2[w, k] for w in range(6) for k in range(3)]), w2[...])
    e2 = (row // 2) % 2
    local2 = (far2 + dot(local3, lanes([down[2, 2 * e2], down[2, 2 * e2 + 1]]))).astype(BF)

    empty1 = jnp.zeros((2, 4, PROBES, 128), BF)
    padded1[pl.ds(0, 2)] = empty1
    padded1[pl.ds(2, 16)] = gathered[...]
    padded1[pl.ds(18, 2)] = empty1
    for w in range(6):
        for k in range(3):
            window1[w, k + 1 - core] = padded1[2 * (row // 2) + w, k + core]
        window1[w, 3 * core] = side[10 + w]
    far1 = dot(
        lanes([window1[w, pl.ds(k, 2)].reshape(-1, 128) for w in range(6) for k in range(3)]),
        w1[...],
    )
    e1 = row % 2
    down1 = lanes([down[1, 2 * e1], down[1, 2 * e1 + 1]])
    none1 = jnp.zeros_like(down1)
    down1 = jnp.concatenate([lanes([down1, none1]), lanes([none1, down1])], axis=0)
    spread1 = dot(local2, down1)
    spread1 = jnp.concatenate([spread1[:, :128], spread1[:, 128:]], axis=0)
    local1 = (far1 + spread1).astype(BF)

    window0[pl.ds(0, 2), pl.ds(1, 4)] = rim[pl.ds(0, 2)]
    window0[pl.ds(2, 2), pl.ds(1, 4)] = mine[...]
    window0[pl.ds(4, 2), pl.ds(1, 4)] = rim[pl.ds(2, 2)]
    for w in range(6):
        window0[w, 5 * core] = side[4 + w]
    for r in range(2):
        window0[r, 5 - 5 * core] = mate[2 + r]
        window0[2 + r, 5 - 5 * core] = others[r, 3 * core]
        window0[4 + r, 5 - 5 * core] = mate[4 + r]
    far0 = dot(
        lanes([window0[w, pl.ds(k, 4)].reshape(-1, 128) for w in range(6) for k in range(3)]),
        w0[...],
    )
    down0 = lanes([down[0, k] for k in range(4)])
    none0 = jnp.zeros_like(down0)
    down0 = jnp.concatenate([lanes([down0, none0]), lanes([none0, down0])], axis=0)
    spread0 = dot(local1, down0).reshape(2, PROBES, 512)
    spread0 = jnp.stack([spread0[:, :, :256], spread0[:, :, 256:]], axis=1).reshape(-1, 256)
    local0 = (far0 + spread0).astype(BF)

    near[0, pl.ds(1, 8)] = above[1]
    near[1, pl.ds(1, 8)] = own[0]
    near[2, pl.ds(1, 8)] = own[1]
    near[3, pl.ds(1, 8)] = below[0]
    for r in range(4):
        near[r, 9 * core] = side[r]
    near[0, 9 - 9 * core] = mate[0]
    near[1, 9 - 9 * core] = other[0, 7 * core]
    near[2, 9 - 9 * core] = other[1, 7 * core]
    near[3, 9 - 9 * core] = mate[1]
    for e in (0, 1):
        joined = lanes([near[e + u, pl.ds(v, 8)].reshape(-1, 128) for u in range(3) for v in range(3)])
        near_sum = dot(joined, table[...]).reshape(8, PROBES, 128)
        far_sum = lax.dot_general(
            local0[:, 128 * e : 128 * e + 128], wide, (((1,), (1,)), ((), ())),
            preferred_element_type=F32,
        ).reshape(4, PROBES, 256)
        for q in range(4):
            for f in (0, 1):
                part = far_sum[q, :, 128 * f : 128 * f + 128]
                out[e, 2 * q + f] = (near_sum[2 * q + f] + part).astype(BF)


def route(rule, size_x, size_y):
    pairs = []
    for a in range(size_x):
        for b in range(size_y):
            x, y = rule(a, b)
            if 0 <= x < size_x and 0 <= y < size_y:
                pairs.append((a * size_y + b, x * size_y + y))
    return pairs


def across(core):
    return 1 if core else -1


def shards(probes, leaf_basis, up_transfer, down_transfer, coupling, far_ids):
    size_x, size_y = lax.axis_size("gx"), lax.axis_size("gy")
    both = ("gx", "gy")

    def move(value, rule):
        return lax.ppermute(value, both, route(rule, size_x, size_y))

    other = move(probes, lambda a, b: (a, b ^ 1))
    above = move(probes, lambda a, b: (a + 1, b))
    below = move(probes, lambda a, b: (a - 1, b))

    smem = pl.BlockSpec(memory_space=pltpu.SMEM)
    whole = pl.BlockSpec(memory_space=pltpu.VMEM)
    w0, w1, w2, w3, w4, w5, table = call(
        prepare_kernel,
        [
            vmem((36 * RANK, 256)), vmem((36 * RANK, 128)), vmem((36 * RANK, 128)),
            vmem((24 * RANK, RANK)), vmem((12 * RANK, RANK)), vmem((3, 6 * RANK, RANK)),
            vmem((9 * 128, 128)),
        ],
        in_specs=[smem, whole],
    )(far_ids, coupling)

    sent, mine, others = call(
        first_kernel,
        [vmem((16, 4, PROBES, 128)), vmem((2, 4, PROBES, 128)), vmem((2, 4, PROBES, 128))],
    )(probes, other, leaf_basis, up_transfer)
    gathered = lax.all_to_all(sent, "gx", 0, 0)

    far_out, side_out, third_out, mate_out, rim, level2, level3 = call(
        second_kernel,
        [
            vmem((PROBES, 128)), vmem((26, PROBES, 128)), vmem((4, PROBES, 128)),
            vmem((6, PROBES, 128)), vmem((4, 4, PROBES, 128)), vmem((8, 2, PROBES, 128)),
            vmem((4, PROBES, 128)),
        ],
        scratch=[pltpu.VMEM((20, PROBES, 128), BF), pltpu.VMEM((12, PROBES, 128), BF)],
    )(gathered, probes, mine, above, below, leaf_basis, up_transfer)

    chips = size_y // 2
    top = move(far_out, lambda a, b: (a, 2 * ((b // 2 + a) % chips) + b % 2))
    side = move(side_out, lambda a, b: (a, b + across(b % 2)))
    third = move(third_out, lambda a, b: (a, b + 3 - 6 * (b % 2)))
    mate = move(mate_out, lambda a, b: (a, b ^ 1))
    top = lax.all_to_all(jnp.broadcast_to(top, (size_x,) + top.shape), "gx", 0, 0)

    block = (PROBES, 128)
    scratch = [
        pltpu.VMEM(lead + block, BF)
        for lead in ((4, 10), (6, 6), (20, 4), (6, 4), (12, 2), (6, 3), (4, 3), (20,))
    ] + [pltpu.VMEM((count + 4, PROBES, RANK), BF) for count in (8, 4, 2)]
    return call(third_kernel, vmem(probes.shape), scratch=scratch)(
        probes, other, above, below, mine, others, rim, gathered, level2, level3,
        side, third, mate, top, w0, w1, w2, w3, w4, w5, table,
        leaf_basis, up_transfer, down_transfer,
    )


def solution(mesh):
    in_specs = (P("gx", "gy", None, None), P(), P(), P(), P(), P())
    out_specs = P("gx", "gy", None, None)
    return jax.shard_map(shards, mesh=mesh, in_specs=in_specs, out_specs=out_specs, check_vma=False)
```

```python
import jax
import jax.numpy as jnp
from jax import lax
from jax.experimental import pallas as pl
from jax.experimental.pallas import tpu as pltpu
from jax.sharding import PartitionSpec as P

LEAF_ROWS = 8
LEAF_COLS = 16
RANK = 64
PROBES = 32
BF = jnp.bfloat16
F32 = jnp.float32

length_scale = 1.5


def dot(left, right):
    return jnp.dot(left, right, preferred_element_type=F32)


def lanes(parts):
    return jnp.concatenate(parts, axis=-1)


def block_slot(e, f, wr, wc):
    return 6 * wr + wc - 3 * min(max(wr - 1 - e, 0), 3) - (
        min(max(wc - 1 - f, 0), 3) if e + 1 <= wr <= e + 3 else 0
    )


def is_near(e, f, wr, wc):
    return e + 1 <= wr <= e + 3 and f + 1 <= wc <= f + 3


def places():
    row = lax.axis_index("gx")
    col = lax.axis_index("gy")
    return row, col, col // 2, col % 2


def prepare_kernel(
    ids_far, coupling_far, up_far, down_far, basis_far, own_far,
    w0, w1, w2, w3, w4, w5, table, wide, up, down0, down1, down2, down3, own,
    ids, coupling, down, basis, ids_sem, level_sems, sems,
):
    row, col, _, _ = places()
    first = pltpu.make_async_copy(ids_far, ids, ids_sem)
    first.start()
    levels = []
    for level in range(8):
        levels.append(
            pltpu.make_async_copy(coupling_far.at[level], coupling.at[level], level_sems.at[level])
        )
    levels[0].start()
    small = [
        pltpu.make_async_copy(source, target, sems.at[at])
        for at, (source, target) in enumerate(
            ((basis_far, basis), (own_far, own), (up_far, up), (down_far, down))
        )
    ]
    for copy in small:
        copy.start()
    for copy in levels[1:]:
        copy.start()

    size = LEAF_ROWS * LEAF_COLS
    theirs = lax.broadcasted_iota(jnp.int32, (size, size), 0)
    ours = lax.broadcasted_iota(jnp.int32, (size, size), 1)
    rows_apart = (theirs // LEAF_COLS - ours // LEAF_COLS).astype(F32)
    cols_apart = (theirs % LEAF_COLS - ours % LEAF_COLS).astype(F32)
    for u in (-1, 0, 1):
        for v in (-1, 0, 1):
            apart_row = rows_apart + float(u * LEAF_ROWS)
            apart_col = cols_apart + float(v * LEAF_COLS)
            scaled = jnp.sqrt(3.0 * (apart_row * apart_row + apart_col * apart_col)) / length_scale
            value = (1.0 + scaled) * jnp.exp(-scaled)
            table[pl.ds((3 * (u + 1) + v + 1) * size, size), :] = value.astype(BF)

    def pair(level, e, wr, wc):
        halves = []
        for f in (0, 1):
            if is_near(e, f, wr, wc):
                halves.append(jnp.zeros((RANK, RANK), BF))
            else:
                halves.append(coupling[level, ids[level, 2 * e + f, block_slot(e, f, wr, wc)]])
        return lanes(halves)

    first.wait()
    levels[0].wait()
    for wr in range(6):
        for wc in range(6):
            at = pl.ds((6 * wr + wc) * RANK, RANK)
            for e in (0, 1):
                w0[at, pl.ds(128 * e, 128)] = pair(0, e, wr, wc)

    for level, out, bit in ((1, w1, row % 2), (2, w2, (row // 2) % 2)):
        levels[level].wait()
        for e in (0, 1):

            @pl.when(bit == e)
            def _(level=level, out=out, e=e):
                for wr in range(6):
                    for wc in range(6):
                        out[pl.ds((6 * wr + wc) * RANK, RANK), :] = pair(level, e, wr, wc)

    def single(level, e, f, wr, wc):
        row_in = jnp.logical_and(wr >= e + 1, wr <= e + 3)
        col_in = jnp.logical_and(wc >= f + 1, wc <= f + 3)
        skipped = 3 * jnp.clip(wr - 1 - e, 0, 3) + jnp.where(row_in, jnp.clip(wc - 1 - f, 0, 3), 0)
        slot = jnp.clip(6 * wr + wc - skipped, 0, 26)
        keep = jnp.where(jnp.logical_and(row_in, col_in), 0.0, 1.0)
        block = coupling[level, ids[level, 2 * e + f, slot]]
        return block * jnp.full((RANK, RANK), keep, F32).astype(BF)

    levels[3].wait()
    e3, f3 = (row // 4) % 2, col % 2
    first3 = 2 - 2 * (row // 8)
    for r in range(4):
        for wc in range(6):
            w3[pl.ds((6 * r + wc) * RANK, RANK), :] = single(3, e3, f3, r + first3, wc)
    levels[4].wait()
    e4, f4 = row // 8, (col // 2) % 2
    for wc in range(6):
        for r in range(2):
            w4[pl.ds((2 * wc + r) * RANK, RANK), :] = single(4, e4, f4, jnp.int32(2 + r), wc)
    for level in (5, 6, 7):
        levels[level].wait()
        f = (col // (1 << (level - 3))) % 2
        for wc in range(6):
            w5[level - 5, pl.ds(wc * RANK, RANK), :] = single(
                level, jnp.int32(0), f, jnp.int32(2), wc
            )

    for copy in small:
        copy.wait()
    blank = jnp.zeros_like(basis)
    wide[...] = jnp.concatenate([lanes([basis[...], blank]), lanes([blank, basis[...]])], axis=0)
    all0 = lanes([down[0, k] for k in range(4)])
    none0 = jnp.zeros_like(all0)
    down0[...] = jnp.concatenate([lanes([all0, none0]), lanes([none0, all0])], axis=0)
    e1, e2 = row % 2, (row // 2) % 2
    both1 = lanes([down[1, 2 * e1], down[1, 2 * e1 + 1]])
    none1 = jnp.zeros_like(both1)
    down1[...] = jnp.concatenate([lanes([both1, none1]), lanes([none1, both1])], axis=0)
    down2[...] = lanes([down[2, 2 * e2], down[2, 2 * e2 + 1]])
    for level in (3, 4, 5, 6):
        e = (row // (1 << (level - 1))) % 2
        f = (col // (1 << (level - 3))) % 2
        down3[level - 3] = down[level, 2 * e + f]


def array(shape, kind=BF):
    return jax.ShapeDtypeStruct(shape, kind)


def call(kernel, out_shape, scratch=(), flops=1 << 24, read=1 << 21, **specs):
    return pl.pallas_call(
        kernel,
        out_shape=out_shape,
        **specs,
        scratch_shapes=list(scratch),
        compiler_params=pltpu.CompilerParams(vmem_limit_bytes=16 << 20),
        cost_estimate=pl.CostEstimate(flops=flops, bytes_accessed=read, transcendentals=0),
    )


def leaf_coeffs(tile, wide_basis):
    rows = tile.shape[0]
    split = tile.reshape(rows, 4, 2, PROBES, 128)
    joined = lanes([split[:, :, 0], split[:, :, 1]]).reshape(-1, 256)
    coeffs = lax.dot_general(
        joined, wide_basis, (((1,), (1,)), ((), ())), preferred_element_type=F32
    )
    return coeffs.astype(BF).reshape(rows, 4, PROBES, 128)


def to_pairs(nodes):
    lead = nodes.shape[:-3]
    split = nodes.reshape(lead + (nodes.shape[-3] // 2, 2, PROBES, RANK))
    return lanes([split[..., 0, :, :], split[..., 1, :, :]])


def raise_pairs(pairs, transfer):
    rows, count = pairs.shape[:2]
    split = pairs.reshape(rows // 2, 2, count, PROBES, 128)
    joined = lanes([split[:, 0], split[:, 1]]).reshape(-1, 256)
    return dot(joined, transfer).astype(BF).reshape(rows // 2, count, PROBES, RANK)


def first_kernel(own, other, above, below, wide, up, sent, mine, beside, rim):
    _, _, _, core = places()
    transfer = up[0].reshape(4 * RANK, RANK)
    kept = {}
    for which, tile in ((core, own), (1 - core, other)):
        coeffs = leaf_coeffs(tile[...], wide[...])
        kept[tile is own] = coeffs
        pairs = to_pairs(raise_pairs(coeffs, transfer)[0])
        for peer in range(16):
            sent[peer, pl.ds(2 * which, 2)] = pairs
    mine[...] = kept[True]
    rim[pl.ds(0, 2)] = leaf_coeffs(above[...], wide[...])
    rim[pl.ds(2, 2)] = leaf_coeffs(below[...], wide[...])

    for r in (0, 1):
        beside[r] = other[r, 7 * core]

        @pl.when(core == 0)
        def _(r=r):
            beside[2 + r] = kept[False][r, 0]

        @pl.when(core == 1)
        def _(r=r):
            beside[2 + r] = kept[False][r, 3]


def second_kernel(
    gathered, own, mine, above, below, rim, up,
    far_out, side_out, third_out, mate_out, level2, level3,
    padded1, padded2,
):
    row, _, _, core = places()
    pairs2 = to_pairs(raise_pairs(gathered[...], up[1].reshape(4 * RANK, RANK)))
    pairs3 = to_pairs(raise_pairs(pairs2, up[2].reshape(4 * RANK, RANK)))[:, 0]
    nodes4 = raise_pairs(pairs3[:, None], up[3].reshape(4 * RANK, RANK))
    far_out[...] = lanes([nodes4[0, 0], nodes4[1, 0]])
    level2[...] = pairs2
    level3[...] = pairs3
    third_out[...] = pairs3

    edge_pair = 3 * core
    edge_col = 7 * core
    nothing = jnp.zeros((2, PROBES, 128), BF)
    padded1[pl.ds(0, 2)] = nothing
    padded1[pl.ds(18, 2)] = nothing
    padded2[pl.ds(0, 2)] = nothing
    padded2[pl.ds(10, 2)] = nothing
    for r in range(16):
        padded1[r + 2] = gathered[r, edge_pair]
    for r in range(8):
        padded2[r + 2] = level2[r, core]
    side_out[0] = above[1, edge_col]
    side_out[1] = own[0, edge_col]
    side_out[2] = own[1, edge_col]
    side_out[3] = below[0, edge_col]
    side_out[4] = rim[0, edge_pair]
    side_out[5] = rim[1, edge_pair]
    side_out[6] = mine[0, edge_pair]
    side_out[7] = mine[1, edge_pair]
    side_out[8] = rim[2, edge_pair]
    side_out[9] = rim[3, edge_pair]
    side_out[pl.ds(10, 6)] = padded1[pl.ds(2 * (row // 2), 6)]
    side_out[pl.ds(16, 6)] = padded2[pl.ds(2 * (row // 4), 6)]
    side_out[pl.ds(22, 4)] = pairs3
    mate_out[0] = above[1, 7 - edge_col]
    mate_out[1] = below[0, 7 - edge_col]
    for r in range(4):
        mate_out[2 + r] = rim[r, 3 - edge_pair]


def third_kernel(
    own, above, below, mine, beside, rim, gathered, level2, level3,
    side, third, mate, w0, w1, w2, w3, table,
    near_sum, far0, far1, far2, far3, tag,
    near, window0, padded1, window1, padded2, window2, window3,
):
    row, _, _, core = places()

    window0[pl.ds(0, 2), pl.ds(1, 4)] = rim[pl.ds(0, 2)]
    window0[pl.ds(2, 2), pl.ds(1, 4)] = mine[...]
    window0[pl.ds(4, 2), pl.ds(1, 4)] = rim[pl.ds(2, 2)]
    for w in range(6):
        window0[w, 5 * core] = side[4 + w]
    for r in range(2):
        window0[r, 5 - 5 * core] = mate[2 + r]
        window0[2 + r, 5 - 5 * core] = beside[2 + r]
        window0[4 + r, 5 - 5 * core] = mate[4 + r]
    far0[...] = dot(
        lanes([window0[w, pl.ds(k, 4)].reshape(-1, 128) for w in range(6) for k in range(3)]),
        w0[...],
    )

    near[0, pl.ds(1, 8)] = above[1]
    near[1, pl.ds(1, 8)] = own[0]
    near[2, pl.ds(1, 8)] = own[1]
    near[3, pl.ds(1, 8)] = below[0]
    for r in range(4):
        near[r, 9 * core] = side[r]
    near[0, 9 - 9 * core] = mate[0]
    near[1, 9 - 9 * core] = beside[0]
    near[2, 9 - 9 * core] = beside[1]
    near[3, 9 - 9 * core] = mate[1]
    for e in (0, 1):
        joined = lanes([near[e + u, pl.ds(v, 8)].reshape(-1, 128) for u in range(3) for v in range(3)])
        near_sum[e] = dot(joined, table[...]).reshape(8, PROBES, 128)

    empty1 = jnp.zeros((2, 4, PROBES, 128), BF)
    padded1[pl.ds(0, 2)] = empty1
    padded1[pl.ds(2, 16)] = gathered[...]
    padded1[pl.ds(18, 2)] = empty1
    for w in range(6):
        for k in range(3):
            window1[w, k + 1 - core] = padded1[2 * (row // 2) + w, k + core]
        window1[w, 3 * core] = side[10 + w]
    far1[...] = dot(
        lanes([window1[w, pl.ds(k, 2)].reshape(-1, 128) for w in range(6) for k in range(3)]),
        w1[...],
    )

    empty2 = jnp.zeros((2, 2, PROBES, 128), BF)
    padded2[pl.ds(0, 2)] = empty2
    padded2[pl.ds(2, 8)] = level2[...]
    padded2[pl.ds(10, 2)] = empty2
    for w in range(6):
        for k in range(2):
            window2[w, k + 1 - core] = padded2[2 * (row // 4) + w, k]
        window2[w, 2 * core] = side[16 + w]
    far2[...] = dot(lanes([window2[w, k] for w in range(6) for k in range(3)]), w2[...])

    for r in range(4):
        window3[r, 2 * core] = side[22 + r]
        window3[r, 1] = level3[r]
        window3[r, 2 - 2 * core] = third[r]
    far3[...] = dot(lanes([window3[r, k] for r in range(4) for k in range(3)]), w3[...])
    tag[...] = jnp.zeros_like(tag)


def copies_kernel(block, tag, out):
    for peer in range(16):
        out[peer] = block[...]


def fourth_kernel(
    top, near_sum, far0, far1, far2, far3, w4, w5, wide, up, down0, down1, down2, down3,
    out,
    padded4, padded5, padded6, padded7,
):
    _, col, chip, _ = places()

    blank = jnp.zeros((2, PROBES, 128), BF)
    padded4[pl.ds(0, 2)] = blank
    padded4[pl.ds(18, 2)] = blank
    for c in range(16):
        padded4[c + 2] = top[(chip - c + 16) % 16]
    by_col = jnp.concatenate([up[4, 0], up[4, 2], up[4, 1], up[4, 3]], axis=0)
    all4 = padded4[pl.ds(2, 16)].reshape(8, 2, PROBES, 128)
    nodes5 = dot(lanes([all4[:, 0], all4[:, 1]]).reshape(-1, 256), by_col)
    nodes5 = nodes5.astype(BF).reshape(8, PROBES, RANK)

    def raise_row(nodes, level):
        pairs = to_pairs(nodes).reshape(-1, 128)
        both = jnp.concatenate([up[level, 0], up[level, 1]], axis=0)
        return dot(pairs, both).astype(BF).reshape(-1, PROBES, RANK)

    nodes6 = raise_row(nodes5, 5)
    nodes7 = raise_row(nodes6, 6)
    gap = jnp.zeros((2, PROBES, RANK), BF)
    for padded, nodes in ((padded5, nodes5), (padded6, nodes6), (padded7, nodes7)):
        count = nodes.shape[0]
        padded[pl.ds(0, 2)] = gap
        padded[pl.ds(2, count)] = nodes
        padded[pl.ds(2 + count, 2)] = gap

    def far_row(padded, level):
        start = 2 * (col // (1 << (level - 2)))
        return dot(lanes([padded[start + k] for k in range(6)]), w5[level - 5])

    start4 = 2 * (chip // 2)
    far4 = dot(lanes([padded4[start4 + k] for k in range(6)]), w4[...])
    local = far_row(padded7, 7).astype(BF)
    local = (far_row(padded6, 6) + dot(local, down3[3])).astype(BF)
    local = (far_row(padded5, 5) + dot(local, down3[2])).astype(BF)
    local = (far4 + dot(local, down3[1])).astype(BF)
    local = (far3[...] + dot(local, down3[0])).astype(BF)
    local2 = (far2[...] + dot(local, down2[...])).astype(BF)
    spread1 = dot(local2, down1[...])
    spread1 = jnp.concatenate([spread1[:, :128], spread1[:, 128:]], axis=0)
    local1 = (far1[...] + spread1).astype(BF)
    spread0 = dot(local1, down0[...]).reshape(2, PROBES, 512)
    spread0 = jnp.stack([spread0[:, :, :256], spread0[:, :, 256:]], axis=1).reshape(-1, 256)
    local0 = (far0[...] + spread0).astype(BF)
    for e in (0, 1):
        far_sum = dot(local0[:, 128 * e : 128 * e + 128], wide[...]).reshape(4, PROBES, 256)
        for q in range(4):
            for f in (0, 1):
                part = far_sum[q, :, 128 * f : 128 * f + 128]
                out[e, 2 * q + f] = (near_sum[e, 2 * q + f] + part).astype(BF)


def route(rule, size_x, size_y):
    pairs = []
    for a in range(size_x):
        for b in range(size_y):
            x, y = rule(a, b)
            if 0 <= x < size_x and 0 <= y < size_y:
                pairs.append((a * size_y + b, x * size_y + y))
    return pairs


def across(core):
    return 1 if core else -1


def shards(probes, leaf_basis, up_transfer, down_transfer, coupling, far_ids):
    size_x, size_y = lax.axis_size("gx"), lax.axis_size("gy")
    both = ("gx", "gy")

    def move(value, rule):
        return lax.ppermute(value, both, route(rule, size_x, size_y))

    other = move(probes, lambda a, b: (a, b ^ 1))
    above = move(probes, lambda a, b: (a + 1, b))
    below = move(probes, lambda a, b: (a - 1, b))

    hbm = pl.BlockSpec(memory_space=pltpu.MemorySpace.HBM)
    block = (PROBES, 128)
    w0, w1, w2, w3, w4, w5, table, wide, up, down0, down1, down2, down3, own = call(
        prepare_kernel,
        [
            array((36 * RANK, 256)), array((36 * RANK, 128)), array((36 * RANK, 128)),
            array((24 * RANK, RANK)), array((12 * RANK, RANK)), array((3, 6 * RANK, RANK)),
            array((9 * 128, 128)), array((128, 256)), array(up_transfer.shape),
            array((128, 512)), array((128, 256)), array((RANK, 128)), array((4, RANK, RANK)),
            array(probes.shape),
        ],
        in_specs=[hbm] * 6,
        scratch=[
            pltpu.SMEM(far_ids.shape, jnp.int32), pltpu.VMEM(coupling.shape, BF),
            pltpu.VMEM(down_transfer.shape, BF), pltpu.VMEM(leaf_basis.shape[::-1], BF),
            pltpu.SemaphoreType.DMA, pltpu.SemaphoreType.DMA((8,)), pltpu.SemaphoreType.DMA((4,)),
        ],
    )(
        *[
            pltpu.with_memory_space_constraint(value, pltpu.MemorySpace.HBM)
            for value in (far_ids, coupling, up_transfer, down_transfer, leaf_basis.T, probes)
        ]
    )

    sent, mine, beside, rim = call(
        first_kernel,
        [array((16, 4) + block), array((2, 4) + block), array((4,) + block), array((4, 4) + block)],
    )(own, other, above, below, wide, up)
    gathered = lax.all_to_all(sent, "gx", 0, 0)

    far_out, side_out, third_out, mate_out, level2, level3 = call(
        second_kernel,
        [
            array(block), array((26,) + block), array((4,) + block), array((6,) + block),
            array((8, 2) + block), array((4,) + block),
        ],
        scratch=[pltpu.VMEM((20,) + block, BF), pltpu.VMEM((12,) + block, BF)],
    )(gathered, own, mine, above, below, rim, up)

    chips = size_y // 2
    side = move(side_out, lambda a, b: (a, b + across(b % 2)))
    third = move(third_out, lambda a, b: (a, b + 3 - 6 * (b % 2)))
    mate = move(mate_out, lambda a, b: (a, b ^ 1))
    top = move(far_out, lambda a, b: (a, 2 * ((b // 2 + a) % chips) + b % 2))

    near_sum, far0, far1, far2, far3, tag = call(
        third_kernel,
        [
            array((2, 8) + block, F32), array((4 * PROBES, 256), F32),
            array((2 * PROBES, 128), F32), array((PROBES, 128), F32), array((PROBES, RANK), F32),
            array((8, 128), F32),
        ],
        scratch=[
            pltpu.VMEM(lead + block, BF)
            for lead in ((4, 10), (6, 6), (20, 4), (6, 4), (12, 2), (6, 3), (4, 3))
        ],
    )(
        own, above, below, mine, beside, rim, gathered, level2, level3, side, third, mate,
        w0, w1, w2, w3, table,
    )
    copies = call(copies_kernel, array((16,) + block))(top, tag)
    top = lax.all_to_all(copies, "gx", 0, 0)

    return call(
        fourth_kernel,
        array(probes.shape),
        scratch=[pltpu.VMEM((20,) + block, BF)]
        + [pltpu.VMEM((count + 4, PROBES, RANK), BF) for count in (8, 4, 2)],
    )(top, near_sum, far0, far1, far2, far3, w4, w5, wide, up, down0, down1, down2, down3)


def solution(mesh):
    in_specs = (P("gx", "gy", None, None), P(), P(), P(), P(), P())
    out_specs = P("gx", "gy", None, None)
    return jax.shard_map(shards, mesh=mesh, in_specs=in_specs, out_specs=out_specs, check_vma=False)
```

```python
import jax
import jax.numpy as jnp
from jax import lax
from jax.experimental import pallas as pl
from jax.experimental.pallas import tpu as pltpu
from jax.sharding import PartitionSpec as P

LEAF_ROWS = 8
LEAF_COLS = 16
RANK = 64
PROBES = 32
BF = jnp.bfloat16
F32 = jnp.float32

length_scale = 1.5


def dot(left, right):
    return jnp.dot(left, right, preferred_element_type=F32)


def lanes(parts):
    return jnp.concatenate(parts, axis=-1)


def block_slot(e, f, wr, wc):
    return 6 * wr + wc - 3 * min(max(wr - 1 - e, 0), 3) - (
        min(max(wc - 1 - f, 0), 3) if e + 1 <= wr <= e + 3 else 0
    )


def is_near(e, f, wr, wc):
    return e + 1 <= wr <= e + 3 and f + 1 <= wc <= f + 3


def places():
    row = lax.axis_index("gx")
    col = lax.axis_index("gy")
    return row, col, col // 2, col % 2


def prepare_kernel(
    ids_far, coupling_far, up_far, down_far, basis_far, own_far,
    w0, w1, w2, w3, w4, w5, table, wide, up, down0, down1, down2, down3, own,
    ids, coupling, down, basis, ids_sem, level_sems, sems,
):
    row, col, _, _ = places()
    first = pltpu.make_async_copy(ids_far, ids, ids_sem)
    first.start()
    levels = []
    for level in range(8):
        levels.append(
            pltpu.make_async_copy(coupling_far.at[level], coupling.at[level], level_sems.at[level])
        )
    levels[0].start()
    small = [
        pltpu.make_async_copy(source, target, sems.at[at])
        for at, (source, target) in enumerate(
            ((basis_far, basis), (own_far, own), (up_far, up), (down_far, down))
        )
    ]
    for copy in small:
        copy.start()
    for copy in levels[1:]:
        copy.start()

    size = LEAF_ROWS * LEAF_COLS
    theirs = lax.broadcasted_iota(jnp.int32, (size, size), 0)
    ours = lax.broadcasted_iota(jnp.int32, (size, size), 1)
    rows_apart = (theirs // LEAF_COLS - ours // LEAF_COLS).astype(F32)
    cols_apart = (theirs % LEAF_COLS - ours % LEAF_COLS).astype(F32)
    for u in (-1, 0, 1):
        for v in (-1, 0, 1):
            apart_row = rows_apart + float(u * LEAF_ROWS)
            apart_col = cols_apart + float(v * LEAF_COLS)
            scaled = jnp.sqrt(3.0 * (apart_row * apart_row + apart_col * apart_col)) / length_scale
            value = (1.0 + scaled) * jnp.exp(-scaled)
            table[pl.ds((3 * (u + 1) + v + 1) * size, size), :] = value.astype(BF)

    def pair(level, e, wr, wc):
        halves = []
        for f in (0, 1):
            if is_near(e, f, wr, wc):
                halves.append(jnp.zeros((RANK, RANK), BF))
            else:
                halves.append(coupling[level, ids[level, 2 * e + f, block_slot(e, f, wr, wc)]])
        return lanes(halves)

    first.wait()
    levels[0].wait()
    for wr in range(6):
        for wc in range(6):
            at = pl.ds((6 * wr + wc) * RANK, RANK)
            for e in (0, 1):
                w0[at, pl.ds(128 * e, 128)] = pair(0, e, wr, wc)

    for level, out, bit in ((1, w1, row % 2), (2, w2, (row // 2) % 2)):
        levels[level].wait()
        for e in (0, 1):

            @pl.when(bit == e)
            def _(level=level, out=out, e=e):
                for wr in range(6):
                    for wc in range(6):
                        out[pl.ds((6 * wr + wc) * RANK, RANK), :] = pair(level, e, wr, wc)

    def single(level, e, f, wr, wc):
        row_in = jnp.logical_and(wr >= e + 1, wr <= e + 3)
        col_in = jnp.logical_and(wc >= f + 1, wc <= f + 3)
        skipped = 3 * jnp.clip(wr - 1 - e, 0, 3) + jnp.where(row_in, jnp.clip(wc - 1 - f, 0, 3), 0)
        slot = jnp.clip(6 * wr + wc - skipped, 0, 26)
        keep = jnp.where(jnp.logical_and(row_in, col_in), 0.0, 1.0)
        block = coupling[level, ids[level, 2 * e + f, slot]]
        return block * jnp.full((RANK, RANK), keep, F32).astype(BF)

    levels[3].wait()
    e3, f3 = (row // 4) % 2, col % 2
    first3 = 2 - 2 * (row // 8)
    for r in range(4):
        for wc in range(6):
            w3[pl.ds((6 * r + wc) * RANK, RANK), :] = single(3, e3, f3, r + first3, wc)
    levels[4].wait()
    e4, f4 = row // 8, (col // 2) % 2
    for wc in range(6):
        for r in range(2):
            w4[pl.ds((2 * wc + r) * RANK, RANK), :] = single(4, e4, f4, jnp.int32(2 + r), wc)
    for level in (5, 6, 7):
        levels[level].wait()
        f = (col // (1 << (level - 3))) % 2
        for wc in range(6):
            w5[level - 5, pl.ds(wc * RANK, RANK), :] = single(
                level, jnp.int32(0), f, jnp.int32(2), wc
            )

    for copy in small:
        copy.wait()
    blank = jnp.zeros_like(basis)
    wide[...] = jnp.concatenate([lanes([basis[...], blank]), lanes([blank, basis[...]])], axis=0)
    all0 = lanes([down[0, k] for k in range(4)])
    none0 = jnp.zeros_like(all0)
    down0[...] = jnp.concatenate([lanes([all0, none0]), lanes([none0, all0])], axis=0)
    e1, e2 = row % 2, (row // 2) % 2
    both1 = lanes([down[1, 2 * e1], down[1, 2 * e1 + 1]])
    none1 = jnp.zeros_like(both1)
    down1[...] = jnp.concatenate([lanes([both1, none1]), lanes([none1, both1])], axis=0)
    down2[...] = lanes([down[2, 2 * e2], down[2, 2 * e2 + 1]])
    for level in (3, 4, 5, 6):
        e = (row // (1 << (level - 1))) % 2
        f = (col // (1 << (level - 3))) % 2
        down3[level - 3] = down[level, 2 * e + f]


def array(shape, kind=BF):
    return jax.ShapeDtypeStruct(shape, kind)


def call(kernel, out_shape, scratch=(), flops=1 << 24, read=1 << 21, **specs):
    return pl.pallas_call(
        kernel,
        out_shape=out_shape,
        **specs,
        scratch_shapes=list(scratch),
        compiler_params=pltpu.CompilerParams(vmem_limit_bytes=16 << 20),
        cost_estimate=pl.CostEstimate(flops=flops, bytes_accessed=read, transcendentals=0),
    )


def leaf_coeffs(tile, wide_basis):
    rows = tile.shape[0]
    split = tile.reshape(rows, 4, 2, PROBES, 128)
    joined = lanes([split[:, :, 0], split[:, :, 1]]).reshape(-1, 256)
    coeffs = lax.dot_general(
        joined, wide_basis, (((1,), (1,)), ((), ())), preferred_element_type=F32
    )
    return coeffs.astype(BF).reshape(rows, 4, PROBES, 128)


def to_pairs(nodes):
    lead = nodes.shape[:-3]
    split = nodes.reshape(lead + (nodes.shape[-3] // 2, 2, PROBES, RANK))
    return lanes([split[..., 0, :, :], split[..., 1, :, :]])


def raise_pairs(pairs, transfer):
    rows, count = pairs.shape[:2]
    split = pairs.reshape(rows // 2, 2, count, PROBES, 128)
    joined = lanes([split[:, 0], split[:, 1]]).reshape(-1, 256)
    return dot(joined, transfer).astype(BF).reshape(rows // 2, count, PROBES, RANK)


def first_kernel(own, above, below, wide, up, pack, low, mine, rim):
    _, _, _, core = places()
    coeffs = leaf_coeffs(own[...], wide[...])
    pairs = to_pairs(raise_pairs(coeffs, up[0].reshape(4 * RANK, RANK))[0])
    mine[...] = coeffs
    rim[pl.ds(0, 2)] = leaf_coeffs(above[...], wide[...])
    rim[pl.ds(2, 2)] = leaf_coeffs(below[...], wide[...])
    low[...] = pairs

    edge_pair = 3 - 3 * core
    edge_col = 7 - 7 * core
    pack[pl.ds(0, 2)] = pairs
    pack[2] = mine[0, edge_pair]
    pack[3] = mine[1, edge_pair]
    pack[4] = own[0, edge_col]
    pack[5] = own[1, edge_col]
    pack[6] = above[1, edge_col]
    pack[7] = below[0, edge_col]
    for r in range(4):
        pack[8 + r] = rim[r, edge_pair]


def strip_kernel(low, packed, sent):
    _, _, _, core = places()
    for peer in range(16):
        sent[peer, pl.ds(2 * core, 2)] = low[...]
        sent[peer, pl.ds(2 - 2 * core, 2)] = packed[pl.ds(0, 2)]


def second_kernel(gathered, up, far_out, level2, level3):
    pairs2 = to_pairs(raise_pairs(gathered[...], up[1].reshape(4 * RANK, RANK)))
    pairs3 = to_pairs(raise_pairs(pairs2, up[2].reshape(4 * RANK, RANK)))[:, 0]
    nodes4 = raise_pairs(pairs3[:, None], up[3].reshape(4 * RANK, RANK))
    far_out[...] = lanes([nodes4[0, 0], nodes4[1, 0]])
    level2[...] = pairs2
    level3[...] = pairs3


def side_kernel(gathered, own, mine, above, below, rim, level2, level3, side_out, padded1, padded2):
    row, _, _, core = places()
    edge_pair = 3 * core
    edge_col = 7 * core
    nothing = jnp.zeros((2, PROBES, 128), BF)
    padded1[pl.ds(0, 2)] = nothing
    padded1[pl.ds(18, 2)] = nothing
    padded2[pl.ds(0, 2)] = nothing
    padded2[pl.ds(10, 2)] = nothing
    for r in range(16):
        padded1[r + 2] = gathered[r, edge_pair]
    for r in range(8):
        padded2[r + 2] = level2[r, core]
    side_out[0] = above[1, edge_col]
    side_out[1] = own[0, edge_col]
    side_out[2] = own[1, edge_col]
    side_out[3] = below[0, edge_col]
    side_out[4] = rim[0, edge_pair]
    side_out[5] = rim[1, edge_pair]
    side_out[6] = mine[0, edge_pair]
    side_out[7] = mine[1, edge_pair]
    side_out[8] = rim[2, edge_pair]
    side_out[9] = rim[3, edge_pair]
    side_out[pl.ds(10, 6)] = padded1[pl.ds(2 * (row // 2), 6)]
    side_out[pl.ds(16, 6)] = padded2[pl.ds(2 * (row // 4), 6)]
    side_out[pl.ds(22, 4)] = level3[...]


def third_kernel(
    own, above, below, mine, packed, rim, gathered, level2, level3,
    side, third, w0, w1, w2, w3, table,
    near_sum, far0, far1, far2, far3, tag,
    near, window0, padded1, window1, padded2, window2, window3,
):
    row, _, _, core = places()

    window0[pl.ds(0, 2), pl.ds(1, 4)] = rim[pl.ds(0, 2)]
    window0[pl.ds(2, 2), pl.ds(1, 4)] = mine[...]
    window0[pl.ds(4, 2), pl.ds(1, 4)] = rim[pl.ds(2, 2)]
    for w in range(6):
        window0[w, 5 * core] = side[4 + w]
    for r in range(2):
        window0[r, 5 - 5 * core] = packed[8 + r]
        window0[2 + r, 5 - 5 * core] = packed[2 + r]
        window0[4 + r, 5 - 5 * core] = packed[10 + r]
    far0[...] = dot(
        lanes([window0[w, pl.ds(k, 4)].reshape(-1, 128) for w in range(6) for k in range(3)]),
        w0[...],
    )

    near[0, pl.ds(1, 8)] = above[1]
    near[1, pl.ds(1, 8)] = own[0]
    near[2, pl.ds(1, 8)] = own[1]
    near[3, pl.ds(1, 8)] = below[0]
    for r in range(4):
        near[r, 9 * core] = side[r]
    near[0, 9 - 9 * core] = packed[6]
    near[1, 9 - 9 * core] = packed[4]
    near[2, 9 - 9 * core] = packed[5]
    near[3, 9 - 9 * core] = packed[7]
    for e in (0, 1):
        joined = lanes([near[e + u, pl.ds(v, 8)].reshape(-1, 128) for u in range(3) for v in range(3)])
        near_sum[e] = dot(joined, table[...]).reshape(8, PROBES, 128)

    empty1 = jnp.zeros((2, 4, PROBES, 128), BF)
    padded1[pl.ds(0, 2)] = empty1
    padded1[pl.ds(2, 16)] = gathered[...]
    padded1[pl.ds(18, 2)] = empty1
    for w in range(6):
        for k in range(3):
            window1[w, k + 1 - core] = padded1[2 * (row // 2) + w, k + core]
        window1[w, 3 * core] = side[10 + w]
    far1[...] = dot(
        lanes([window1[w, pl.ds(k, 2)].reshape(-1, 128) for w in range(6) for k in range(3)]),
        w1[...],
    )

    empty2 = jnp.zeros((2, 2, PROBES, 128), BF)
    padded2[pl.ds(0, 2)] = empty2
    padded2[pl.ds(2, 8)] = level2[...]
    padded2[pl.ds(10, 2)] = empty2
    for w in range(6):
        for k in range(2):
            window2[w, k + 1 - core] = padded2[2 * (row // 4) + w, k]
        window2[w, 2 * core] = side[16 + w]
    far2[...] = dot(lanes([window2[w, k] for w in range(6) for k in range(3)]), w2[...])

    for r in range(4):
        window3[r, 2 * core] = side[22 + r]
        window3[r, 1] = level3[r]
        window3[r, 2 - 2 * core] = third[r]
    far3[...] = dot(lanes([window3[r, k] for r in range(4) for k in range(3)]), w3[...])
    tag[...] = jnp.zeros_like(tag)


def copies_kernel(block, tag, out):
    for peer in range(16):
        out[peer] = block[...]


def fourth_kernel(
    top, near_sum, far0, far1, far2, far3, w4, w5, wide, up, down0, down1, down2, down3,
    out,
    padded4, padded5, padded6, padded7,
):
    _, col, chip, _ = places()

    blank = jnp.zeros((2, PROBES, 128), BF)
    padded4[pl.ds(0, 2)] = blank
    padded4[pl.ds(18, 2)] = blank
    for c in range(16):
        padded4[c + 2] = top[(chip - c + 16) % 16]
    by_col = jnp.concatenate([up[4, 0], up[4, 2], up[4, 1], up[4, 3]], axis=0)
    all4 = padded4[pl.ds(2, 16)].reshape(8, 2, PROBES, 128)
    nodes5 = dot(lanes([all4[:, 0], all4[:, 1]]).reshape(-1, 256), by_col)
    nodes5 = nodes5.astype(BF).reshape(8, PROBES, RANK)

    def raise_row(nodes, level):
        pairs = to_pairs(nodes).reshape(-1, 128)
        both = jnp.concatenate([up[level, 0], up[level, 1]], axis=0)
        return dot(pairs, both).astype(BF).reshape(-1, PROBES, RANK)

    nodes6 = raise_row(nodes5, 5)
    nodes7 = raise_row(nodes6, 6)
    gap = jnp.zeros((2, PROBES, RANK), BF)
    for padded, nodes in ((padded5, nodes5), (padded6, nodes6), (padded7, nodes7)):
        count = nodes.shape[0]
        padded[pl.ds(0, 2)] = gap
        padded[pl.ds(2, count)] = nodes
        padded[pl.ds(2 + count, 2)] = gap

    def far_row(padded, level):
        start = 2 * (col // (1 << (level - 2)))
        return dot(lanes([padded[start + k] for k in range(6)]), w5[level - 5])

    start4 = 2 * (chip // 2)
    far4 = dot(lanes([padded4[start4 + k] for k in range(6)]), w4[...])
    local = far_row(padded7, 7).astype(BF)
    local = (far_row(padded6, 6) + dot(local, down3[3])).astype(BF)
    local = (far_row(padded5, 5) + dot(local, down3[2])).astype(BF)
    local = (far4 + dot(local, down3[1])).astype(BF)
    local = (far3[...] + dot(local, down3[0])).astype(BF)
    local2 = (far2[...] + dot(local, down2[...])).astype(BF)
    spread1 = dot(local2, down1[...])
    spread1 = jnp.concatenate([spread1[:, :128], spread1[:, 128:]], axis=0)
    local1 = (far1[...] + spread1).astype(BF)
    spread0 = dot(local1, down0[...]).reshape(2, PROBES, 512)
    spread0 = jnp.stack([spread0[:, :, :256], spread0[:, :, 256:]], axis=1).reshape(-1, 256)
    local0 = (far0[...] + spread0).astype(BF)
    for e in (0, 1):
        far_sum = dot(local0[:, 128 * e : 128 * e + 128], wide[...]).reshape(4, PROBES, 256)
        for q in range(4):
            for f in (0, 1):
                part = far_sum[q, :, 128 * f : 128 * f + 128]
                out[e, 2 * q + f] = (near_sum[e, 2 * q + f] + part).astype(BF)


def route(rule, size_x, size_y):
    pairs = []
    for a in range(size_x):
        for b in range(size_y):
            x, y = rule(a, b)
            if 0 <= x < size_x and 0 <= y < size_y:
                pairs.append((a * size_y + b, x * size_y + y))
    return pairs


def across(core):
    return 1 if core else -1


def shards(probes, leaf_basis, up_transfer, down_transfer, coupling, far_ids):
    size_x, size_y = lax.axis_size("gx"), lax.axis_size("gy")
    both = ("gx", "gy")

    def move(value, rule):
        return lax.ppermute(value, both, route(rule, size_x, size_y))

    above = move(probes, lambda a, b: (a + 1, b))
    below = move(probes, lambda a, b: (a - 1, b))

    hbm = pl.BlockSpec(memory_space=pltpu.MemorySpace.HBM)
    block = (PROBES, 128)
    w0, w1, w2, w3, w4, w5, table, wide, up, down0, down1, down2, down3, own = call(
        prepare_kernel,
        [
            array((36 * RANK, 256)), array((36 * RANK, 128)), array((36 * RANK, 128)),
            array((24 * RANK, RANK)), array((12 * RANK, RANK)), array((3, 6 * RANK, RANK)),
            array((9 * 128, 128)), array((128, 256)), array(up_transfer.shape),
            array((128, 512)), array((128, 256)), array((RANK, 128)), array((4, RANK, RANK)),
            array(probes.shape),
        ],
        in_specs=[hbm] * 6,
        scratch=[
            pltpu.SMEM(far_ids.shape, jnp.int32), pltpu.VMEM(coupling.shape, BF),
            pltpu.VMEM(down_transfer.shape, BF), pltpu.VMEM(leaf_basis.shape[::-1], BF),
            pltpu.SemaphoreType.DMA, pltpu.SemaphoreType.DMA((8,)), pltpu.SemaphoreType.DMA((4,)),
        ],
    )(
        *[
            pltpu.with_memory_space_constraint(value, pltpu.MemorySpace.HBM)
            for value in (far_ids, coupling, up_transfer, down_transfer, leaf_basis.T, probes)
        ]
    )

    pack, low, mine, rim = call(
        first_kernel,
        [array((12,) + block), array((2,) + block), array((2, 4) + block), array((4, 4) + block)],
    )(own, above, below, wide, up)
    packed = move(pack, lambda a, b: (a, b ^ 1))
    sent = call(strip_kernel, array((16, 4) + block))(low, packed)
    gathered = lax.all_to_all(sent, "gx", 0, 0)

    far_out, level2, level3 = call(
        second_kernel,
        [array(block), array((8, 2) + block), array((4,) + block)],
    )(gathered, up)
    side_out = call(
        side_kernel,
        array((26,) + block),
        scratch=[pltpu.VMEM((20,) + block, BF), pltpu.VMEM((12,) + block, BF)],
        flops=1 << 32,
    )(gathered, own, mine, above, below, rim, level2, level3)

    chips = size_y // 2
    side = move(side_out, lambda a, b: (a, b + across(b % 2)))
    third = move(level3, lambda a, b: (a, b + 3 - 6 * (b % 2)))
    top = move(far_out, lambda a, b: (a, 2 * ((b // 2 + a) % chips) + b % 2))

    near_sum, far0, far1, far2, far3, tag = call(
        third_kernel,
        [
            array((2, 8) + block, F32), array((4 * PROBES, 256), F32),
            array((2 * PROBES, 128), F32), array((PROBES, 128), F32), array((PROBES, RANK), F32),
            array((8, 128), F32),
        ],
        scratch=[
            pltpu.VMEM(lead + block, BF)
            for lead in ((4, 10), (6, 6), (20, 4), (6, 4), (12, 2), (6, 3), (4, 3))
        ],
        flops=1,
        read=1,
    )(
        own, above, below, mine, packed, rim, gathered, level2, level3, side, third,
        w0, w1, w2, w3, table,
    )
    copies = call(copies_kernel, array((16,) + block))(top, tag)
    top = lax.all_to_all(copies, "gx", 0, 0)

    return call(
        fourth_kernel,
        array(probes.shape),
        scratch=[pltpu.VMEM((20,) + block, BF)]
        + [pltpu.VMEM((count + 4, PROBES, RANK), BF) for count in (8, 4, 2)],
    )(top, near_sum, far0, far1, far2, far3, w4, w5, wide, up, down0, down1, down2, down3)


def solution(mesh):
    in_specs = (P("gx", "gy", None, None), P(), P(), P(), P(), P())
    out_specs = P("gx", "gy", None, None)
    return jax.shard_map(shards, mesh=mesh, in_specs=in_specs, out_specs=out_specs, check_vma=False)
```

```python
import jax
import jax.numpy as jnp
from jax import lax
from jax.experimental import pallas as pl
from jax.experimental.pallas import tpu as pltpu
from jax.sharding import PartitionSpec as P

LEAF_ROWS = 8
LEAF_COLS = 16
RANK = 64
PROBES = 32
BF = jnp.bfloat16
F32 = jnp.float32

length_scale = 1.5


def dot(left, right):
    return jnp.dot(left, right, preferred_element_type=F32)


def lanes(parts):
    return jnp.concatenate(parts, axis=-1)


def block_slot(e, f, wr, wc):
    return 6 * wr + wc - 3 * min(max(wr - 1 - e, 0), 3) - (
        min(max(wc - 1 - f, 0), 3) if e + 1 <= wr <= e + 3 else 0
    )


def is_near(e, f, wr, wc):
    return e + 1 <= wr <= e + 3 and f + 1 <= wc <= f + 3


def places():
    row = lax.axis_index("gx")
    col = lax.axis_index("gy")
    return row, col, col // 2, col % 2


def prepare_kernel(
    ids_far, coupling_far, up_far, down_far, basis_far, own_far,
    w0, w1, w2, w3, w4, w5, table, wide, up, down0, down1, down2, down3, own,
    ids, coupling, down, basis, ids_sem, level_sems, sems,
):
    row, col, _, _ = places()
    first = pltpu.make_async_copy(ids_far, ids, ids_sem)
    first.start()
    levels = []
    for level in range(8):
        levels.append(
            pltpu.make_async_copy(coupling_far.at[level], coupling.at[level], level_sems.at[level])
        )
    levels[0].start()
    small = [
        pltpu.make_async_copy(source, target, sems.at[at])
        for at, (source, target) in enumerate(
            ((basis_far, basis), (own_far, own), (up_far, up), (down_far, down))
        )
    ]
    for copy in small:
        copy.start()
    for copy in levels[1:]:
        copy.start()

    size = LEAF_ROWS * LEAF_COLS
    theirs = lax.broadcasted_iota(jnp.int32, (size, size), 0)
    ours = lax.broadcasted_iota(jnp.int32, (size, size), 1)
    rows_apart = (theirs // LEAF_COLS - ours // LEAF_COLS).astype(F32)
    cols_apart = (theirs % LEAF_COLS - ours % LEAF_COLS).astype(F32)
    for u in (-1, 0, 1):
        for v in (-1, 0, 1):
            apart_row = rows_apart + float(u * LEAF_ROWS)
            apart_col = cols_apart + float(v * LEAF_COLS)
            scaled = jnp.sqrt(3.0 * (apart_row * apart_row + apart_col * apart_col)) / length_scale
            value = (1.0 + scaled) * jnp.exp(-scaled)
            table[pl.ds((3 * (u + 1) + v + 1) * size, size), :] = value.astype(BF)

    def pair(level, e, wr, wc):
        halves = []
        for f in (0, 1):
            if is_near(e, f, wr, wc):
                halves.append(jnp.zeros((RANK, RANK), BF))
            else:
                halves.append(coupling[level, ids[level, 2 * e + f, block_slot(e, f, wr, wc)]])
        return lanes(halves)

    first.wait()
    levels[0].wait()
    for wr in range(6):
        for wc in range(6):
            at = pl.ds((6 * wr + wc) * RANK, RANK)
            for e in (0, 1):
                w0[at, pl.ds(128 * e, 128)] = pair(0, e, wr, wc)

    for level, out, bit in ((1, w1, row % 2), (2, w2, (row // 2) % 2)):
        levels[level].wait()
        for e in (0, 1):

            @pl.when(bit == e)
            def _(level=level, out=out, e=e):
                for wr in range(6):
                    for wc in range(6):
                        out[pl.ds((6 * wr + wc) * RANK, RANK), :] = pair(level, e, wr, wc)

    def single(level, e, f, wr, wc):
        row_in = jnp.logical_and(wr >= e + 1, wr <= e + 3)
        col_in = jnp.logical_and(wc >= f + 1, wc <= f + 3)
        skipped = 3 * jnp.clip(wr - 1 - e, 0, 3) + jnp.where(row_in, jnp.clip(wc - 1 - f, 0, 3), 0)
        slot = jnp.clip(6 * wr + wc - skipped, 0, 26)
        keep = jnp.where(jnp.logical_and(row_in, col_in), 0.0, 1.0)
        block = coupling[level, ids[level, 2 * e + f, slot]]
        return block * jnp.full((RANK, RANK), keep, F32).astype(BF)

    levels[3].wait()
    e3, f3 = (row // 4) % 2, col % 2
    first3 = 2 - 2 * (row // 8)
    for r in range(4):
        for wc in range(6):
            w3[pl.ds((6 * r + wc) * RANK, RANK), :] = single(3, e3, f3, r + first3, wc)
    levels[4].wait()
    e4, f4 = row // 8, (col // 2) % 2
    for wc in range(6):
        for r in range(2):
            w4[pl.ds((2 * wc + r) * RANK, RANK), :] = single(4, e4, f4, jnp.int32(2 + r), wc)
    for level in (5, 6, 7):
        levels[level].wait()
        f = (col // (1 << (level - 3))) % 2
        for wc in range(6):
            w5[level - 5, pl.ds(wc * RANK, RANK), :] = single(
                level, jnp.int32(0), f, jnp.int32(2), wc
            )

    for copy in small:
        copy.wait()
    blank = jnp.zeros_like(basis)
    wide[...] = jnp.concatenate([lanes([basis[...], blank]), lanes([blank, basis[...]])], axis=0)
    all0 = lanes([down[0, k] for k in range(4)])
    none0 = jnp.zeros_like(all0)
    down0[...] = jnp.concatenate([lanes([all0, none0]), lanes([none0, all0])], axis=0)
    e1, e2 = row % 2, (row // 2) % 2
    both1 = lanes([down[1, 2 * e1], down[1, 2 * e1 + 1]])
    none1 = jnp.zeros_like(both1)
    down1[...] = jnp.concatenate([lanes([both1, none1]), lanes([none1, both1])], axis=0)
    down2[...] = lanes([down[2, 2 * e2], down[2, 2 * e2 + 1]])
    for level in (3, 4, 5, 6):
        e = (row // (1 << (level - 1))) % 2
        f = (col // (1 << (level - 3))) % 2
        down3[level - 3] = down[level, 2 * e + f]


def array(shape, kind=BF):
    return jax.ShapeDtypeStruct(shape, kind)


def call(kernel, out_shape, scratch=(), flops=1 << 24, read=1 << 21, **specs):
    return pl.pallas_call(
        kernel,
        out_shape=out_shape,
        **specs,
        scratch_shapes=list(scratch),
        compiler_params=pltpu.CompilerParams(vmem_limit_bytes=16 << 20),
        cost_estimate=pl.CostEstimate(flops=flops, bytes_accessed=read, transcendentals=0),
    )


def leaf_coeffs(tile, wide_basis):
    rows = tile.shape[0]
    split = tile.reshape(rows, 4, 2, PROBES, 128)
    joined = lanes([split[:, :, 0], split[:, :, 1]]).reshape(-1, 256)
    coeffs = lax.dot_general(
        joined, wide_basis, (((1,), (1,)), ((), ())), preferred_element_type=F32
    )
    return coeffs.astype(BF).reshape(rows, 4, PROBES, 128)


def to_pairs(nodes):
    lead = nodes.shape[:-3]
    split = nodes.reshape(lead + (nodes.shape[-3] // 2, 2, PROBES, RANK))
    return lanes([split[..., 0, :, :], split[..., 1, :, :]])


def raise_pairs(pairs, transfer):
    rows, count = pairs.shape[:2]
    split = pairs.reshape(rows // 2, 2, count, PROBES, 128)
    joined = lanes([split[:, 0], split[:, 1]]).reshape(-1, 256)
    return dot(joined, transfer).astype(BF).reshape(rows // 2, count, PROBES, RANK)


def first_kernel(own, above, below, wide, up, pack, low, mine, rim):
    _, _, _, core = places()
    coeffs = leaf_coeffs(own[...], wide[...])
    pairs = to_pairs(raise_pairs(coeffs, up[0].reshape(4 * RANK, RANK))[0])
    mine[...] = coeffs
    rim[pl.ds(0, 2)] = leaf_coeffs(above[...], wide[...])
    rim[pl.ds(2, 2)] = leaf_coeffs(below[...], wide[...])
    low[...] = pairs

    edge_pair = 3 - 3 * core
    edge_col = 7 - 7 * core
    pack[pl.ds(0, 2)] = pairs
    pack[2] = mine[0, edge_pair]
    pack[3] = mine[1, edge_pair]
    pack[4] = own[0, edge_col]
    pack[5] = own[1, edge_col]
    pack[6] = above[1, edge_col]
    pack[7] = below[0, edge_col]
    for r in range(4):
        pack[8 + r] = rim[r, edge_pair]


def strip_kernel(low, packed, sent):
    _, _, _, core = places()
    for peer in range(16):
        sent[peer, pl.ds(2 * core, 2)] = low[...]
        sent[peer, pl.ds(2 - 2 * core, 2)] = packed[pl.ds(0, 2)]


def second_kernel(gathered, up, far_out, level2, level3):
    pairs2 = to_pairs(raise_pairs(gathered[...], up[1].reshape(4 * RANK, RANK)))
    pairs3 = to_pairs(raise_pairs(pairs2, up[2].reshape(4 * RANK, RANK)))[:, 0]
    nodes4 = raise_pairs(pairs3[:, None], up[3].reshape(4 * RANK, RANK))
    far_out[...] = lanes([nodes4[0, 0], nodes4[1, 0]])
    level2[...] = pairs2
    level3[...] = pairs3


def side_kernel(gathered, own, mine, above, below, rim, level2, level3, side_out, padded1, padded2):
    row, _, _, core = places()
    edge_pair = 3 * core
    edge_col = 7 * core
    nothing = jnp.zeros((2, PROBES, 128), BF)
    padded1[pl.ds(0, 2)] = nothing
    padded1[pl.ds(18, 2)] = nothing
    padded2[pl.ds(0, 2)] = nothing
    padded2[pl.ds(10, 2)] = nothing
    for r in range(16):
        padded1[r + 2] = gathered[r, edge_pair]
    for r in range(8):
        padded2[r + 2] = level2[r, core]
    side_out[0] = above[1, edge_col]
    side_out[1] = own[0, edge_col]
    side_out[2] = own[1, edge_col]
    side_out[3] = below[0, edge_col]
    side_out[4] = rim[0, edge_pair]
    side_out[5] = rim[1, edge_pair]
    side_out[6] = mine[0, edge_pair]
    side_out[7] = mine[1, edge_pair]
    side_out[8] = rim[2, edge_pair]
    side_out[9] = rim[3, edge_pair]
    side_out[pl.ds(10, 6)] = padded1[pl.ds(2 * (row // 2), 6)]
    side_out[pl.ds(16, 6)] = padded2[pl.ds(2 * (row // 4), 6)]
    side_out[pl.ds(22, 4)] = level3[...]


def third_kernel(
    own, above, below, mine, packed, rim, gathered, level2, level3,
    side, third, far_out, w0, w1, w2, w3, table,
    near_sum, far0, far1, far2, far3, copies,
    near, window0, padded1, window1, padded2, window2, window3,
):
    row, _, _, core = places()

    window0[pl.ds(0, 2), pl.ds(1, 4)] = rim[pl.ds(0, 2)]
    window0[pl.ds(2, 2), pl.ds(1, 4)] = mine[...]
    window0[pl.ds(4, 2), pl.ds(1, 4)] = rim[pl.ds(2, 2)]
    for w in range(6):
        window0[w, 5 * core] = side[4 + w]
    for r in range(2):
        window0[r, 5 - 5 * core] = packed[8 + r]
        window0[2 + r, 5 - 5 * core] = packed[2 + r]
        window0[4 + r, 5 - 5 * core] = packed[10 + r]
    far0[...] = dot(
        lanes([window0[w, pl.ds(k, 4)].reshape(-1, 128) for w in range(6) for k in range(3)]),
        w0[...],
    )

    near[0, pl.ds(1, 8)] = above[1]
    near[1, pl.ds(1, 8)] = own[0]
    near[2, pl.ds(1, 8)] = own[1]
    near[3, pl.ds(1, 8)] = below[0]
    for r in range(4):
        near[r, 9 * core] = side[r]
    near[0, 9 - 9 * core] = packed[6]
    near[1, 9 - 9 * core] = packed[4]
    near[2, 9 - 9 * core] = packed[5]
    near[3, 9 - 9 * core] = packed[7]
    for e in (0, 1):
        joined = lanes([near[e + u, pl.ds(v, 8)].reshape(-1, 128) for u in range(3) for v in range(3)])
        near_sum[e] = dot(joined, table[...]).reshape(8, PROBES, 128)

    empty1 = jnp.zeros((2, 4, PROBES, 128), BF)
    padded1[pl.ds(0, 2)] = empty1
    padded1[pl.ds(2, 16)] = gathered[...]
    padded1[pl.ds(18, 2)] = empty1
    for w in range(6):
        for k in range(3):
            window1[w, k + 1 - core] = padded1[2 * (row // 2) + w, k + core]
        window1[w, 3 * core] = side[10 + w]
    far1[...] = dot(
        lanes([window1[w, pl.ds(k, 2)].reshape(-1, 128) for w in range(6) for k in range(3)]),
        w1[...],
    )

    empty2 = jnp.zeros((2, 2, PROBES, 128), BF)
    padded2[pl.ds(0, 2)] = empty2
    padded2[pl.ds(2, 8)] = level2[...]
    padded2[pl.ds(10, 2)] = empty2
    for w in range(6):
        for k in range(2):
            window2[w, k + 1 - core] = padded2[2 * (row // 4) + w, k]
        window2[w, 2 * core] = side[16 + w]
    far2[...] = dot(lanes([window2[w, k] for w in range(6) for k in range(3)]), w2[...])

    for r in range(4):
        window3[r, 2 * core] = side[22 + r]
        window3[r, 1] = level3[r]
        window3[r, 2 - 2 * core] = third[r]
    far3[...] = dot(lanes([window3[r, k] for r in range(4) for k in range(3)]), w3[...])
    for peer in range(16):
        copies[peer] = far_out[...]


def fourth_kernel(
    top, near_sum, far0, far1, far2, far3, w4, w5, wide, up, down0, down1, down2, down3,
    out,
    padded4, padded5, padded6, padded7,
):
    _, col, chip, _ = places()

    blank = jnp.zeros((2, PROBES, 128), BF)
    padded4[pl.ds(0, 2)] = blank
    padded4[pl.ds(18, 2)] = blank
    for c in range(16):
        padded4[c + 2] = top[c]
    by_col = jnp.concatenate([up[4, 0], up[4, 2], up[4, 1], up[4, 3]], axis=0)
    all4 = padded4[pl.ds(2, 16)].reshape(8, 2, PROBES, 128)
    nodes5 = dot(lanes([all4[:, 0], all4[:, 1]]).reshape(-1, 256), by_col)
    nodes5 = nodes5.astype(BF).reshape(8, PROBES, RANK)

    def raise_row(nodes, level):
        pairs = to_pairs(nodes).reshape(-1, 128)
        both = jnp.concatenate([up[level, 0], up[level, 1]], axis=0)
        return dot(pairs, both).astype(BF).reshape(-1, PROBES, RANK)

    nodes6 = raise_row(nodes5, 5)
    nodes7 = raise_row(nodes6, 6)
    gap = jnp.zeros((2, PROBES, RANK), BF)
    for padded, nodes in ((padded5, nodes5), (padded6, nodes6), (padded7, nodes7)):
        count = nodes.shape[0]
        padded[pl.ds(0, 2)] = gap
        padded[pl.ds(2, count)] = nodes
        padded[pl.ds(2 + count, 2)] = gap

    def far_row(padded, level):
        start = 2 * (col // (1 << (level - 2)))
        return dot(lanes([padded[start + k] for k in range(6)]), w5[level - 5])

    start4 = 2 * (chip // 2)
    far4 = dot(lanes([padded4[start4 + k] for k in range(6)]), w4[...])
    local = far_row(padded7, 7).astype(BF)
    local = (far_row(padded6, 6) + dot(local, down3[3])).astype(BF)
    local = (far_row(padded5, 5) + dot(local, down3[2])).astype(BF)
    local = (far4 + dot(local, down3[1])).astype(BF)
    local = (far3[...] + dot(local, down3[0])).astype(BF)
    local2 = (far2[...] + dot(local, down2[...])).astype(BF)
    spread1 = dot(local2, down1[...])
    spread1 = jnp.concatenate([spread1[:, :128], spread1[:, 128:]], axis=0)
    local1 = (far1[...] + spread1).astype(BF)
    spread0 = dot(local1, down0[...]).reshape(2, PROBES, 512)
    spread0 = jnp.stack([spread0[:, :, :256], spread0[:, :, 256:]], axis=1).reshape(-1, 256)
    local0 = (far0[...] + spread0).astype(BF)
    for e in (0, 1):
        far_sum = dot(local0[:, 128 * e : 128 * e + 128], wide[...]).reshape(4, PROBES, 256)
        for q in range(4):
            for f in (0, 1):
                part = far_sum[q, :, 128 * f : 128 * f + 128]
                out[e, 2 * q + f] = (near_sum[e, 2 * q + f] + part).astype(BF)


def route(rule, size_x, size_y):
    pairs = []
    for a in range(size_x):
        for b in range(size_y):
            x, y = rule(a, b)
            if 0 <= x < size_x and 0 <= y < size_y:
                pairs.append((a * size_y + b, x * size_y + y))
    return pairs


def across(core):
    return 1 if core else -1


def shards(probes, leaf_basis, up_transfer, down_transfer, coupling, far_ids):
    size_x, size_y = lax.axis_size("gx"), lax.axis_size("gy")
    both = ("gx", "gy")

    def move(value, rule):
        return lax.ppermute(value, both, route(rule, size_x, size_y))

    above = move(probes, lambda a, b: (a + 1, b))
    below = move(probes, lambda a, b: (a - 1, b))

    hbm = pl.BlockSpec(memory_space=pltpu.MemorySpace.HBM)
    block = (PROBES, 128)
    w0, w1, w2, w3, w4, w5, table, wide, up, down0, down1, down2, down3, own = call(
        prepare_kernel,
        [
            array((36 * RANK, 256)), array((36 * RANK, 128)), array((36 * RANK, 128)),
            array((24 * RANK, RANK)), array((12 * RANK, RANK)), array((3, 6 * RANK, RANK)),
            array((9 * 128, 128)), array((128, 256)), array(up_transfer.shape),
            array((128, 512)), array((128, 256)), array((RANK, 128)), array((4, RANK, RANK)),
            array(probes.shape),
        ],
        in_specs=[hbm] * 6,
        scratch=[
            pltpu.SMEM(far_ids.shape, jnp.int32), pltpu.VMEM(coupling.shape, BF),
            pltpu.VMEM(down_transfer.shape, BF), pltpu.VMEM(leaf_basis.shape[::-1], BF),
            pltpu.SemaphoreType.DMA, pltpu.SemaphoreType.DMA((8,)), pltpu.SemaphoreType.DMA((4,)),
        ],
    )(
        *[
            pltpu.with_memory_space_constraint(value, pltpu.MemorySpace.HBM)
            for value in (far_ids, coupling, up_transfer, down_transfer, leaf_basis.T, probes)
        ]
    )

    pack, low, mine, rim = call(
        first_kernel,
        [array((12,) + block), array((2,) + block), array((2, 4) + block), array((4, 4) + block)],
    )(own, above, below, wide, up)
    packed = move(pack, lambda a, b: (a, b ^ 1))
    sent = call(strip_kernel, array((16, 4) + block))(low, packed)
    gathered = lax.all_to_all(sent, "gx", 0, 0)

    far_out, level2, level3 = call(
        second_kernel,
        [array(block), array((8, 2) + block), array((4,) + block)],
    )(gathered, up)
    side_out = call(
        side_kernel,
        array((26,) + block),
        scratch=[pltpu.VMEM((20,) + block, BF), pltpu.VMEM((12,) + block, BF)],
        flops=1 << 32,
    )(gathered, own, mine, above, below, rim, level2, level3)

    chips = size_y // 2
    side = move(side_out, lambda a, b: (a, b + across(b % 2)))
    third = move(level3, lambda a, b: (a, b + 3 - 6 * (b % 2)))

    near_sum, far0, far1, far2, far3, copies = call(
        third_kernel,
        [
            array((2, 8) + block, F32), array((4 * PROBES, 256), F32),
            array((2 * PROBES, 128), F32), array((PROBES, 128), F32), array((PROBES, RANK), F32),
            array((16,) + block),
        ],
        scratch=[
            pltpu.VMEM(lead + block, BF)
            for lead in ((4, 10), (6, 6), (20, 4), (6, 4), (12, 2), (6, 3), (4, 3))
        ],
        flops=1,
        read=1,
    )(
        own, above, below, mine, packed, rim, gathered, level2, level3, side, third, far_out,
        w0, w1, w2, w3, table,
    )
    columns = [[2 * chip + core for chip in range(chips)] for core in (0, 1)]
    top = lax.all_to_all(copies, "gy", 0, 0, axis_index_groups=columns)

    return call(
        fourth_kernel,
        array(probes.shape),
        scratch=[pltpu.VMEM((20,) + block, BF)]
        + [pltpu.VMEM((count + 4, PROBES, RANK), BF) for count in (8, 4, 2)],
    )(top, near_sum, far0, far1, far2, far3, w4, w5, wide, up, down0, down1, down2, down3)


def solution(mesh):
    in_specs = (P("gx", "gy", None, None), P(), P(), P(), P(), P())
    out_specs = P("gx", "gy", None, None)
    return jax.shard_map(shards, mesh=mesh, in_specs=in_specs, out_specs=out_specs, check_vma=False)
```

```python
import jax
import jax.numpy as jnp
from jax import lax
from jax.experimental import pallas as pl
from jax.experimental.pallas import tpu as pltpu
from jax.sharding import PartitionSpec as P

LEAF_ROWS = 8
LEAF_COLS = 16
RANK = 64
PROBES = 32
BF = jnp.bfloat16
F32 = jnp.float32

length_scale = 1.5


def dot(left, right):
    return jnp.dot(left, right, preferred_element_type=F32)


def lanes(parts):
    return jnp.concatenate(parts, axis=-1)


def block_slot(e, f, wr, wc):
    return 6 * wr + wc - 3 * min(max(wr - 1 - e, 0), 3) - (
        min(max(wc - 1 - f, 0), 3) if e + 1 <= wr <= e + 3 else 0
    )


def is_near(e, f, wr, wc):
    return e + 1 <= wr <= e + 3 and f + 1 <= wc <= f + 3


def places():
    row = lax.axis_index("gx")
    col = lax.axis_index("gy")
    return row, col, col // 2, col % 2


def prepare_kernel(
    ids_far, coupling_far, up_far, down_far, basis_far, own_far,
    w0, w1, w2, w3, w4, w5, table, wide, up, down0, down1, down2, down3, own,
    ids, coupling, down, basis, ids_sem, level_sems, sems,
):
    row, col, _, _ = places()
    first = pltpu.make_async_copy(ids_far, ids, ids_sem)
    first.start()
    levels = []
    for level in range(8):
        levels.append(
            pltpu.make_async_copy(coupling_far.at[level], coupling.at[level], level_sems.at[level])
        )
    levels[0].start()
    small = [
        pltpu.make_async_copy(source, target, sems.at[at])
        for at, (source, target) in enumerate(
            ((basis_far, basis), (own_far, own), (up_far, up), (down_far, down))
        )
    ]
    for copy in small:
        copy.start()
    for copy in levels[1:]:
        copy.start()

    size = LEAF_ROWS * LEAF_COLS
    theirs = lax.broadcasted_iota(jnp.int32, (size, size), 0)
    ours = lax.broadcasted_iota(jnp.int32, (size, size), 1)
    rows_apart = (theirs // LEAF_COLS - ours // LEAF_COLS).astype(F32)
    cols_apart = (theirs % LEAF_COLS - ours % LEAF_COLS).astype(F32)
    for u in (-1, 0, 1):
        for v in (-1, 0, 1):
            apart_row = rows_apart + float(u * LEAF_ROWS)
            apart_col = cols_apart + float(v * LEAF_COLS)
            scaled = jnp.sqrt(3.0 * (apart_row * apart_row + apart_col * apart_col)) / length_scale
            value = (1.0 + scaled) * jnp.exp(-scaled)
            table[pl.ds((3 * (u + 1) + v + 1) * size, size), :] = value.astype(BF)

    def pair(level, e, wr, wc):
        halves = []
        for f in (0, 1):
            if is_near(e, f, wr, wc):
                halves.append(jnp.zeros((RANK, RANK), BF))
            else:
                halves.append(coupling[level, ids[level, 2 * e + f, block_slot(e, f, wr, wc)]])
        return lanes(halves)

    first.wait()
    levels[0].wait()
    for wr in range(6):
        for wc in range(6):
            at = pl.ds((6 * wr + wc) * RANK, RANK)
            for e in (0, 1):
                w0[at, pl.ds(128 * e, 128)] = pair(0, e, wr, wc)

    for level, out, bit in ((1, w1, row % 2), (2, w2, (row // 2) % 2)):
        levels[level].wait()
        for e in (0, 1):

            @pl.when(bit == e)
            def _(level=level, out=out, e=e):
                for wr in range(6):
                    for wc in range(6):
                        out[pl.ds((6 * wr + wc) * RANK, RANK), :] = pair(level, e, wr, wc)

    def single(level, e, f, wr, wc):
        row_in = jnp.logical_and(wr >= e + 1, wr <= e + 3)
        col_in = jnp.logical_and(wc >= f + 1, wc <= f + 3)
        skipped = 3 * jnp.clip(wr - 1 - e, 0, 3) + jnp.where(row_in, jnp.clip(wc - 1 - f, 0, 3), 0)
        slot = jnp.clip(6 * wr + wc - skipped, 0, 26)
        keep = jnp.where(jnp.logical_and(row_in, col_in), 0.0, 1.0)
        block = coupling[level, ids[level, 2 * e + f, slot]]
        return block * jnp.full((RANK, RANK), keep, F32).astype(BF)

    levels[3].wait()
    e3, f3 = (row // 4) % 2, col % 2
    first3 = 2 - 2 * (row // 8)
    for r in range(4):
        for wc in range(6):
            w3[pl.ds((6 * r + wc) * RANK, RANK), :] = single(3, e3, f3, r + first3, wc)
    levels[4].wait()
    e4, f4 = row // 8, (col // 2) % 2
    for wc in range(6):
        for r in range(2):
            w4[pl.ds((2 * wc + r) * RANK, RANK), :] = single(4, e4, f4, jnp.int32(2 + r), wc)
    for level in (5, 6, 7):
        levels[level].wait()
        f = (col // (1 << (level - 3))) % 2
        for wc in range(6):
            w5[level - 5, pl.ds(wc * RANK, RANK), :] = single(
                level, jnp.int32(0), f, jnp.int32(2), wc
            )

    for copy in small:
        copy.wait()
    blank = jnp.zeros_like(basis)
    wide[...] = jnp.concatenate([lanes([basis[...], blank]), lanes([blank, basis[...]])], axis=0)
    all0 = lanes([down[0, k] for k in range(4)])
    none0 = jnp.zeros_like(all0)
    down0[...] = jnp.concatenate([lanes([all0, none0]), lanes([none0, all0])], axis=0)
    e1, e2 = row % 2, (row // 2) % 2
    both1 = lanes([down[1, 2 * e1], down[1, 2 * e1 + 1]])
    none1 = jnp.zeros_like(both1)
    down1[...] = jnp.concatenate([lanes([both1, none1]), lanes([none1, both1])], axis=0)
    down2[...] = lanes([down[2, 2 * e2], down[2, 2 * e2 + 1]])
    for level in (3, 4, 5, 6):
        e = (row // (1 << (level - 1))) % 2
        f = (col // (1 << (level - 3))) % 2
        down3[level - 3] = down[level, 2 * e + f]


def array(shape, kind=BF):
    return jax.ShapeDtypeStruct(shape, kind)


def call(kernel, out_shape, scratch=(), flops=1 << 24, read=1 << 21, **specs):
    return pl.pallas_call(
        kernel,
        out_shape=out_shape,
        **specs,
        scratch_shapes=list(scratch),
        compiler_params=pltpu.CompilerParams(vmem_limit_bytes=16 << 20),
        cost_estimate=pl.CostEstimate(flops=flops, bytes_accessed=read, transcendentals=0),
    )


def leaf_coeffs(tile, wide_basis):
    rows = tile.shape[0]
    split = tile.reshape(rows, 4, 2, PROBES, 128)
    joined = lanes([split[:, :, 0], split[:, :, 1]]).reshape(-1, 256)
    coeffs = lax.dot_general(
        joined, wide_basis, (((1,), (1,)), ((), ())), preferred_element_type=F32
    )
    return coeffs.astype(BF).reshape(rows, 4, PROBES, 128)


def to_pairs(nodes):
    lead = nodes.shape[:-3]
    split = nodes.reshape(lead + (nodes.shape[-3] // 2, 2, PROBES, RANK))
    return lanes([split[..., 0, :, :], split[..., 1, :, :]])


def raise_pairs(pairs, transfer):
    rows, count = pairs.shape[:2]
    split = pairs.reshape(rows // 2, 2, count, PROBES, 128)
    joined = lanes([split[:, 0], split[:, 1]]).reshape(-1, 256)
    return dot(joined, transfer).astype(BF).reshape(rows // 2, count, PROBES, RANK)


def first_kernel(own, above, below, wide, up, pack, low, mine, rim):
    _, _, _, core = places()
    coeffs = leaf_coeffs(own[...], wide[...])
    pairs = to_pairs(raise_pairs(coeffs, up[0].reshape(4 * RANK, RANK))[0])
    mine[...] = coeffs
    rim[pl.ds(0, 2)] = leaf_coeffs(above[...], wide[...])
    rim[pl.ds(2, 2)] = leaf_coeffs(below[...], wide[...])
    low[...] = pairs

    edge_pair = 3 - 3 * core
    edge_col = 7 - 7 * core
    pack[pl.ds(0, 2)] = pairs
    pack[2] = mine[0, edge_pair]
    pack[3] = mine[1, edge_pair]
    pack[4] = own[0, edge_col]
    pack[5] = own[1, edge_col]
    pack[6] = above[1, edge_col]
    pack[7] = below[0, edge_col]
    for r in range(4):
        pack[8 + r] = rim[r, edge_pair]


def strip_kernel(low, packed, sent):
    _, _, _, core = places()
    for peer in range(16):
        sent[peer, pl.ds(2 * core, 2)] = low[...]
        sent[peer, pl.ds(2 - 2 * core, 2)] = packed[pl.ds(0, 2)]


def second_kernel(gathered, up, far_out, level2, level3):
    pairs2 = to_pairs(raise_pairs(gathered[...], up[1].reshape(4 * RANK, RANK)))
    pairs3 = to_pairs(raise_pairs(pairs2, up[2].reshape(4 * RANK, RANK)))[:, 0]
    nodes4 = raise_pairs(pairs3[:, None], up[3].reshape(4 * RANK, RANK))
    far_out[...] = lanes([nodes4[0, 0], nodes4[1, 0]])
    level2[...] = pairs2
    level3[...] = pairs3


def side_kernel(gathered, own, mine, above, below, rim, level2, level3, side_out, padded1, padded2):
    row, _, _, core = places()
    edge_pair = 3 * core
    edge_col = 7 * core
    nothing = jnp.zeros((2, PROBES, 128), BF)
    padded1[pl.ds(0, 2)] = nothing
    padded1[pl.ds(18, 2)] = nothing
    padded2[pl.ds(0, 2)] = nothing
    padded2[pl.ds(10, 2)] = nothing
    for r in range(16):
        padded1[r + 2] = gathered[r, edge_pair]
    for r in range(8):
        padded2[r + 2] = level2[r, core]
    side_out[0] = above[1, edge_col]
    side_out[1] = own[0, edge_col]
    side_out[2] = own[1, edge_col]
    side_out[3] = below[0, edge_col]
    side_out[4] = rim[0, edge_pair]
    side_out[5] = rim[1, edge_pair]
    side_out[6] = mine[0, edge_pair]
    side_out[7] = mine[1, edge_pair]
    side_out[8] = rim[2, edge_pair]
    side_out[9] = rim[3, edge_pair]
    side_out[pl.ds(10, 6)] = padded1[pl.ds(2 * (row // 2), 6)]
    side_out[pl.ds(16, 6)] = padded2[pl.ds(2 * (row // 4), 6)]
    side_out[pl.ds(22, 4)] = level3[...]


def third_kernel(
    own, above, below, mine, packed, rim, gathered, level2, level3,
    side, third, arrived, w0, w1, w2, w3, table,
    near_sum, far0, far1, far2, far3, copies,
    near, window0, padded1, window1, padded2, window2, window3,
):
    row, _, _, core = places()

    window0[pl.ds(0, 2), pl.ds(1, 4)] = rim[pl.ds(0, 2)]
    window0[pl.ds(2, 2), pl.ds(1, 4)] = mine[...]
    window0[pl.ds(4, 2), pl.ds(1, 4)] = rim[pl.ds(2, 2)]
    for w in range(6):
        window0[w, 5 * core] = side[4 + w]
    for r in range(2):
        window0[r, 5 - 5 * core] = packed[8 + r]
        window0[2 + r, 5 - 5 * core] = packed[2 + r]
        window0[4 + r, 5 - 5 * core] = packed[10 + r]
    far0[...] = dot(
        lanes([window0[w, pl.ds(k, 4)].reshape(-1, 128) for w in range(6) for k in range(3)]),
        w0[...],
    )

    near[0, pl.ds(1, 8)] = above[1]
    near[1, pl.ds(1, 8)] = own[0]
    near[2, pl.ds(1, 8)] = own[1]
    near[3, pl.ds(1, 8)] = below[0]
    for r in range(4):
        near[r, 9 * core] = side[r]
    near[0, 9 - 9 * core] = packed[6]
    near[1, 9 - 9 * core] = packed[4]
    near[2, 9 - 9 * core] = packed[5]
    near[3, 9 - 9 * core] = packed[7]
    for e in (0, 1):
        joined = lanes([near[e + u, pl.ds(v, 8)].reshape(-1, 128) for u in range(3) for v in range(3)])
        near_sum[e] = dot(joined, table[...]).reshape(8, PROBES, 128)

    empty1 = jnp.zeros((2, 4, PROBES, 128), BF)
    padded1[pl.ds(0, 2)] = empty1
    padded1[pl.ds(2, 16)] = gathered[...]
    padded1[pl.ds(18, 2)] = empty1
    for w in range(6):
        for k in range(3):
            window1[w, k + 1 - core] = padded1[2 * (row // 2) + w, k + core]
        window1[w, 3 * core] = side[10 + w]
    far1[...] = dot(
        lanes([window1[w, pl.ds(k, 2)].reshape(-1, 128) for w in range(6) for k in range(3)]),
        w1[...],
    )

    empty2 = jnp.zeros((2, 2, PROBES, 128), BF)
    padded2[pl.ds(0, 2)] = empty2
    padded2[pl.ds(2, 8)] = level2[...]
    padded2[pl.ds(10, 2)] = empty2
    for w in range(6):
        for k in range(2):
            window2[w, k + 1 - core] = padded2[2 * (row // 4) + w, k]
        window2[w, 2 * core] = side[16 + w]
    far2[...] = dot(lanes([window2[w, k] for w in range(6) for k in range(3)]), w2[...])

    for r in range(4):
        window3[r, 2 * core] = side[22 + r]
        window3[r, 1] = level3[r]
        window3[r, 2 - 2 * core] = third[r]
    far3[...] = dot(lanes([window3[r, k] for r in range(4) for k in range(3)]), w3[...])
    for peer in range(16):
        copies[peer] = arrived[...]


def arrival_kernel(block, out):
    out[...] = block[...]


def fourth_kernel(
    top, near_sum, far0, far1, far2, far3, w4, w5, wide, up, down0, down1, down2, down3,
    out,
    padded4, padded5, padded6, padded7,
):
    _, col, chip, _ = places()

    blank = jnp.zeros((2, PROBES, 128), BF)
    padded4[pl.ds(0, 2)] = blank
    padded4[pl.ds(18, 2)] = blank
    for c in range(16):
        padded4[c + 2] = top[(chip - c + 16) % 16]
    by_col = jnp.concatenate([up[4, 0], up[4, 2], up[4, 1], up[4, 3]], axis=0)
    all4 = padded4[pl.ds(2, 16)].reshape(8, 2, PROBES, 128)
    nodes5 = dot(lanes([all4[:, 0], all4[:, 1]]).reshape(-1, 256), by_col)
    nodes5 = nodes5.astype(BF).reshape(8, PROBES, RANK)

    def raise_row(nodes, level):
        pairs = to_pairs(nodes).reshape(-1, 128)
        both = jnp.concatenate([up[level, 0], up[level, 1]], axis=0)
        return dot(pairs, both).astype(BF).reshape(-1, PROBES, RANK)

    nodes6 = raise_row(nodes5, 5)
    nodes7 = raise_row(nodes6, 6)
    gap = jnp.zeros((2, PROBES, RANK), BF)
    for padded, nodes in ((padded5, nodes5), (padded6, nodes6), (padded7, nodes7)):
        count = nodes.shape[0]
        padded[pl.ds(0, 2)] = gap
        padded[pl.ds(2, count)] = nodes
        padded[pl.ds(2 + count, 2)] = gap

    def far_row(padded, level):
        start = 2 * (col // (1 << (level - 2)))
        return dot(lanes([padded[start + k] for k in range(6)]), w5[level - 5])

    start4 = 2 * (chip // 2)
    far4 = dot(lanes([padded4[start4 + k] for k in range(6)]), w4[...])
    local = far_row(padded7, 7).astype(BF)
    local = (far_row(padded6, 6) + dot(local, down3[3])).astype(BF)
    local = (far_row(padded5, 5) + dot(local, down3[2])).astype(BF)
    local = (far4 + dot(local, down3[1])).astype(BF)
    local = (far3[...] + dot(local, down3[0])).astype(BF)
    local2 = (far2[...] + dot(local, down2[...])).astype(BF)
    spread1 = dot(local2, down1[...])
    spread1 = jnp.concatenate([spread1[:, :128], spread1[:, 128:]], axis=0)
    local1 = (far1[...] + spread1).astype(BF)
    spread0 = dot(local1, down0[...]).reshape(2, PROBES, 512)
    spread0 = jnp.stack([spread0[:, :, :256], spread0[:, :, 256:]], axis=1).reshape(-1, 256)
    local0 = (far0[...] + spread0).astype(BF)
    for e in (0, 1):
        far_sum = dot(local0[:, 128 * e : 128 * e + 128], wide[...]).reshape(4, PROBES, 256)
        for q in range(4):
            for f in (0, 1):
                part = far_sum[q, :, 128 * f : 128 * f + 128]
                out[e, 2 * q + f] = (near_sum[e, 2 * q + f] + part).astype(BF)


def route(rule, size_x, size_y):
    pairs = []
    for a in range(size_x):
        for b in range(size_y):
            x, y = rule(a, b)
            if 0 <= x < size_x and 0 <= y < size_y:
                pairs.append((a * size_y + b, x * size_y + y))
    return pairs


def across(core):
    return 1 if core else -1


def shards(probes, leaf_basis, up_transfer, down_transfer, coupling, far_ids):
    size_x, size_y = lax.axis_size("gx"), lax.axis_size("gy")
    both = ("gx", "gy")

    def move(value, rule):
        return lax.ppermute(value, both, route(rule, size_x, size_y))

    above = move(probes, lambda a, b: (a + 1, b))
    below = move(probes, lambda a, b: (a - 1, b))

    hbm = pl.BlockSpec(memory_space=pltpu.MemorySpace.HBM)
    block = (PROBES, 128)
    w0, w1, w2, w3, w4, w5, table, wide, up, down0, down1, down2, down3, own = call(
        prepare_kernel,
        [
            array((36 * RANK, 256)), array((36 * RANK, 128)), array((36 * RANK, 128)),
            array((24 * RANK, RANK)), array((12 * RANK, RANK)), array((3, 6 * RANK, RANK)),
            array((9 * 128, 128)), array((128, 256)), array(up_transfer.shape),
            array((128, 512)), array((128, 256)), array((RANK, 128)), array((4, RANK, RANK)),
            array(probes.shape),
        ],
        in_specs=[hbm] * 6,
        scratch=[
            pltpu.SMEM(far_ids.shape, jnp.int32), pltpu.VMEM(coupling.shape, BF),
            pltpu.VMEM(down_transfer.shape, BF), pltpu.VMEM(leaf_basis.shape[::-1], BF),
            pltpu.SemaphoreType.DMA, pltpu.SemaphoreType.DMA((8,)), pltpu.SemaphoreType.DMA((4,)),
        ],
    )(
        *[
            pltpu.with_memory_space_constraint(value, pltpu.MemorySpace.HBM)
            for value in (far_ids, coupling, up_transfer, down_transfer, leaf_basis.T, probes)
        ]
    )

    pack, low, mine, rim = call(
        first_kernel,
        [array((12,) + block), array((2,) + block), array((2, 4) + block), array((4, 4) + block)],
    )(own, above, below, wide, up)
    packed = move(pack, lambda a, b: (a, b ^ 1))
    sent = call(strip_kernel, array((16, 4) + block))(low, packed)
    gathered = lax.all_to_all(sent, "gx", 0, 0)

    far_out, level2, level3 = call(
        second_kernel,
        [array(block), array((8, 2) + block), array((4,) + block)],
    )(gathered, up)
    side_out = call(
        side_kernel,
        array((26,) + block),
        scratch=[pltpu.VMEM((20,) + block, BF), pltpu.VMEM((12,) + block, BF)],
        flops=1 << 32,
    )(gathered, own, mine, above, below, rim, level2, level3)

    chips = size_y // 2
    side = move(side_out, lambda a, b: (a, b + across(b % 2)))
    third = move(level3, lambda a, b: (a, b + 3 - 6 * (b % 2)))
    top = move(far_out, lambda a, b: (a, 2 * ((b // 2 + a) % chips) + b % 2))

    arrived = call(arrival_kernel, array(block), flops=1 << 36)(top)
    near_sum, far0, far1, far2, far3, copies = call(
        third_kernel,
        [
            array((2, 8) + block, F32), array((4 * PROBES, 256), F32),
            array((2 * PROBES, 128), F32), array((PROBES, 128), F32), array((PROBES, RANK), F32),
            array((16,) + block),
        ],
        scratch=[
            pltpu.VMEM(lead + block, BF)
            for lead in ((4, 10), (6, 6), (20, 4), (6, 4), (12, 2), (6, 3), (4, 3))
        ],
        flops=1,
        read=1,
    )(
        own, above, below, mine, packed, rim, gathered, level2, level3, side, third, arrived,
        w0, w1, w2, w3, table,
    )
    top = lax.all_to_all(copies, "gx", 0, 0)

    return call(
        fourth_kernel,
        array(probes.shape),
        scratch=[pltpu.VMEM((20,) + block, BF)]
        + [pltpu.VMEM((count + 4, PROBES, RANK), BF) for count in (8, 4, 2)],
    )(top, near_sum, far0, far1, far2, far3, w4, w5, wide, up, down0, down1, down2, down3)


def solution(mesh):
    in_specs = (P("gx", "gy", None, None), P(), P(), P(), P(), P())
    out_specs = P("gx", "gy", None, None)
    return jax.shard_map(shards, mesh=mesh, in_specs=in_specs, out_specs=out_specs, check_vma=False)
```

```python
import jax
import jax.numpy as jnp
from jax import lax
from jax.experimental import pallas as pl
from jax.experimental.pallas import tpu as pltpu
from jax.sharding import PartitionSpec as P

LEAF_ROWS = 8
LEAF_COLS = 16
RANK = 64
PROBES = 32
BF = jnp.bfloat16
F32 = jnp.float32

length_scale = 1.5


def dot(left, right):
    return jnp.dot(left, right, preferred_element_type=F32)


def lanes(parts):
    return jnp.concatenate(parts, axis=-1)


def block_slot(e, f, wr, wc):
    return 6 * wr + wc - 3 * min(max(wr - 1 - e, 0), 3) - (
        min(max(wc - 1 - f, 0), 3) if e + 1 <= wr <= e + 3 else 0
    )


def is_near(e, f, wr, wc):
    return e + 1 <= wr <= e + 3 and f + 1 <= wc <= f + 3


def places():
    row = lax.axis_index("gx")
    col = lax.axis_index("gy")
    return row, col, col // 2, col % 2


def build_weights(
    ids_far, coupling_far, down_far, w0, w1, w2, w3, w4, w5, table, down0, down1, down2, down3,
    ids, coupling, down, sems,
):
    row, col, _, _ = places()
    first = pltpu.make_async_copy(ids_far, ids, sems.at[8])
    first.start()
    levels = []
    for level in range(8):
        levels.append(
            pltpu.make_async_copy(coupling_far.at[level], coupling.at[level], sems.at[level])
        )
        levels[-1].start()
    other = pltpu.make_async_copy(down_far, down, sems.at[9])
    other.start()

    size = LEAF_ROWS * LEAF_COLS
    theirs = lax.broadcasted_iota(jnp.int32, (size, size), 0)
    ours = lax.broadcasted_iota(jnp.int32, (size, size), 1)
    rows_apart = (theirs // LEAF_COLS - ours // LEAF_COLS).astype(F32)
    cols_apart = (theirs % LEAF_COLS - ours % LEAF_COLS).astype(F32)
    for u in (-1, 0, 1):
        for v in (-1, 0, 1):
            apart_row = rows_apart + float(u * LEAF_ROWS)
            apart_col = cols_apart + float(v * LEAF_COLS)
            scaled = jnp.sqrt(3.0 * (apart_row * apart_row + apart_col * apart_col)) / length_scale
            value = (1.0 + scaled) * jnp.exp(-scaled)
            table[pl.ds((3 * (u + 1) + v + 1) * size, size), :] = value.astype(BF)

    def pair(level, e, wr, wc):
        halves = []
        for f in (0, 1):
            if is_near(e, f, wr, wc):
                halves.append(jnp.zeros((RANK, RANK), BF))
            else:
                halves.append(coupling[level, ids[level, 2 * e + f, block_slot(e, f, wr, wc)]])
        return lanes(halves)

    first.wait()
    levels[0].wait()
    for wr in range(6):
        for wc in range(6):
            at = pl.ds((6 * wr + wc) * RANK, RANK)
            for e in (0, 1):
                w0[at, pl.ds(128 * e, 128)] = pair(0, e, wr, wc)

    for level, out, bit in ((1, w1, row % 2), (2, w2, (row // 2) % 2)):
        levels[level].wait()
        for e in (0, 1):

            @pl.when(bit == e)
            def _(level=level, out=out, e=e):
                for wr in range(6):
                    for wc in range(6):
                        out[pl.ds((6 * wr + wc) * RANK, RANK), :] = pair(level, e, wr, wc)

    def single(level, e, f, wr, wc):
        row_in = jnp.logical_and(wr >= e + 1, wr <= e + 3)
        col_in = jnp.logical_and(wc >= f + 1, wc <= f + 3)
        skipped = 3 * jnp.clip(wr - 1 - e, 0, 3) + jnp.where(row_in, jnp.clip(wc - 1 - f, 0, 3), 0)
        slot = jnp.clip(6 * wr + wc - skipped, 0, 26)
        keep = jnp.where(jnp.logical_and(row_in, col_in), 0.0, 1.0)
        block = coupling[level, ids[level, 2 * e + f, slot]]
        return block * jnp.full((RANK, RANK), keep, F32).astype(BF)

    levels[3].wait()
    e3, f3 = (row // 4) % 2, col % 2
    first3 = 2 - 2 * (row // 8)
    for r in range(4):
        for wc in range(6):
            w3[pl.ds((6 * r + wc) * RANK, RANK), :] = single(3, e3, f3, r + first3, wc)
    levels[4].wait()
    e4, f4 = row // 8, (col // 2) % 2
    for wc in range(6):
        for r in range(2):
            w4[pl.ds((2 * wc + r) * RANK, RANK), :] = single(4, e4, f4, jnp.int32(2 + r), wc)
    for level in (5, 6, 7):
        levels[level].wait()
        f = (col // (1 << (level - 3))) % 2
        for wc in range(6):
            w5[level - 5, pl.ds(wc * RANK, RANK), :] = single(
                level, jnp.int32(0), f, jnp.int32(2), wc
            )

    other.wait()
    all0 = lanes([down[0, k] for k in range(4)])
    none0 = jnp.zeros_like(all0)
    down0[...] = jnp.concatenate([lanes([all0, none0]), lanes([none0, all0])], axis=0)
    e1, e2 = row % 2, (row // 2) % 2
    both1 = lanes([down[1, 2 * e1], down[1, 2 * e1 + 1]])
    none1 = jnp.zeros_like(both1)
    down1[...] = jnp.concatenate([lanes([both1, none1]), lanes([none1, both1])], axis=0)
    down2[...] = lanes([down[2, 2 * e2], down[2, 2 * e2 + 1]])
    for level in (3, 4, 5, 6):
        e = (row // (1 << (level - 1))) % 2
        f = (col // (1 << (level - 3))) % 2
        down3[level - 3] = down[level, 2 * e + f]


EARLY_PLANES = 7


def start_kernel(
    ids_far, coupling_far, down_far, up_far, basis_far, own_far,
    wide, up, own, mine, low,
    w0, w1, w2, w3, w4, w5, table, down0, down1, down2, down3,
    ids, coupling, down, basis, sems, small_sems,
):
    _, _, chip, _ = places()
    small = [
        pltpu.make_async_copy(source, target, small_sems.at[at])
        for at, (source, target) in enumerate(((basis_far, basis), (own_far, own), (up_far, up)))
    ]
    for copy in small:
        copy.start()
    for copy in small:
        copy.wait()
    blank = jnp.zeros_like(basis)
    wide[...] = jnp.concatenate([lanes([basis[...], blank]), lanes([blank, basis[...]])], axis=0)
    coeffs = leaf_coeffs(own[...], wide[...])
    mine[...] = coeffs
    low[...] = to_pairs(raise_pairs(coeffs, up[0].reshape(4 * RANK, RANK))[0])

    @pl.when(chip < EARLY_PLANES)
    def _():
        build_weights(
            ids_far, coupling_far, down_far,
            w0, w1, w2, w3, w4, w5, table, down0, down1, down2, down3,
            ids, coupling, down, sems,
        )


def later_kernel(ids_far, coupling_far, down_far, tag, *refs):
    _, _, chip, _ = places()
    weights, scratch = refs[11:22], refs[22:]

    @pl.when(chip >= EARLY_PLANES)
    def _():
        build_weights(ids_far, coupling_far, down_far, *weights, *scratch)


def array(shape, kind=BF):
    return jax.ShapeDtypeStruct(shape, kind)


def call(kernel, out_shape, scratch=(), flops=1 << 24, read=1 << 21, **specs):
    return pl.pallas_call(
        kernel,
        out_shape=out_shape,
        **specs,
        scratch_shapes=list(scratch),
        compiler_params=pltpu.CompilerParams(vmem_limit_bytes=16 << 20),
        cost_estimate=pl.CostEstimate(flops=flops, bytes_accessed=read, transcendentals=0),
    )


def leaf_coeffs(tile, wide_basis):
    rows = tile.shape[0]
    split = tile.reshape(rows, 4, 2, PROBES, 128)
    joined = lanes([split[:, :, 0], split[:, :, 1]]).reshape(-1, 256)
    coeffs = lax.dot_general(
        joined, wide_basis, (((1,), (1,)), ((), ())), preferred_element_type=F32
    )
    return coeffs.astype(BF).reshape(rows, 4, PROBES, 128)


def to_pairs(nodes):
    lead = nodes.shape[:-3]
    split = nodes.reshape(lead + (nodes.shape[-3] // 2, 2, PROBES, RANK))
    return lanes([split[..., 0, :, :], split[..., 1, :, :]])


def raise_pairs(pairs, transfer):
    rows, count = pairs.shape[:2]
    split = pairs.reshape(rows // 2, 2, count, PROBES, 128)
    joined = lanes([split[:, 0], split[:, 1]]).reshape(-1, 256)
    return dot(joined, transfer).astype(BF).reshape(rows // 2, count, PROBES, RANK)


def rim_kernel(above, below, wide, low, rim, sent):
    rim[pl.ds(0, 2)] = leaf_coeffs(above[...], wide[...])
    rim[pl.ds(2, 2)] = leaf_coeffs(below[...], wide[...])
    for peer in range(16):
        sent[peer] = low[...]


def strip_kernel(gathered, own, mine, above, below, rim, up, pack, level2, level3, padded1, padded2):
    row, _, _, core = places()
    pairs2 = to_pairs(raise_pairs(gathered[...], up[1].reshape(4 * RANK, RANK)))
    nodes3 = raise_pairs(pairs2, up[2].reshape(4 * RANK, RANK))[:, 0]
    level2[...] = pairs2[:, 0]
    level3[...] = nodes3
    nothing = jnp.zeros((2, PROBES, 128), BF)
    padded1[pl.ds(0, 2)] = nothing
    padded1[pl.ds(18, 2)] = nothing
    padded2[pl.ds(0, 2)] = nothing
    padded2[pl.ds(2, 8)] = pairs2[:, 0]
    padded2[pl.ds(10, 2)] = nothing
    for r in range(16):
        padded1[r + 2] = gathered[r, 1 - core]
    edge_pair = 3 - 3 * core
    edge_col = 7 - 7 * core
    pack[pl.ds(0, 6)] = padded1[pl.ds(2 * (row // 2), 6)]
    pack[pl.ds(6, 6)] = padded2[pl.ds(2 * (row // 4), 6)]
    pack[12] = lanes([nodes3[0], nodes3[1]])
    pack[13] = lanes([nodes3[2], nodes3[3]])
    pack[14] = mine[0, edge_pair]
    pack[15] = mine[1, edge_pair]
    pack[16] = own[0, edge_col]
    pack[17] = own[1, edge_col]
    pack[18] = above[1, edge_col]
    pack[19] = below[0, edge_col]
    for r in range(4):
        pack[20 + r] = rim[r, edge_pair]


def second_kernel(
    packed, gathered, level2, level3_own, own, mine, above, below, rim, up,
    far_out, side_out, level3, padded1, padded2,
):
    row, _, _, core = places()
    theirs = []
    for at in (12, 13):
        block = packed[at]
        theirs += [block[:, :RANK], block[:, RANK:]]

    @pl.when(core == 0)
    def _():
        for r in range(4):
            level3[r] = lanes([level3_own[r], theirs[r]])

    @pl.when(core == 1)
    def _():
        for r in range(4):
            level3[r] = lanes([theirs[r], level3_own[r]])

    pairs3 = level3[...]
    nodes4 = raise_pairs(pairs3[:, None], up[3].reshape(4 * RANK, RANK))
    far_out[...] = lanes([nodes4[0, 0], nodes4[1, 0]])

    edge_pair = 3 * core
    edge_col = 7 * core
    nothing = jnp.zeros((2, PROBES, 128), BF)
    padded1[pl.ds(0, 2)] = nothing
    padded1[pl.ds(18, 2)] = nothing
    padded2[pl.ds(0, 2)] = nothing
    padded2[pl.ds(2, 8)] = level2[...]
    padded2[pl.ds(10, 2)] = nothing
    for r in range(16):
        padded1[r + 2] = gathered[r, core]
    side_out[0] = above[1, edge_col]
    side_out[1] = own[0, edge_col]
    side_out[2] = own[1, edge_col]
    side_out[3] = below[0, edge_col]
    side_out[4] = rim[0, edge_pair]
    side_out[5] = rim[1, edge_pair]
    side_out[6] = mine[0, edge_pair]
    side_out[7] = mine[1, edge_pair]
    side_out[8] = rim[2, edge_pair]
    side_out[9] = rim[3, edge_pair]
    side_out[pl.ds(10, 6)] = padded1[pl.ds(2 * (row // 2), 6)]
    side_out[pl.ds(16, 6)] = padded2[pl.ds(2 * (row // 4), 6)]
    side_out[pl.ds(22, 4)] = pairs3


def third_kernel(
    own, above, below, mine, packed, rim, gathered, level2, level3,
    side, third, w0, w1, w2, w3, table,
    near_sum, far0, far1, far2, far3, tag,
    near, window0, padded1, window1, padded2, window2, window3,
):
    row, _, _, core = places()

    window0[pl.ds(0, 2), pl.ds(1, 4)] = rim[pl.ds(0, 2)]
    window0[pl.ds(2, 2), pl.ds(1, 4)] = mine[...]
    window0[pl.ds(4, 2), pl.ds(1, 4)] = rim[pl.ds(2, 2)]
    for w in range(6):
        window0[w, 5 * core] = side[4 + w]
    for r in range(2):
        window0[r, 5 - 5 * core] = packed[20 + r]
        window0[2 + r, 5 - 5 * core] = packed[14 + r]
        window0[4 + r, 5 - 5 * core] = packed[22 + r]
    far0[...] = dot(
        lanes([window0[w, pl.ds(k, 4)].reshape(-1, 128) for w in range(6) for k in range(3)]),
        w0[...],
    )

    near[0, pl.ds(1, 8)] = above[1]
    near[1, pl.ds(1, 8)] = own[0]
    near[2, pl.ds(1, 8)] = own[1]
    near[3, pl.ds(1, 8)] = below[0]
    for r in range(4):
        near[r, 9 * core] = side[r]
    near[0, 9 - 9 * core] = packed[18]
    near[1, 9 - 9 * core] = packed[16]
    near[2, 9 - 9 * core] = packed[17]
    near[3, 9 - 9 * core] = packed[19]
    for e in (0, 1):
        joined = lanes([near[e + u, pl.ds(v, 8)].reshape(-1, 128) for u in range(3) for v in range(3)])
        near_sum[e] = dot(joined, table[...]).reshape(8, PROBES, 128)

    empty1 = jnp.zeros((2, 2, PROBES, 128), BF)
    padded1[pl.ds(0, 2)] = empty1
    padded1[pl.ds(2, 16)] = gathered[...]
    padded1[pl.ds(18, 2)] = empty1
    window1[:, pl.ds(1, 2)] = padded1[pl.ds(2 * (row // 2), 6)]
    for w in range(6):
        window1[w, 3 - 3 * core] = packed[w]
        window1[w, 3 * core] = side[10 + w]
    far1[...] = dot(
        lanes([window1[w, pl.ds(k, 2)].reshape(-1, 128) for w in range(6) for k in range(3)]),
        w1[...],
    )

    empty2 = jnp.zeros((2, PROBES, 128), BF)
    padded2[pl.ds(0, 2)] = empty2
    padded2[pl.ds(2, 8)] = level2[...]
    padded2[pl.ds(10, 2)] = empty2
    window2[:, 1] = padded2[pl.ds(2 * (row // 4), 6)]
    for w in range(6):
        window2[w, 2 - 2 * core] = packed[6 + w]
        window2[w, 2 * core] = side[16 + w]
    far2[...] = dot(lanes([window2[w, k] for w in range(6) for k in range(3)]), w2[...])

    for r in range(4):
        window3[r, 2 * core] = side[22 + r]
        window3[r, 1] = level3[r]
        window3[r, 2 - 2 * core] = third[r]
    far3[...] = dot(lanes([window3[r, k] for r in range(4) for k in range(3)]), w3[...])
    tag[...] = jnp.zeros_like(tag)


def copies_kernel(block, tag, out):
    for peer in range(16):
        out[peer] = block[...]


def fourth_kernel(
    top, near_sum, far0, far1, far2, far3, w4, w5, wide, up, down0, down1, down2, down3,
    out,
    padded4, padded5, padded6, padded7,
):
    _, col, chip, _ = places()

    blank = jnp.zeros((2, PROBES, 128), BF)
    padded4[pl.ds(0, 2)] = blank
    padded4[pl.ds(18, 2)] = blank
    for c in range(16):
        padded4[c + 2] = top[(chip - c + 16) % 16]
    by_col = jnp.concatenate([up[4, 0], up[4, 2], up[4, 1], up[4, 3]], axis=0)
    all4 = padded4[pl.ds(2, 16)].reshape(8, 2, PROBES, 128)
    nodes5 = dot(lanes([all4[:, 0], all4[:, 1]]).reshape(-1, 256), by_col)
    nodes5 = nodes5.astype(BF).reshape(8, PROBES, RANK)

    def raise_row(nodes, level):
        pairs = to_pairs(nodes).reshape(-1, 128)
        both = jnp.concatenate([up[level, 0], up[level, 1]], axis=0)
        return dot(pairs, both).astype(BF).reshape(-1, PROBES, RANK)

    nodes6 = raise_row(nodes5, 5)
    nodes7 = raise_row(nodes6, 6)
    gap = jnp.zeros((2, PROBES, RANK), BF)
    for padded, nodes in ((padded5, nodes5), (padded6, nodes6), (padded7, nodes7)):
        count = nodes.shape[0]
        padded[pl.ds(0, 2)] = gap
        padded[pl.ds(2, count)] = nodes
        padded[pl.ds(2 + count, 2)] = gap

    def far_row(padded, level):
        start = 2 * (col // (1 << (level - 2)))
        return dot(lanes([padded[start + k] for k in range(6)]), w5[level - 5])

    start4 = 2 * (chip // 2)
    far4 = dot(lanes([padded4[start4 + k] for k in range(6)]), w4[...])
    local = far_row(padded7, 7).astype(BF)
    local = (far_row(padded6, 6) + dot(local, down3[3])).astype(BF)
    local = (far_row(padded5, 5) + dot(local, down3[2])).astype(BF)
    local = (far4 + dot(local, down3[1])).astype(BF)
    local = (far3[...] + dot(local, down3[0])).astype(BF)
    local2 = (far2[...] + dot(local, down2[...])).astype(BF)
    spread1 = dot(local2, down1[...])
    spread1 = jnp.concatenate([spread1[:, :128], spread1[:, 128:]], axis=0)
    local1 = (far1[...] + spread1).astype(BF)
    spread0 = dot(local1, down0[...]).reshape(2, PROBES, 512)
    spread0 = jnp.stack([spread0[:, :, :256], spread0[:, :, 256:]], axis=1).reshape(-1, 256)
    local0 = (far0[...] + spread0).astype(BF)
    for e in (0, 1):
        far_sum = dot(local0[:, 128 * e : 128 * e + 128], wide[...]).reshape(4, PROBES, 256)
        for q in range(4):
            for f in (0, 1):
                part = far_sum[q, :, 128 * f : 128 * f + 128]
                out[e, 2 * q + f] = (near_sum[e, 2 * q + f] + part).astype(BF)


def route(rule, size_x, size_y):
    pairs = []
    for a in range(size_x):
        for b in range(size_y):
            x, y = rule(a, b)
            if 0 <= x < size_x and 0 <= y < size_y:
                pairs.append((a * size_y + b, x * size_y + y))
    return pairs


def across(core):
    return 1 if core else -1


def shards(probes, leaf_basis, up_transfer, down_transfer, coupling, far_ids):
    size_x, size_y = lax.axis_size("gx"), lax.axis_size("gy")
    both = ("gx", "gy")

    def move(value, rule):
        return lax.ppermute(value, both, route(rule, size_x, size_y))

    above = move(probes, lambda a, b: (a + 1, b))
    below = move(probes, lambda a, b: (a - 1, b))

    hbm = pl.BlockSpec(memory_space=pltpu.MemorySpace.HBM)
    whole = pl.BlockSpec(memory_space=pltpu.VMEM)
    block = (PROBES, 128)
    far_inputs = [
        pltpu.with_memory_space_constraint(value, pltpu.MemorySpace.HBM)
        for value in (far_ids, coupling, down_transfer, up_transfer, leaf_basis.T, probes)
    ]
    weight_shapes = [
        array((36 * RANK, 256)), array((36 * RANK, 128)), array((36 * RANK, 128)),
        array((24 * RANK, RANK)), array((12 * RANK, RANK)), array((3, 6 * RANK, RANK)),
        array((9 * 128, 128)), array((128, 512)), array((128, 256)), array((RANK, 128)),
        array((4, RANK, RANK)),
    ]
    build_scratch = [
        pltpu.SMEM(far_ids.shape, jnp.int32), pltpu.VMEM(coupling.shape, BF),
        pltpu.VMEM(down_transfer.shape, BF),
    ]
    wide, up, own, mine, low, *weights = call(
        start_kernel,
        [
            array((128, 256)), array(up_transfer.shape), array(probes.shape),
            array((2, 4) + block), array((2,) + block),
        ]
        + weight_shapes,
        in_specs=[hbm] * 6,
        scratch=build_scratch
        + [
            pltpu.VMEM(leaf_basis.shape[::-1], BF), pltpu.SemaphoreType.DMA((10,)),
            pltpu.SemaphoreType.DMA((3,)),
        ],
    )(*far_inputs)

    rim, sent = call(rim_kernel, [array((4, 4) + block), array((16, 2) + block)])(
        above, below, wide, low
    )
    gathered = lax.all_to_all(sent, "gx", 0, 0)

    pack, level2, level3_own = call(
        strip_kernel,
        [array((24,) + block), array((8,) + block), array((4, PROBES, RANK))],
        scratch=[pltpu.VMEM((20,) + block, BF), pltpu.VMEM((12,) + block, BF)],
    )(gathered, own, mine, above, below, rim, up)
    packed = move(pack, lambda a, b: (a, b ^ 1))
    far_out, side_out, level3 = call(
        second_kernel,
        [array(block), array((26,) + block), array((4,) + block)],
        scratch=[pltpu.VMEM((20,) + block, BF), pltpu.VMEM((12,) + block, BF)],
    )(packed, gathered, level2, level3_own, own, mine, above, below, rim, up)

    chips = size_y // 2
    side = move(side_out, lambda a, b: (a, b + across(b % 2)))
    third = move(level3, lambda a, b: (a, b + 3 - 6 * (b % 2)))
    top = move(far_out, lambda a, b: (a, 2 * ((b // 2 + a) % chips) + b % 2))

    weights = call(
        later_kernel,
        weight_shapes,
        in_specs=[hbm] * 3 + [whole] * 12,
        input_output_aliases={4 + at: at for at in range(11)},
        scratch=build_scratch + [pltpu.SemaphoreType.DMA((10,))],
    )(*far_inputs[:3], third, *weights)
    w0, w1, w2, w3, w4, w5, table, down0, down1, down2, down3 = weights

    near_sum, far0, far1, far2, far3, tag = call(
        third_kernel,
        [
            array((2, 8) + block, F32), array((4 * PROBES, 256), F32),
            array((2 * PROBES, 128), F32), array((PROBES, 128), F32), array((PROBES, RANK), F32),
            array((8, 128), F32),
        ],
        scratch=[
            pltpu.VMEM(lead + block, BF)
            for lead in ((4, 10), (6, 6), (20, 2), (6, 4), (12,), (6, 3), (4, 3))
        ],
        flops=1,
        read=1,
    )(
        own, above, below, mine, packed, rim, gathered, level2, level3, side, third,
        w0, w1, w2, w3, table,
    )
    copies = call(copies_kernel, array((16,) + block))(top, tag)
    top = lax.all_to_all(copies, "gx", 0, 0)

    return call(
        fourth_kernel,
        array(probes.shape),
        scratch=[pltpu.VMEM((20,) + block, BF)]
        + [pltpu.VMEM((count + 4, PROBES, RANK), BF) for count in (8, 4, 2)],
    )(top, near_sum, far0, far1, far2, far3, w4, w5, wide, up, down0, down1, down2, down3)


def solution(mesh):
    in_specs = (P("gx", "gy", None, None), P(), P(), P(), P(), P())
    out_specs = P("gx", "gy", None, None)
    return jax.shard_map(shards, mesh=mesh, in_specs=in_specs, out_specs=out_specs, check_vma=False)
```

```python
import jax
import jax.numpy as jnp
from jax import lax
from jax.experimental import pallas as pl
from jax.experimental.pallas import tpu as pltpu
from jax.sharding import PartitionSpec as P

LEAF_ROWS = 8
LEAF_COLS = 16
RANK = 64
PROBES = 32
BF = jnp.bfloat16
F32 = jnp.float32

length_scale = 1.5


def dot(left, right):
    return jnp.dot(left, right, preferred_element_type=F32)


def lanes(parts):
    return jnp.concatenate(parts, axis=-1)


def block_slot(e, f, wr, wc):
    return 6 * wr + wc - 3 * min(max(wr - 1 - e, 0), 3) - (
        min(max(wc - 1 - f, 0), 3) if e + 1 <= wr <= e + 3 else 0
    )


def is_near(e, f, wr, wc):
    return e + 1 <= wr <= e + 3 and f + 1 <= wc <= f + 3


def places():
    row = lax.axis_index("gx")
    col = lax.axis_index("gy")
    return row, col, col // 2, col % 2


def build_weights(
    ids_far, coupling_far, down_far, wide, up,
    w0, w1, w2, w3, table, down0, down1, down2, up5, up6, up7, top_far, top_leaf,
    ids, coupling, down, sems,
):
    row, col, _, _ = places()
    first = pltpu.make_async_copy(ids_far, ids, sems.at[8])
    first.start()
    levels = []
    for level in range(8):
        levels.append(
            pltpu.make_async_copy(coupling_far.at[level], coupling.at[level], sems.at[level])
        )
        levels[-1].start()
    other = pltpu.make_async_copy(down_far, down, sems.at[9])
    other.start()

    size = LEAF_ROWS * LEAF_COLS
    theirs = lax.broadcasted_iota(jnp.int32, (size, size), 0)
    ours = lax.broadcasted_iota(jnp.int32, (size, size), 1)
    rows_apart = (theirs // LEAF_COLS - ours // LEAF_COLS).astype(F32)
    cols_apart = (theirs % LEAF_COLS - ours % LEAF_COLS).astype(F32)
    for u in (-1, 0, 1):
        for v in (-1, 0, 1):
            apart_row = rows_apart + float(u * LEAF_ROWS)
            apart_col = cols_apart + float(v * LEAF_COLS)
            scaled = jnp.sqrt(3.0 * (apart_row * apart_row + apart_col * apart_col)) / length_scale
            value = (1.0 + scaled) * jnp.exp(-scaled)
            table[pl.ds((3 * (u + 1) + v + 1) * size, size), :] = value.astype(BF)

    def pair(level, e, wr, wc):
        halves = []
        for f in (0, 1):
            if is_near(e, f, wr, wc):
                halves.append(jnp.zeros((RANK, RANK), BF))
            else:
                halves.append(coupling[level, ids[level, 2 * e + f, block_slot(e, f, wr, wc)]])
        return lanes(halves)

    first.wait()
    levels[0].wait()
    for wr in range(6):
        for wc in range(6):
            at = pl.ds((6 * wr + wc) * RANK, RANK)
            for e in (0, 1):
                w0[at, pl.ds(128 * e, 128)] = pair(0, e, wr, wc)

    for level, out, bit in ((1, w1, row % 2), (2, w2, (row // 2) % 2)):
        levels[level].wait()
        for e in (0, 1):

            @pl.when(bit == e)
            def _(level=level, out=out, e=e):
                for wr in range(6):
                    for wc in range(6):
                        out[pl.ds((6 * wr + wc) * RANK, RANK), :] = pair(level, e, wr, wc)

    def single(level, e, f, wr, wc):
        row_in = jnp.logical_and(wr >= e + 1, wr <= e + 3)
        col_in = jnp.logical_and(wc >= f + 1, wc <= f + 3)
        skipped = 3 * jnp.clip(wr - 1 - e, 0, 3) + jnp.where(row_in, jnp.clip(wc - 1 - f, 0, 3), 0)
        slot = jnp.clip(6 * wr + wc - skipped, 0, 26)
        keep = jnp.where(jnp.logical_and(row_in, col_in), 0.0, 1.0)
        block = coupling[level, ids[level, 2 * e + f, slot]]
        return block * jnp.full((RANK, RANK), keep, F32).astype(BF)

    levels[3].wait()
    e3, f3 = (row // 4) % 2, col % 2
    first3 = 2 - 2 * (row // 8)
    for r in range(4):
        for wc in range(6):
            w3[pl.ds((6 * r + wc) * RANK, RANK), :] = single(3, e3, f3, r + first3, wc)

    other.wait()
    chain = None
    first_row = 0
    for level in (4, 5, 6, 7):
        levels[level].wait()
        e = (row // (1 << (level - 1))) % 2
        f = (col // (1 << (level - 3))) % 2
        e_up = (row // (1 << (level - 2))) % 2
        f_up = (col // (1 << (level - 4))) % 2
        step = down[level - 1, 2 * e_up + f_up]
        chain = step if chain is None else dot(step, chain).astype(BF)
        rows = 2 if level == 4 else 1
        blocks = [
            single(level, e, f, jnp.int32(2 + r), wc) for wc in range(6) for r in range(rows)
        ]
        stacked = dot(jnp.concatenate(blocks, axis=0), chain).astype(BF)
        top_far[pl.ds(first_row, stacked.shape[0]), :] = stacked
        first_row += stacked.shape[0]
    from4 = jnp.concatenate([up[4, 0], up[4, 2], up[4, 1], up[4, 3]], axis=0)
    from5 = jnp.concatenate([dot(from4, up[5, f]).astype(BF) for f in (0, 1)], axis=0)
    up5[...] = from4
    up6[...] = from5
    up7[...] = jnp.concatenate([dot(from5, up[6, f]).astype(BF) for f in (0, 1)], axis=0)

    all0 = lanes([down[0, k] for k in range(4)])
    none0 = jnp.zeros_like(all0)
    down0[...] = jnp.concatenate([lanes([all0, none0]), lanes([none0, all0])], axis=0)
    e1, e2 = row % 2, (row // 2) % 2
    both1 = lanes([down[1, 2 * e1], down[1, 2 * e1 + 1]])
    none1 = jnp.zeros_like(both1)
    down1[...] = jnp.concatenate([lanes([both1, none1]), lanes([none1, both1])], axis=0)
    down2[...] = lanes([down[2, 2 * e2], down[2, 2 * e2 + 1]])

    node1 = dot(down2[...], down1[...]).astype(BF)
    for t in (0, 1):
        node0 = dot(node1[:, 128 * t : 128 * t + 128], down0[...]).astype(BF)
        for q in (0, 1):
            for e in (0, 1):
                at = 256 * q + 128 * e
                leaves = dot(node0[:, at : at + 128], wide[...]).astype(BF)
                top_leaf[:, pl.ds(256 * (4 * e + 2 * t + q), 256)] = leaves


EARLY_PLANES = 7


def start_kernel(
    ids_far, coupling_far, down_far, up_far, basis_far, own_far,
    wide, up, own, mine, low,
    w0, w1, w2, w3, table, down0, down1, down2, up5, up6, up7, top_far, top_leaf,
    ids, coupling, down, basis, sems, small_sems,
):
    _, _, chip, _ = places()
    small = [
        pltpu.make_async_copy(source, target, small_sems.at[at])
        for at, (source, target) in enumerate(((basis_far, basis), (own_far, own), (up_far, up)))
    ]
    for copy in small:
        copy.start()
    for copy in small:
        copy.wait()
    blank = jnp.zeros_like(basis)
    wide[...] = jnp.concatenate([lanes([basis[...], blank]), lanes([blank, basis[...]])], axis=0)
    coeffs = leaf_coeffs(own[...], wide[...])
    mine[...] = coeffs
    low[...] = to_pairs(raise_pairs(coeffs, up[0].reshape(4 * RANK, RANK))[0])

    @pl.when(chip < EARLY_PLANES)
    def _():
        build_weights(
            ids_far, coupling_far, down_far, wide, up,
            w0, w1, w2, w3, table, down0, down1, down2, up5, up6, up7, top_far, top_leaf,
            ids, coupling, down, sems,
        )


def later_kernel(ids_far, coupling_far, down_far, wide, up, tag, *refs):
    _, _, chip, _ = places()
    weights, scratch = refs[13:26], refs[26:]

    @pl.when(chip >= EARLY_PLANES)
    def _():
        build_weights(ids_far, coupling_far, down_far, wide, up, *weights, *scratch)


def array(shape, kind=BF):
    return jax.ShapeDtypeStruct(shape, kind)


def call(kernel, out_shape, scratch=(), flops=1 << 24, read=1 << 21, **specs):
    return pl.pallas_call(
        kernel,
        out_shape=out_shape,
        **specs,
        scratch_shapes=list(scratch),
        compiler_params=pltpu.CompilerParams(vmem_limit_bytes=16 << 20),
        cost_estimate=pl.CostEstimate(flops=flops, bytes_accessed=read, transcendentals=0),
    )


def leaf_coeffs(tile, wide_basis):
    rows = tile.shape[0]
    split = tile.reshape(rows, 4, 2, PROBES, 128)
    joined = lanes([split[:, :, 0], split[:, :, 1]]).reshape(-1, 256)
    coeffs = lax.dot_general(
        joined, wide_basis, (((1,), (1,)), ((), ())), preferred_element_type=F32
    )
    return coeffs.astype(BF).reshape(rows, 4, PROBES, 128)


def to_pairs(nodes):
    lead = nodes.shape[:-3]
    split = nodes.reshape(lead + (nodes.shape[-3] // 2, 2, PROBES, RANK))
    return lanes([split[..., 0, :, :], split[..., 1, :, :]])


def raise_pairs(pairs, transfer):
    rows, count = pairs.shape[:2]
    split = pairs.reshape(rows // 2, 2, count, PROBES, 128)
    joined = lanes([split[:, 0], split[:, 1]]).reshape(-1, 256)
    return dot(joined, transfer).astype(BF).reshape(rows // 2, count, PROBES, RANK)


def rim_kernel(above, below, wide, low, rim, sent):
    rim[pl.ds(0, 2)] = leaf_coeffs(above[...], wide[...])
    rim[pl.ds(2, 2)] = leaf_coeffs(below[...], wide[...])
    for peer in range(16):
        sent[peer] = low[...]


def strip_kernel(gathered, own, mine, above, below, rim, up, pack, level2, level3, padded1, padded2):
    row, _, _, core = places()
    pairs2 = to_pairs(raise_pairs(gathered[...], up[1].reshape(4 * RANK, RANK)))
    level2[...] = pairs2[:, 0]
    level3[...] = raise_pairs(pairs2, up[2].reshape(4 * RANK, RANK))[:, 0]
    nothing = jnp.zeros((2, PROBES, 128), BF)
    padded1[pl.ds(0, 2)] = nothing
    padded1[pl.ds(18, 2)] = nothing
    padded2[pl.ds(0, 2)] = nothing
    padded2[pl.ds(2, 8)] = level2[...]
    padded2[pl.ds(10, 2)] = nothing
    for r in range(16):
        padded1[r + 2] = gathered[r, 1 - core]
    edge_pair = 3 - 3 * core
    edge_col = 7 - 7 * core
    pack[pl.ds(0, 6)] = padded1[pl.ds(2 * (row // 2), 6)]
    pack[pl.ds(6, 6)] = padded2[pl.ds(2 * (row // 4), 6)]
    pack[12] = lanes([level3[0], level3[1]])
    pack[13] = lanes([level3[2], level3[3]])
    pack[14] = mine[0, edge_pair]
    pack[15] = mine[1, edge_pair]
    pack[16] = own[0, edge_col]
    pack[17] = own[1, edge_col]
    pack[18] = above[1, edge_col]
    pack[19] = below[0, edge_col]
    for r in range(4):
        pack[20 + r] = rim[r, edge_pair]


def second_kernel(
    packed, gathered, level2, level3_own, own, mine, above, below, rim, up,
    far_out, side_out, level3, padded1, padded2,
):
    row, _, _, core = places()
    theirs = []
    for at in (12, 13):
        block = packed[at]
        theirs += [block[:, :RANK], block[:, RANK:]]

    @pl.when(core == 0)
    def _():
        for r in range(4):
            level3[r] = lanes([level3_own[r], theirs[r]])

    @pl.when(core == 1)
    def _():
        for r in range(4):
            level3[r] = lanes([theirs[r], level3_own[r]])

    pairs3 = level3[...]
    nodes4 = raise_pairs(pairs3[:, None], up[3].reshape(4 * RANK, RANK))
    far_out[...] = lanes([nodes4[0, 0], nodes4[1, 0]])

    edge_pair = 3 * core
    edge_col = 7 * core
    nothing = jnp.zeros((2, PROBES, 128), BF)
    padded1[pl.ds(0, 2)] = nothing
    padded1[pl.ds(18, 2)] = nothing
    padded2[pl.ds(0, 2)] = nothing
    padded2[pl.ds(2, 8)] = level2[...]
    padded2[pl.ds(10, 2)] = nothing
    for r in range(16):
        padded1[r + 2] = gathered[r, core]
    side_out[0] = above[1, edge_col]
    side_out[1] = own[0, edge_col]
    side_out[2] = own[1, edge_col]
    side_out[3] = below[0, edge_col]
    side_out[4] = rim[0, edge_pair]
    side_out[5] = rim[1, edge_pair]
    side_out[6] = mine[0, edge_pair]
    side_out[7] = mine[1, edge_pair]
    side_out[8] = rim[2, edge_pair]
    side_out[9] = rim[3, edge_pair]
    side_out[pl.ds(10, 6)] = padded1[pl.ds(2 * (row // 2), 6)]
    side_out[pl.ds(16, 6)] = padded2[pl.ds(2 * (row // 4), 6)]
    side_out[pl.ds(22, 4)] = pairs3


def third_kernel(
    own, above, below, mine, packed, rim, gathered, level2, side, w0, w1, w2, table,
    near_sum, far0, far1, far2,
    near, window0, padded1, window1, padded2, window2,
):
    row, _, _, core = places()

    window0[pl.ds(0, 2), pl.ds(1, 4)] = rim[pl.ds(0, 2)]
    window0[pl.ds(2, 2), pl.ds(1, 4)] = mine[...]
    window0[pl.ds(4, 2), pl.ds(1, 4)] = rim[pl.ds(2, 2)]
    for w in range(6):
        window0[w, 5 * core] = side[4 + w]
    for r in range(2):
        window0[r, 5 - 5 * core] = packed[20 + r]
        window0[2 + r, 5 - 5 * core] = packed[14 + r]
        window0[4 + r, 5 - 5 * core] = packed[22 + r]
    far0[...] = dot(
        lanes([window0[w, pl.ds(k, 4)].reshape(-1, 128) for w in range(6) for k in range(3)]),
        w0[...],
    )

    near[0, pl.ds(1, 8)] = above[1]
    near[1, pl.ds(1, 8)] = own[0]
    near[2, pl.ds(1, 8)] = own[1]
    near[3, pl.ds(1, 8)] = below[0]
    for r in range(4):
        near[r, 9 * core] = side[r]
    near[0, 9 - 9 * core] = packed[18]
    near[1, 9 - 9 * core] = packed[16]
    near[2, 9 - 9 * core] = packed[17]
    near[3, 9 - 9 * core] = packed[19]
    for e in (0, 1):
        joined = lanes([near[e + u, pl.ds(v, 8)].reshape(-1, 128) for u in range(3) for v in range(3)])
        near_sum[e] = dot(joined, table[...]).reshape(8, PROBES, 128)

    empty1 = jnp.zeros((2, 2, PROBES, 128), BF)
    padded1[pl.ds(0, 2)] = empty1
    padded1[pl.ds(2, 16)] = gathered[...]
    padded1[pl.ds(18, 2)] = empty1
    window1[:, pl.ds(1, 2)] = padded1[pl.ds(2 * (row // 2), 6)]
    for w in range(6):
        window1[w, 3 - 3 * core] = packed[w]
        window1[w, 3 * core] = side[10 + w]
    far1[...] = dot(
        lanes([window1[w, pl.ds(k, 2)].reshape(-1, 128) for w in range(6) for k in range(3)]),
        w1[...],
    )

    empty2 = jnp.zeros((2, PROBES, 128), BF)
    padded2[pl.ds(0, 2)] = empty2
    padded2[pl.ds(2, 8)] = level2[...]
    padded2[pl.ds(10, 2)] = empty2
    window2[:, 1] = padded2[pl.ds(2 * (row // 4), 6)]
    for w in range(6):
        window2[w, 2 - 2 * core] = packed[6 + w]
        window2[w, 2 * core] = side[16 + w]
    far2[...] = dot(lanes([window2[w, k] for w in range(6) for k in range(3)]), w2[...])


def lower_kernel(
    side, third, level3, w3, near_sum, far0, far1, far2, down0, down1, down2, wide, partial, window3
):
    _, _, _, core = places()
    for r in range(4):
        window3[r, 2 * core] = side[22 + r]
        window3[r, 1] = level3[r]
        window3[r, 2 - 2 * core] = third[r]
    far3 = dot(lanes([window3[r, k] for r in range(4) for k in range(3)]), w3[...])
    local2 = (far2[...] + dot(far3.astype(BF), down2[...])).astype(BF)
    spread1 = dot(local2, down1[...])
    spread1 = jnp.concatenate([spread1[:, :128], spread1[:, 128:]], axis=0)
    local1 = (far1[...] + spread1).astype(BF)
    spread0 = dot(local1, down0[...]).reshape(2, PROBES, 512)
    spread0 = jnp.stack([spread0[:, :, :256], spread0[:, :, 256:]], axis=1).reshape(-1, 256)
    local0 = (far0[...] + spread0).astype(BF)
    for e in (0, 1):
        far_sum = dot(local0[:, 128 * e : 128 * e + 128], wide[...]).reshape(4, PROBES, 256)
        for q in range(4):
            for f in (0, 1):
                part = far_sum[q, :, 128 * f : 128 * f + 128]
                partial[e, 2 * q + f] = near_sum[e, 2 * q + f] + part


def copies_kernel(block, partial, out):
    for peer in range(16):
        out[peer] = block[...]


def fourth_kernel(
    top, partial, up5, up6, up7, top_far, top_leaf, out, padded4, padded5, padded6, padded7
):
    _, col, chip, _ = places()
    blank = jnp.zeros((2, PROBES, 128), BF)
    padded4[pl.ds(0, 2)] = blank
    padded4[pl.ds(18, 2)] = blank
    for c in range(16):
        padded4[c + 2] = top[(chip - c + 16) % 16]
    gap = jnp.zeros((2, PROBES, RANK), BF)
    for padded, transfer, count in ((padded5, up5, 8), (padded6, up6, 4), (padded7, up7, 2)):
        children = padded4[pl.ds(2, 16)].reshape(count, 16 // count, PROBES, 128)
        joined = lanes([children[:, k] for k in range(16 // count)])
        nodes = dot(joined.reshape(count * PROBES, -1), transfer[...])
        padded[pl.ds(0, 2)] = gap
        padded[pl.ds(2, count)] = nodes.astype(BF).reshape(count, PROBES, RANK)
        padded[pl.ds(2 + count, 2)] = gap
    start4 = 2 * (chip // 2)
    window = [padded4[start4 + k] for k in range(6)]
    for padded, level in ((padded5, 5), (padded6, 6), (padded7, 7)):
        start = 2 * (col // (1 << (level - 2)))
        window += [padded[start + k] for k in range(6)]
    local = dot(lanes(window), top_far[...]).astype(BF)
    spread = dot(local, top_leaf[...])
    for e in (0, 1):
        for c in range(8):
            at = 128 * (8 * e + c)
            out[e, c] = (partial[e, c] + spread[:, at : at + 128]).astype(BF)


def route(rule, size_x, size_y):
    pairs = []
    for a in range(size_x):
        for b in range(size_y):
            x, y = rule(a, b)
            if 0 <= x < size_x and 0 <= y < size_y:
                pairs.append((a * size_y + b, x * size_y + y))
    return pairs


def across(core):
    return 1 if core else -1


def shards(probes, leaf_basis, up_transfer, down_transfer, coupling, far_ids):
    size_x, size_y = lax.axis_size("gx"), lax.axis_size("gy")
    both = ("gx", "gy")

    def move(value, rule):
        return lax.ppermute(value, both, route(rule, size_x, size_y))

    above = move(probes, lambda a, b: (a + 1, b))
    below = move(probes, lambda a, b: (a - 1, b))

    hbm = pl.BlockSpec(memory_space=pltpu.MemorySpace.HBM)
    whole = pl.BlockSpec(memory_space=pltpu.VMEM)
    block = (PROBES, 128)
    far_inputs = [
        pltpu.with_memory_space_constraint(value, pltpu.MemorySpace.HBM)
        for value in (far_ids, coupling, down_transfer, up_transfer, leaf_basis.T, probes)
    ]
    weight_shapes = [
        array((36 * RANK, 256)), array((36 * RANK, 128)), array((36 * RANK, 128)),
        array((24 * RANK, RANK)), array((9 * 128, 128)), array((128, 512)), array((128, 256)),
        array((RANK, 128)), array((256, RANK)), array((512, RANK)), array((1024, RANK)),
        array((30 * RANK, RANK)), array((RANK, 16 * 128)),
    ]
    build_scratch = [
        pltpu.SMEM(far_ids.shape, jnp.int32), pltpu.VMEM(coupling.shape, BF),
        pltpu.VMEM(down_transfer.shape, BF),
    ]
    wide, up, own, mine, low, *weights = call(
        start_kernel,
        [
            array((128, 256)), array(up_transfer.shape), array(probes.shape),
            array((2, 4) + block), array((2,) + block),
        ]
        + weight_shapes,
        in_specs=[hbm] * 6,
        scratch=build_scratch
        + [
            pltpu.VMEM(leaf_basis.shape[::-1], BF), pltpu.SemaphoreType.DMA((10,)),
            pltpu.SemaphoreType.DMA((3,)),
        ],
    )(*far_inputs)
    rim, sent = call(rim_kernel, [array((4, 4) + block), array((16, 2) + block)])(
        above, below, wide, low
    )
    gathered = lax.all_to_all(sent, "gx", 0, 0)

    pack, level2, level3_own = call(
        strip_kernel,
        [array((24,) + block), array((8,) + block), array((4, PROBES, RANK))],
        scratch=[pltpu.VMEM((20,) + block, BF), pltpu.VMEM((12,) + block, BF)],
    )(gathered, own, mine, above, below, rim, up)
    packed = move(pack, lambda a, b: (a, b ^ 1))
    far_out, side_out, level3 = call(
        second_kernel,
        [array(block), array((26,) + block), array((4,) + block)],
        scratch=[pltpu.VMEM((20,) + block, BF), pltpu.VMEM((12,) + block, BF)],
    )(packed, gathered, level2, level3_own, own, mine, above, below, rim, up)

    chips = size_y // 2
    side = move(side_out, lambda a, b: (a, b + across(b % 2)))
    third = move(level3, lambda a, b: (a, b + 3 - 6 * (b % 2)))
    top = move(far_out, lambda a, b: (a, 2 * ((b // 2 + a) % chips) + b % 2))

    count = len(weight_shapes)
    weights = call(
        later_kernel,
        weight_shapes,
        in_specs=[hbm] * 3 + [whole] * (3 + count),
        input_output_aliases={6 + at: at for at in range(count)},
        scratch=build_scratch + [pltpu.SemaphoreType.DMA((10,))],
    )(*far_inputs[:3], wide, up, side, *weights)
    w0, w1, w2, w3, table, down0, down1, down2, up5, up6, up7, top_far, top_leaf = weights

    near_sum, far0, far1, far2 = call(
        third_kernel,
        [
            array((2, 8) + block, F32), array((4 * PROBES, 256), F32),
            array((2 * PROBES, 128), F32), array((PROBES, 128), F32),
        ],
        scratch=[
            pltpu.VMEM(lead + block, BF)
            for lead in ((4, 10), (6, 6), (20, 2), (6, 4), (12,), (6, 3))
        ],
    )(own, above, below, mine, packed, rim, gathered, level2, side, w0, w1, w2, table)
    partial = call(
        lower_kernel,
        array((2, 8) + block, F32),
        scratch=[pltpu.VMEM((4, 3) + block, BF)],
    )(side, third, level3, w3, near_sum, far0, far1, far2, down0, down1, down2, wide)
    copies = call(copies_kernel, array((16,) + block))(top, partial)
    top = lax.all_to_all(copies, "gx", 0, 0)

    return call(
        fourth_kernel,
        array(probes.shape),
        scratch=[pltpu.VMEM((20,) + block, BF)]
        + [pltpu.VMEM((nodes + 4, PROBES, RANK), BF) for nodes in (8, 4, 2)],
    )(top, partial, up5, up6, up7, top_far, top_leaf)


def solution(mesh):
    in_specs = (P("gx", "gy", None, None), P(), P(), P(), P(), P())
    out_specs = P("gx", "gy", None, None)
    return jax.shard_map(shards, mesh=mesh, in_specs=in_specs, out_specs=out_specs, check_vma=False)
```

```python
import jax
import jax.numpy as jnp
from jax import lax
from jax.experimental import pallas as pl
from jax.experimental.pallas import tpu as pltpu
from jax.sharding import PartitionSpec as P

LEAF_ROWS = 8
LEAF_COLS = 16
RANK = 64
PROBES = 32
BF = jnp.bfloat16
F32 = jnp.float32

length_scale = 1.5


def dot(left, right):
    return jnp.dot(left, right, preferred_element_type=F32)


def lanes(parts):
    return jnp.concatenate(parts, axis=-1)


def block_slot(e, f, wr, wc):
    return 6 * wr + wc - 3 * min(max(wr - 1 - e, 0), 3) - (
        min(max(wc - 1 - f, 0), 3) if e + 1 <= wr <= e + 3 else 0
    )


def is_near(e, f, wr, wc):
    return e + 1 <= wr <= e + 3 and f + 1 <= wc <= f + 3


def places():
    row = lax.axis_index("gx")
    col = lax.axis_index("gy")
    return row, col, col // 2, col % 2


def build_weights(
    ids_far, coupling_far, down_far, wide, up,
    w0, w1, w2, w3, table, down0, down1, down2, up5, up6, up7, top_far, top_leaf, wx,
    ids, coupling, down, sems,
):
    row, col, _, _ = places()
    first = pltpu.make_async_copy(ids_far, ids, sems.at[8])
    first.start()
    levels = []
    for level in range(8):
        levels.append(
            pltpu.make_async_copy(coupling_far.at[level], coupling.at[level], sems.at[level])
        )
        levels[-1].start()
    other = pltpu.make_async_copy(down_far, down, sems.at[9])
    other.start()

    size = LEAF_ROWS * LEAF_COLS
    theirs = lax.broadcasted_iota(jnp.int32, (size, size), 0)
    ours = lax.broadcasted_iota(jnp.int32, (size, size), 1)
    rows_apart = (theirs // LEAF_COLS - ours // LEAF_COLS).astype(F32)
    cols_apart = (theirs % LEAF_COLS - ours % LEAF_COLS).astype(F32)
    for u in (-1, 0, 1):
        for v in (-1, 0, 1):
            apart_row = rows_apart + float(u * LEAF_ROWS)
            apart_col = cols_apart + float(v * LEAF_COLS)
            scaled = jnp.sqrt(3.0 * (apart_row * apart_row + apart_col * apart_col)) / length_scale
            value = (1.0 + scaled) * jnp.exp(-scaled)
            table[pl.ds((3 * (u + 1) + v + 1) * size, size), :] = value.astype(BF)

    def pair(level, e, wr, wc):
        halves = []
        for f in (0, 1):
            if is_near(e, f, wr, wc):
                halves.append(jnp.zeros((RANK, RANK), BF))
            else:
                halves.append(coupling[level, ids[level, 2 * e + f, block_slot(e, f, wr, wc)]])
        return lanes(halves)

    first.wait()
    levels[0].wait()
    for wr in range(6):
        for wc in range(6):
            at = pl.ds((6 * wr + wc) * RANK, RANK)
            for e in (0, 1):
                w0[at, pl.ds(128 * e, 128)] = pair(0, e, wr, wc)

    for level, out, bit in ((1, w1, row % 2), (2, w2, (row // 2) % 2)):
        levels[level].wait()
        for e in (0, 1):

            @pl.when(bit == e)
            def _(level=level, out=out, e=e):
                for wr in range(6):
                    for wc in range(6):
                        out[pl.ds((6 * wr + wc) * RANK, RANK), :] = pair(level, e, wr, wc)

    def single(level, e, f, wr, wc):
        row_in = jnp.logical_and(wr >= e + 1, wr <= e + 3)
        col_in = jnp.logical_and(wc >= f + 1, wc <= f + 3)
        skipped = 3 * jnp.clip(wr - 1 - e, 0, 3) + jnp.where(row_in, jnp.clip(wc - 1 - f, 0, 3), 0)
        slot = jnp.clip(6 * wr + wc - skipped, 0, 26)
        keep = jnp.where(jnp.logical_and(row_in, col_in), 0.0, 1.0)
        block = coupling[level, ids[level, 2 * e + f, slot]]
        return block * jnp.full((RANK, RANK), keep, F32).astype(BF)

    levels[3].wait()
    e3, f3 = (row // 4) % 2, col % 2
    first3 = 2 - 2 * (row // 8)
    for r in range(4):
        for wc in range(6):
            w3[pl.ds((6 * r + wc) * RANK, RANK), :] = single(3, e3, f3, r + first3, wc)

    @pl.when(row == 0)
    def _():
        for r in range(4):
            for k in (0, 1):
                wc = k + 4 - 4 * f3
                for p in (0, 1):
                    wx[pl.ds((2 * r + k) * RANK, RANK), pl.ds(128 * p, 128)] = lanes(
                        [single(3, e, f3, jnp.int32(r + 2 - 2 * p), wc) for e in (0, 1)]
                    )

    other.wait()
    chain = None
    first_row = 0
    for level in (4, 5, 6, 7):
        levels[level].wait()
        e = (row // (1 << (level - 1))) % 2
        f = (col // (1 << (level - 3))) % 2
        e_up = (row // (1 << (level - 2))) % 2
        f_up = (col // (1 << (level - 4))) % 2
        step = down[level - 1, 2 * e_up + f_up]
        chain = step if chain is None else dot(step, chain).astype(BF)
        rows = 2 if level == 4 else 1
        blocks = [
            single(level, e, f, jnp.int32(2 + r), wc) for wc in range(6) for r in range(rows)
        ]
        stacked = dot(jnp.concatenate(blocks, axis=0), chain).astype(BF)
        top_far[pl.ds(first_row, stacked.shape[0]), :] = stacked
        first_row += stacked.shape[0]
    from4 = jnp.concatenate([up[4, 0], up[4, 2], up[4, 1], up[4, 3]], axis=0)
    from5 = jnp.concatenate([dot(from4, up[5, f]).astype(BF) for f in (0, 1)], axis=0)
    up5[...] = from4
    up6[...] = from5
    up7[...] = jnp.concatenate([dot(from5, up[6, f]).astype(BF) for f in (0, 1)], axis=0)

    all0 = lanes([down[0, k] for k in range(4)])
    none0 = jnp.zeros_like(all0)
    down0[...] = jnp.concatenate([lanes([all0, none0]), lanes([none0, all0])], axis=0)
    e1, e2 = row % 2, (row // 2) % 2
    both1 = lanes([down[1, 2 * e1], down[1, 2 * e1 + 1]])
    none1 = jnp.zeros_like(both1)
    down1[...] = jnp.concatenate([lanes([both1, none1]), lanes([none1, both1])], axis=0)
    down2[...] = lanes([down[2, 2 * e2], down[2, 2 * e2 + 1]])

    node1 = dot(down2[...], down1[...]).astype(BF)
    for t in (0, 1):
        node0 = dot(node1[:, 128 * t : 128 * t + 128], down0[...]).astype(BF)
        for q in (0, 1):
            for e in (0, 1):
                at = 256 * q + 128 * e
                leaves = dot(node0[:, at : at + 128], wide[...]).astype(BF)
                top_leaf[:, pl.ds(256 * (4 * e + 2 * t + q), 256)] = leaves


EARLY_PLANES = 7


def start_kernel(
    ids_far, coupling_far, down_far, up_far, basis_far, own_far,
    wide, up, own, mine, low,
    w0, w1, w2, w3, table, down0, down1, down2, up5, up6, up7, top_far, top_leaf, wx,
    ids, coupling, down, basis, sems, small_sems,
):
    _, _, chip, _ = places()
    small = [
        pltpu.make_async_copy(source, target, small_sems.at[at])
        for at, (source, target) in enumerate(((basis_far, basis), (own_far, own), (up_far, up)))
    ]
    for copy in small:
        copy.start()
    for copy in small:
        copy.wait()
    blank = jnp.zeros_like(basis)
    wide[...] = jnp.concatenate([lanes([basis[...], blank]), lanes([blank, basis[...]])], axis=0)
    coeffs = leaf_coeffs(own[...], wide[...])
    mine[...] = coeffs
    low[...] = to_pairs(raise_pairs(coeffs, up[0].reshape(4 * RANK, RANK))[0])

    @pl.when(chip < EARLY_PLANES)
    def _():
        build_weights(
            ids_far, coupling_far, down_far, wide, up,
            w0, w1, w2, w3, table, down0, down1, down2, up5, up6, up7, top_far, top_leaf, wx,
            ids, coupling, down, sems,
        )


def later_kernel(ids_far, coupling_far, down_far, wide, up, tag, *refs):
    _, _, chip, _ = places()
    weights, scratch = refs[14:28], refs[28:]

    @pl.when(chip >= EARLY_PLANES)
    def _():
        build_weights(ids_far, coupling_far, down_far, wide, up, *weights, *scratch)


def array(shape, kind=BF):
    return jax.ShapeDtypeStruct(shape, kind)


def call(kernel, out_shape, scratch=(), flops=1 << 24, read=1 << 21, **specs):
    return pl.pallas_call(
        kernel,
        out_shape=out_shape,
        **specs,
        scratch_shapes=list(scratch),
        compiler_params=pltpu.CompilerParams(vmem_limit_bytes=16 << 20),
        cost_estimate=pl.CostEstimate(flops=flops, bytes_accessed=read, transcendentals=0),
    )


def leaf_coeffs(tile, wide_basis):
    rows = tile.shape[0]
    split = tile.reshape(rows, 4, 2, PROBES, 128)
    joined = lanes([split[:, :, 0], split[:, :, 1]]).reshape(-1, 256)
    coeffs = lax.dot_general(
        joined, wide_basis, (((1,), (1,)), ((), ())), preferred_element_type=F32
    )
    return coeffs.astype(BF).reshape(rows, 4, PROBES, 128)


def to_pairs(nodes):
    lead = nodes.shape[:-3]
    split = nodes.reshape(lead + (nodes.shape[-3] // 2, 2, PROBES, RANK))
    return lanes([split[..., 0, :, :], split[..., 1, :, :]])


def raise_pairs(pairs, transfer):
    rows, count = pairs.shape[:2]
    split = pairs.reshape(rows // 2, 2, count, PROBES, 128)
    joined = lanes([split[:, 0], split[:, 1]]).reshape(-1, 256)
    return dot(joined, transfer).astype(BF).reshape(rows // 2, count, PROBES, RANK)


def rim_kernel(above, below, wide, low, rim, sent):
    rim[pl.ds(0, 2)] = leaf_coeffs(above[...], wide[...])
    rim[pl.ds(2, 2)] = leaf_coeffs(below[...], wide[...])
    for peer in range(16):
        sent[peer] = low[...]


def strip_kernel(gathered, own, mine, above, below, rim, up, pack, level2, level3, padded1, padded2):
    row, _, _, core = places()
    pairs2 = to_pairs(raise_pairs(gathered[...], up[1].reshape(4 * RANK, RANK)))
    level2[...] = pairs2[:, 0]
    level3[...] = raise_pairs(pairs2, up[2].reshape(4 * RANK, RANK))[:, 0]
    nothing = jnp.zeros((2, PROBES, 128), BF)
    padded1[pl.ds(0, 2)] = nothing
    padded1[pl.ds(18, 2)] = nothing
    padded2[pl.ds(0, 2)] = nothing
    padded2[pl.ds(2, 8)] = level2[...]
    padded2[pl.ds(10, 2)] = nothing
    for r in range(16):
        padded1[r + 2] = gathered[r, 1 - core]
    edge_pair = 3 - 3 * core
    edge_col = 7 - 7 * core
    pack[pl.ds(0, 6)] = padded1[pl.ds(2 * (row // 2), 6)]
    pack[pl.ds(6, 6)] = padded2[pl.ds(2 * (row // 4), 6)]
    pack[12] = lanes([level3[0], level3[1]])
    pack[13] = lanes([level3[2], level3[3]])
    pack[14] = mine[0, edge_pair]
    pack[15] = mine[1, edge_pair]
    pack[16] = own[0, edge_col]
    pack[17] = own[1, edge_col]
    pack[18] = above[1, edge_col]
    pack[19] = below[0, edge_col]
    for r in range(4):
        pack[20 + r] = rim[r, edge_pair]


def second_kernel(
    packed, gathered, level2, level3_own, own, mine, above, below, rim, up,
    far_out, side_out, level3, padded1, padded2,
):
    row, _, _, core = places()
    theirs = []
    for at in (12, 13):
        block = packed[at]
        theirs += [block[:, :RANK], block[:, RANK:]]

    @pl.when(core == 0)
    def _():
        for r in range(4):
            level3[r] = lanes([level3_own[r], theirs[r]])

    @pl.when(core == 1)
    def _():
        for r in range(4):
            level3[r] = lanes([theirs[r], level3_own[r]])

    pairs3 = level3[...]
    nodes4 = raise_pairs(pairs3[:, None], up[3].reshape(4 * RANK, RANK))
    far_out[...] = lanes([nodes4[0, 0], nodes4[1, 0]])

    edge_pair = 3 * core
    edge_col = 7 * core
    nothing = jnp.zeros((2, PROBES, 128), BF)
    padded1[pl.ds(0, 2)] = nothing
    padded1[pl.ds(18, 2)] = nothing
    padded2[pl.ds(0, 2)] = nothing
    padded2[pl.ds(2, 8)] = level2[...]
    padded2[pl.ds(10, 2)] = nothing
    for r in range(16):
        padded1[r + 2] = gathered[r, core]
    side_out[0] = above[1, edge_col]
    side_out[1] = own[0, edge_col]
    side_out[2] = own[1, edge_col]
    side_out[3] = below[0, edge_col]
    side_out[4] = rim[0, edge_pair]
    side_out[5] = rim[1, edge_pair]
    side_out[6] = mine[0, edge_pair]
    side_out[7] = mine[1, edge_pair]
    side_out[8] = rim[2, edge_pair]
    side_out[9] = rim[3, edge_pair]
    side_out[pl.ds(10, 6)] = padded1[pl.ds(2 * (row // 2), 6)]
    side_out[pl.ds(16, 6)] = padded2[pl.ds(2 * (row // 4), 6)]
    side_out[pl.ds(22, 4)] = pairs3


def third_kernel(
    own, above, below, mine, packed, rim, gathered, level2, side, w0, w1, w2, table,
    near_sum, far0, far1, far2,
    near, window0, padded1, window1, padded2, window2,
):
    row, _, _, core = places()

    window0[pl.ds(0, 2), pl.ds(1, 4)] = rim[pl.ds(0, 2)]
    window0[pl.ds(2, 2), pl.ds(1, 4)] = mine[...]
    window0[pl.ds(4, 2), pl.ds(1, 4)] = rim[pl.ds(2, 2)]
    for w in range(6):
        window0[w, 5 * core] = side[4 + w]
    for r in range(2):
        window0[r, 5 - 5 * core] = packed[20 + r]
        window0[2 + r, 5 - 5 * core] = packed[14 + r]
        window0[4 + r, 5 - 5 * core] = packed[22 + r]
    far0[...] = dot(
        lanes([window0[w, pl.ds(k, 4)].reshape(-1, 128) for w in range(6) for k in range(3)]),
        w0[...],
    )

    near[0, pl.ds(1, 8)] = above[1]
    near[1, pl.ds(1, 8)] = own[0]
    near[2, pl.ds(1, 8)] = own[1]
    near[3, pl.ds(1, 8)] = below[0]
    for r in range(4):
        near[r, 9 * core] = side[r]
    near[0, 9 - 9 * core] = packed[18]
    near[1, 9 - 9 * core] = packed[16]
    near[2, 9 - 9 * core] = packed[17]
    near[3, 9 - 9 * core] = packed[19]
    for e in (0, 1):
        joined = lanes([near[e + u, pl.ds(v, 8)].reshape(-1, 128) for u in range(3) for v in range(3)])
        near_sum[e] = dot(joined, table[...]).reshape(8, PROBES, 128)

    empty1 = jnp.zeros((2, 2, PROBES, 128), BF)
    padded1[pl.ds(0, 2)] = empty1
    padded1[pl.ds(2, 16)] = gathered[...]
    padded1[pl.ds(18, 2)] = empty1
    window1[:, pl.ds(1, 2)] = padded1[pl.ds(2 * (row // 2), 6)]
    for w in range(6):
        window1[w, 3 - 3 * core] = packed[w]
        window1[w, 3 * core] = side[10 + w]
    far1[...] = dot(
        lanes([window1[w, pl.ds(k, 2)].reshape(-1, 128) for w in range(6) for k in range(3)]),
        w1[...],
    )

    empty2 = jnp.zeros((2, PROBES, 128), BF)
    padded2[pl.ds(0, 2)] = empty2
    padded2[pl.ds(2, 8)] = level2[...]
    padded2[pl.ds(10, 2)] = empty2
    window2[:, 1] = padded2[pl.ds(2 * (row // 4), 6)]
    for w in range(6):
        window2[w, 2 - 2 * core] = packed[6 + w]
        window2[w, 2 * core] = side[16 + w]
    far2[...] = dot(lanes([window2[w, k] for w in range(6) for k in range(3)]), w2[...])


def lower_kernel(
    side, level3, w3, near_sum, far0, far1, far2, down0, down1, down2, wide, partial, window3
):
    _, _, _, core = places()
    for r in range(4):
        window3[r, 2 * core] = side[22 + r]
        window3[r, 1] = level3[r]
        window3[r, 2 - 2 * core] = jnp.zeros((PROBES, 128), BF)
    far3 = dot(lanes([window3[r, k] for r in range(4) for k in range(3)]), w3[...])
    local2 = (far2[...] + dot(far3.astype(BF), down2[...])).astype(BF)
    spread1 = dot(local2, down1[...])
    spread1 = jnp.concatenate([spread1[:, :128], spread1[:, 128:]], axis=0)
    local1 = (far1[...] + spread1).astype(BF)
    spread0 = dot(local1, down0[...]).reshape(2, PROBES, 512)
    spread0 = jnp.stack([spread0[:, :, :256], spread0[:, :, 256:]], axis=1).reshape(-1, 256)
    local0 = (far0[...] + spread0).astype(BF)
    for e in (0, 1):
        far_sum = dot(local0[:, 128 * e : 128 * e + 128], wide[...]).reshape(4, PROBES, 256)
        for q in range(4):
            for f in (0, 1):
                part = far_sum[q, :, 128 * f : 128 * f + 128]
                partial[e, 2 * q + f] = near_sum[e, 2 * q + f] + part


def copies_kernel(block, third, wx, partial, out):
    row, _, _, _ = places()
    for peer in range(16):
        out[peer, pl.ds(0, PROBES)] = block[...]

    @pl.when(row == 0)
    def _():
        parts = dot(lanes([third[r] for r in range(4)]), wx[...]).astype(BF)
        for node in range(4):
            part = parts[:, RANK * node : RANK * node + RANK]
            packed = lanes([part[: PROBES // 2], part[PROBES // 2 :]])
            for peer in range(4 * node, 4 * node + 4):
                out[peer, pl.ds(PROBES, PROBES // 2)] = packed

    @pl.when(row != 0)
    def _():
        for peer in range(16):
            out[peer, pl.ds(PROBES, PROBES // 2)] = jnp.zeros((PROBES // 2, 128), BF)


def fourth_kernel(
    top, partial, up5, up6, up7, top_far, top_leaf, out, padded4, padded5, padded6, padded7
):
    _, col, chip, _ = places()
    blank = jnp.zeros((2, PROBES, 128), BF)
    padded4[pl.ds(0, 2)] = blank
    padded4[pl.ds(18, 2)] = blank
    for c in range(16):
        padded4[c + 2] = top[(chip - c + 16) % 16, pl.ds(0, PROBES)]
    gap = jnp.zeros((2, PROBES, RANK), BF)
    for padded, transfer, count in ((padded5, up5, 8), (padded6, up6, 4), (padded7, up7, 2)):
        children = padded4[pl.ds(2, 16)].reshape(count, 16 // count, PROBES, 128)
        joined = lanes([children[:, k] for k in range(16 // count)])
        nodes = dot(joined.reshape(count * PROBES, -1), transfer[...])
        padded[pl.ds(0, 2)] = gap
        padded[pl.ds(2, count)] = nodes.astype(BF).reshape(count, PROBES, RANK)
        padded[pl.ds(2 + count, 2)] = gap
    start4 = 2 * (chip // 2)
    window = [padded4[start4 + k] for k in range(6)]
    for padded, level in ((padded5, 5), (padded6, 6), (padded7, 7)):
        start = 2 * (col // (1 << (level - 2)))
        window += [padded[start + k] for k in range(6)]
    packed = top[0, pl.ds(PROBES, PROBES // 2)].astype(F32)
    beyond = jnp.concatenate([packed[:, :RANK], packed[:, RANK:]], axis=0)
    local = (dot(lanes(window), top_far[...]) + beyond).astype(BF)
    spread = dot(local, top_leaf[...])
    for e in (0, 1):
        for c in range(8):
            at = 128 * (8 * e + c)
            out[e, c] = (partial[e, c] + spread[:, at : at + 128]).astype(BF)


def route(rule, size_x, size_y):
    pairs = []
    for a in range(size_x):
        for b in range(size_y):
            x, y = rule(a, b)
            if 0 <= x < size_x and 0 <= y < size_y:
                pairs.append((a * size_y + b, x * size_y + y))
    return pairs


def across(core):
    return 1 if core else -1


def shards(probes, leaf_basis, up_transfer, down_transfer, coupling, far_ids):
    size_x, size_y = lax.axis_size("gx"), lax.axis_size("gy")
    both = ("gx", "gy")

    def move(value, rule):
        return lax.ppermute(value, both, route(rule, size_x, size_y))

    above = move(probes, lambda a, b: (a + 1, b))
    below = move(probes, lambda a, b: (a - 1, b))

    hbm = pl.BlockSpec(memory_space=pltpu.MemorySpace.HBM)
    whole = pl.BlockSpec(memory_space=pltpu.VMEM)
    block = (PROBES, 128)
    far_inputs = [
        pltpu.with_memory_space_constraint(value, pltpu.MemorySpace.HBM)
        for value in (far_ids, coupling, down_transfer, up_transfer, leaf_basis.T, probes)
    ]
    weight_shapes = [
        array((36 * RANK, 256)), array((36 * RANK, 128)), array((36 * RANK, 128)),
        array((24 * RANK, RANK)), array((9 * 128, 128)), array((128, 512)), array((128, 256)),
        array((RANK, 128)), array((256, RANK)), array((512, RANK)), array((1024, RANK)),
        array((30 * RANK, RANK)), array((RANK, 16 * 128)), array((8 * RANK, 4 * RANK)),
    ]
    build_scratch = [
        pltpu.SMEM(far_ids.shape, jnp.int32), pltpu.VMEM(coupling.shape, BF),
        pltpu.VMEM(down_transfer.shape, BF),
    ]
    wide, up, own, mine, low, *weights = call(
        start_kernel,
        [
            array((128, 256)), array(up_transfer.shape), array(probes.shape),
            array((2, 4) + block), array((2,) + block),
        ]
        + weight_shapes,
        in_specs=[hbm] * 6,
        scratch=build_scratch
        + [
            pltpu.VMEM(leaf_basis.shape[::-1], BF), pltpu.SemaphoreType.DMA((10,)),
            pltpu.SemaphoreType.DMA((3,)),
        ],
    )(*far_inputs)
    rim, sent = call(rim_kernel, [array((4, 4) + block), array((16, 2) + block)])(
        above, below, wide, low
    )
    gathered = lax.all_to_all(sent, "gx", 0, 0)

    pack, level2, level3_own = call(
        strip_kernel,
        [array((24,) + block), array((8,) + block), array((4, PROBES, RANK))],
        scratch=[pltpu.VMEM((20,) + block, BF), pltpu.VMEM((12,) + block, BF)],
    )(gathered, own, mine, above, below, rim, up)
    packed = move(pack, lambda a, b: (a, b ^ 1))
    far_out, side_out, level3 = call(
        second_kernel,
        [array(block), array((26,) + block), array((4,) + block)],
        scratch=[pltpu.VMEM((20,) + block, BF), pltpu.VMEM((12,) + block, BF)],
    )(packed, gathered, level2, level3_own, own, mine, above, below, rim, up)

    chips = size_y // 2
    side = move(side_out, lambda a, b: (a, b + across(b % 2)))
    third = move(level3, lambda a, b: (a, b + 3 - 6 * (b % 2)) if a == 0 else (-1, -1))
    top = move(far_out, lambda a, b: (a, 2 * ((b // 2 + a) % chips) + b % 2))

    count = len(weight_shapes)
    weights = call(
        later_kernel,
        weight_shapes,
        in_specs=[hbm] * 3 + [whole] * (3 + count),
        input_output_aliases={6 + at: at for at in range(count)},
        scratch=build_scratch + [pltpu.SemaphoreType.DMA((10,))],
    )(*far_inputs[:3], wide, up, side, *weights)
    w0, w1, w2, w3, table, down0, down1, down2, up5, up6, up7, top_far, top_leaf, wx = weights

    near_sum, far0, far1, far2 = call(
        third_kernel,
        [
            array((2, 8) + block, F32), array((4 * PROBES, 256), F32),
            array((2 * PROBES, 128), F32), array((PROBES, 128), F32),
        ],
        scratch=[
            pltpu.VMEM(lead + block, BF)
            for lead in ((4, 10), (6, 6), (20, 2), (6, 4), (12,), (6, 3))
        ],
    )(own, above, below, mine, packed, rim, gathered, level2, side, w0, w1, w2, table)
    partial = call(
        lower_kernel,
        array((2, 8) + block, F32),
        scratch=[pltpu.VMEM((4, 3) + block, BF)],
    )(side, level3, w3, near_sum, far0, far1, far2, down0, down1, down2, wide)
    copies = call(copies_kernel, array((16, PROBES + PROBES // 2, 128)))(top, third, wx, partial)
    top = lax.all_to_all(copies, "gx", 0, 0)

    return call(
        fourth_kernel,
        array(probes.shape),
        scratch=[pltpu.VMEM((20,) + block, BF)]
        + [pltpu.VMEM((nodes + 4, PROBES, RANK), BF) for nodes in (8, 4, 2)],
    )(top, partial, up5, up6, up7, top_far, top_leaf)


def solution(mesh):
    in_specs = (P("gx", "gy", None, None), P(), P(), P(), P(), P())
    out_specs = P("gx", "gy", None, None)
    return jax.shard_map(shards, mesh=mesh, in_specs=in_specs, out_specs=out_specs, check_vma=False)
```

```python
import jax
import jax.numpy as jnp
from jax import lax
from jax.experimental import pallas as pl
from jax.experimental.pallas import tpu as pltpu
from jax.sharding import PartitionSpec as P

LEAF_ROWS = 8
LEAF_COLS = 16
RANK = 64
PROBES = 32
BF = jnp.bfloat16
F32 = jnp.float32

length_scale = 1.5


def dot(left, right):
    return jnp.dot(left, right, preferred_element_type=F32)


def lanes(parts):
    return jnp.concatenate(parts, axis=-1)


def block_slot(e, f, wr, wc):
    return 6 * wr + wc - 3 * min(max(wr - 1 - e, 0), 3) - (
        min(max(wc - 1 - f, 0), 3) if e + 1 <= wr <= e + 3 else 0
    )


def is_near(e, f, wr, wc):
    return e + 1 <= wr <= e + 3 and f + 1 <= wc <= f + 3


def places():
    row = lax.axis_index("gx")
    col = lax.axis_index("gy")
    return row, col, col // 2, col % 2


def build_weights(
    ids_far, coupling_far, down_far, wide, up,
    w0, w1, w2, w3, table, down0, down1, down2, top_leaf, wt, wx,
    ids, coupling, down, sems,
):
    row, col, _, _ = places()
    first = pltpu.make_async_copy(ids_far, ids, sems.at[8])
    first.start()
    levels = []
    for level in range(8):
        levels.append(
            pltpu.make_async_copy(coupling_far.at[level], coupling.at[level], sems.at[level])
        )
        levels[-1].start()
    other = pltpu.make_async_copy(down_far, down, sems.at[9])
    other.start()

    size = LEAF_ROWS * LEAF_COLS
    theirs = lax.broadcasted_iota(jnp.int32, (size, size), 0)
    ours = lax.broadcasted_iota(jnp.int32, (size, size), 1)
    rows_apart = (theirs // LEAF_COLS - ours // LEAF_COLS).astype(F32)
    cols_apart = (theirs % LEAF_COLS - ours % LEAF_COLS).astype(F32)
    for u in (-1, 0, 1):
        for v in (-1, 0, 1):
            apart_row = rows_apart + float(u * LEAF_ROWS)
            apart_col = cols_apart + float(v * LEAF_COLS)
            scaled = jnp.sqrt(3.0 * (apart_row * apart_row + apart_col * apart_col)) / length_scale
            value = (1.0 + scaled) * jnp.exp(-scaled)
            table[pl.ds((3 * (u + 1) + v + 1) * size, size), :] = value.astype(BF)

    def pair(level, e, wr, wc):
        halves = []
        for f in (0, 1):
            if is_near(e, f, wr, wc):
                halves.append(jnp.zeros((RANK, RANK), BF))
            else:
                halves.append(coupling[level, ids[level, 2 * e + f, block_slot(e, f, wr, wc)]])
        return lanes(halves)

    first.wait()
    levels[0].wait()
    for wr in range(6):
        for wc in range(6):
            at = pl.ds((6 * wr + wc) * RANK, RANK)
            for e in (0, 1):
                w0[at, pl.ds(128 * e, 128)] = pair(0, e, wr, wc)

    for level, out, bit in ((1, w1, row % 2), (2, w2, (row // 2) % 2)):
        levels[level].wait()
        for e in (0, 1):

            @pl.when(bit == e)
            def _(level=level, out=out, e=e):
                for wr in range(6):
                    for wc in range(6):
                        out[pl.ds((6 * wr + wc) * RANK, RANK), :] = pair(level, e, wr, wc)

    def single(level, e, f, wr, wc):
        row_in = jnp.logical_and(wr >= e + 1, wr <= e + 3)
        col_in = jnp.logical_and(wc >= f + 1, wc <= f + 3)
        skipped = 3 * jnp.clip(wr - 1 - e, 0, 3) + jnp.where(row_in, jnp.clip(wc - 1 - f, 0, 3), 0)
        slot = jnp.clip(6 * wr + wc - skipped, 0, 26)
        keep = jnp.where(jnp.logical_and(row_in, col_in), 0.0, 1.0)
        block = coupling[level, ids[level, 2 * e + f, slot]]
        return block * jnp.full((RANK, RANK), keep, F32).astype(BF)

    levels[3].wait()
    e3, f3 = (row // 4) % 2, col % 2
    first3 = 2 - 2 * (row // 8)
    for r in range(4):
        for wc in range(6):
            w3[pl.ds((6 * r + wc) * RANK, RANK), :] = single(3, e3, f3, r + first3, wc)

    @pl.when(row == 0)
    def _():
        for r in range(4):
            for k in (0, 1):
                wc = k + 4 - 4 * f3
                for p in (0, 1):
                    wx[pl.ds((2 * r + k) * RANK, RANK), pl.ds(128 * p, 128)] = lanes(
                        [single(3, e, f3, jnp.int32(r + 2 - 2 * p), wc) for e in (0, 1)]
                    )

    other.wait()
    chip = col // 2
    plane = (chip - row + 16) % 16

    def coupled(level, e, wr, height):
        levels_up = plane // (1 << height), chip // (1 << height)
        f = levels_up[1] % 2
        wc = levels_up[0] - levels_up[1] + 2 + f
        inside = jnp.where(jnp.logical_and(wc >= 0, wc <= 5), 1.0, 0.0)
        block = single(level, e, f, jnp.int32(wr), jnp.clip(wc, 0, 5))
        return block.astype(F32) * jnp.full((RANK, RANK), inside, F32)

    for level in (4, 5, 6, 7):
        levels[level].wait()
    zero = jnp.int32(0)
    inner = coupled(7, zero, 2, 3).astype(BF)
    inner = dot(dot(up[6, (plane // 4) % 2], inner).astype(BF), down[6, (chip // 4) % 2])
    inner = (inner + coupled(6, zero, 2, 2)).astype(BF)
    inner = dot(dot(up[5, (plane // 2) % 2], inner).astype(BF), down[5, (chip // 2) % 2])
    inner = (inner + coupled(5, zero, 2, 1)).astype(BF)
    for source in (0, 1):
        raised = dot(up[4, 2 * source + plane % 2], inner).astype(BF)
        for target in (0, 1):
            local4 = dot(raised, down[4, 2 * target + chip % 2])
            local4 = (local4 + coupled(4, jnp.int32(target), source + 2, 0)).astype(BF)
            nodes = lanes([dot(local4, down[3, 2 * e + f3]).astype(BF) for e in (0, 1)])
            wt[pl.ds(RANK * source, RANK), pl.ds(128 * target, 128)] = nodes

    all0 = lanes([down[0, k] for k in range(4)])
    none0 = jnp.zeros_like(all0)
    down0[...] = jnp.concatenate([lanes([all0, none0]), lanes([none0, all0])], axis=0)
    e1, e2 = row % 2, (row // 2) % 2
    both1 = lanes([down[1, 2 * e1], down[1, 2 * e1 + 1]])
    none1 = jnp.zeros_like(both1)
    down1[...] = jnp.concatenate([lanes([both1, none1]), lanes([none1, both1])], axis=0)
    down2[...] = lanes([down[2, 2 * e2], down[2, 2 * e2 + 1]])

    node1 = dot(down2[...], down1[...]).astype(BF)
    for t in (0, 1):
        node0 = dot(node1[:, 128 * t : 128 * t + 128], down0[...]).astype(BF)
        for q in (0, 1):
            for e in (0, 1):
                at = 256 * q + 128 * e
                leaves = dot(node0[:, at : at + 128], wide[...]).astype(BF)
                top_leaf[:, pl.ds(256 * (4 * e + 2 * t + q), 256)] = leaves


EARLY_PLANES = 7


def start_kernel(
    ids_far, coupling_far, down_far, up_far, basis_far, own_far,
    wide, up, own, mine, low,
    w0, w1, w2, w3, table, down0, down1, down2, top_leaf, wt, wx,
    ids, coupling, down, basis, sems, small_sems,
):
    _, _, chip, _ = places()
    small = [
        pltpu.make_async_copy(source, target, small_sems.at[at])
        for at, (source, target) in enumerate(((basis_far, basis), (own_far, own), (up_far, up)))
    ]
    for copy in small:
        copy.start()
    for copy in small:
        copy.wait()
    blank = jnp.zeros_like(basis)
    wide[...] = jnp.concatenate([lanes([basis[...], blank]), lanes([blank, basis[...]])], axis=0)
    coeffs = leaf_coeffs(own[...], wide[...])
    mine[...] = coeffs
    low[...] = to_pairs(raise_pairs(coeffs, up[0].reshape(4 * RANK, RANK))[0])

    @pl.when(chip < EARLY_PLANES)
    def _():
        build_weights(
            ids_far, coupling_far, down_far, wide, up,
            w0, w1, w2, w3, table, down0, down1, down2, top_leaf, wt, wx,
            ids, coupling, down, sems,
        )


def later_kernel(ids_far, coupling_far, down_far, wide, up, tag, *refs):
    _, _, chip, _ = places()
    weights, scratch = refs[11:22], refs[22:]

    @pl.when(chip >= EARLY_PLANES)
    def _():
        build_weights(ids_far, coupling_far, down_far, wide, up, *weights, *scratch)


def array(shape, kind=BF):
    return jax.ShapeDtypeStruct(shape, kind)


def call(kernel, out_shape, scratch=(), flops=1 << 24, read=1 << 21, **specs):
    return pl.pallas_call(
        kernel,
        out_shape=out_shape,
        **specs,
        scratch_shapes=list(scratch),
        compiler_params=pltpu.CompilerParams(vmem_limit_bytes=16 << 20),
        cost_estimate=pl.CostEstimate(flops=flops, bytes_accessed=read, transcendentals=0),
    )


def leaf_coeffs(tile, wide_basis):
    rows = tile.shape[0]
    split = tile.reshape(rows, 4, 2, PROBES, 128)
    joined = lanes([split[:, :, 0], split[:, :, 1]]).reshape(-1, 256)
    coeffs = lax.dot_general(
        joined, wide_basis, (((1,), (1,)), ((), ())), preferred_element_type=F32
    )
    return coeffs.astype(BF).reshape(rows, 4, PROBES, 128)


def to_pairs(nodes):
    lead = nodes.shape[:-3]
    split = nodes.reshape(lead + (nodes.shape[-3] // 2, 2, PROBES, RANK))
    return lanes([split[..., 0, :, :], split[..., 1, :, :]])


def raise_pairs(pairs, transfer):
    rows, count = pairs.shape[:2]
    split = pairs.reshape(rows // 2, 2, count, PROBES, 128)
    joined = lanes([split[:, 0], split[:, 1]]).reshape(-1, 256)
    return dot(joined, transfer).astype(BF).reshape(rows // 2, count, PROBES, RANK)


def rim_kernel(above, below, wide, low, rim, sent):
    rim[pl.ds(0, 2)] = leaf_coeffs(above[...], wide[...])
    rim[pl.ds(2, 2)] = leaf_coeffs(below[...], wide[...])
    for peer in range(16):
        sent[peer] = low[...]


def strip_kernel(gathered, own, mine, above, below, rim, up, pack, level2, level3, padded1, padded2):
    row, _, _, core = places()
    pairs2 = to_pairs(raise_pairs(gathered[...], up[1].reshape(4 * RANK, RANK)))
    level2[...] = pairs2[:, 0]
    level3[...] = raise_pairs(pairs2, up[2].reshape(4 * RANK, RANK))[:, 0]
    nothing = jnp.zeros((2, PROBES, 128), BF)
    padded1[pl.ds(0, 2)] = nothing
    padded1[pl.ds(18, 2)] = nothing
    padded2[pl.ds(0, 2)] = nothing
    padded2[pl.ds(2, 8)] = level2[...]
    padded2[pl.ds(10, 2)] = nothing
    for r in range(16):
        padded1[r + 2] = gathered[r, 1 - core]
    edge_pair = 3 - 3 * core
    edge_col = 7 - 7 * core
    pack[pl.ds(0, 6)] = padded1[pl.ds(2 * (row // 2), 6)]
    pack[pl.ds(6, 6)] = padded2[pl.ds(2 * (row // 4), 6)]
    pack[12] = lanes([level3[0], level3[1]])
    pack[13] = lanes([level3[2], level3[3]])
    pack[14] = mine[0, edge_pair]
    pack[15] = mine[1, edge_pair]
    pack[16] = own[0, edge_col]
    pack[17] = own[1, edge_col]
    pack[18] = above[1, edge_col]
    pack[19] = below[0, edge_col]
    for r in range(4):
        pack[20 + r] = rim[r, edge_pair]


def second_kernel(
    packed, gathered, level2, level3_own, own, mine, above, below, rim, up,
    far_out, side_out, level3, padded1, padded2,
):
    row, _, _, core = places()
    theirs = []
    for at in (12, 13):
        block = packed[at]
        theirs += [block[:, :RANK], block[:, RANK:]]

    @pl.when(core == 0)
    def _():
        for r in range(4):
            level3[r] = lanes([level3_own[r], theirs[r]])

    @pl.when(core == 1)
    def _():
        for r in range(4):
            level3[r] = lanes([theirs[r], level3_own[r]])

    pairs3 = level3[...]
    nodes4 = raise_pairs(pairs3[:, None], up[3].reshape(4 * RANK, RANK))
    far_out[...] = lanes([nodes4[0, 0], nodes4[1, 0]])

    edge_pair = 3 * core
    edge_col = 7 * core
    nothing = jnp.zeros((2, PROBES, 128), BF)
    padded1[pl.ds(0, 2)] = nothing
    padded1[pl.ds(18, 2)] = nothing
    padded2[pl.ds(0, 2)] = nothing
    padded2[pl.ds(2, 8)] = level2[...]
    padded2[pl.ds(10, 2)] = nothing
    for r in range(16):
        padded1[r + 2] = gathered[r, core]
    side_out[0] = above[1, edge_col]
    side_out[1] = own[0, edge_col]
    side_out[2] = own[1, edge_col]
    side_out[3] = below[0, edge_col]
    side_out[4] = rim[0, edge_pair]
    side_out[5] = rim[1, edge_pair]
    side_out[6] = mine[0, edge_pair]
    side_out[7] = mine[1, edge_pair]
    side_out[8] = rim[2, edge_pair]
    side_out[9] = rim[3, edge_pair]
    side_out[pl.ds(10, 6)] = padded1[pl.ds(2 * (row // 2), 6)]
    side_out[pl.ds(16, 6)] = padded2[pl.ds(2 * (row // 4), 6)]
    side_out[pl.ds(22, 4)] = pairs3


def third_kernel(
    own, above, below, mine, packed, rim, gathered, level2, side, w0, w1, w2, table,
    near_sum, far0, far1, far2,
    near, window0, padded1, window1, padded2, window2,
):
    row, _, _, core = places()

    window0[pl.ds(0, 2), pl.ds(1, 4)] = rim[pl.ds(0, 2)]
    window0[pl.ds(2, 2), pl.ds(1, 4)] = mine[...]
    window0[pl.ds(4, 2), pl.ds(1, 4)] = rim[pl.ds(2, 2)]
    for w in range(6):
        window0[w, 5 * core] = side[4 + w]
    for r in range(2):
        window0[r, 5 - 5 * core] = packed[20 + r]
        window0[2 + r, 5 - 5 * core] = packed[14 + r]
        window0[4 + r, 5 - 5 * core] = packed[22 + r]
    far0[...] = dot(
        lanes([window0[w, pl.ds(k, 4)].reshape(-1, 128) for w in range(6) for k in range(3)]),
        w0[...],
    )

    near[0, pl.ds(1, 8)] = above[1]
    near[1, pl.ds(1, 8)] = own[0]
    near[2, pl.ds(1, 8)] = own[1]
    near[3, pl.ds(1, 8)] = below[0]
    for r in range(4):
        near[r, 9 * core] = side[r]
    near[0, 9 - 9 * core] = packed[18]
    near[1, 9 - 9 * core] = packed[16]
    near[2, 9 - 9 * core] = packed[17]
    near[3, 9 - 9 * core] = packed[19]
    for e in (0, 1):
        joined = lanes([near[e + u, pl.ds(v, 8)].reshape(-1, 128) for u in range(3) for v in range(3)])
        near_sum[e] = dot(joined, table[...]).reshape(8, PROBES, 128)

    empty1 = jnp.zeros((2, 2, PROBES, 128), BF)
    padded1[pl.ds(0, 2)] = empty1
    padded1[pl.ds(2, 16)] = gathered[...]
    padded1[pl.ds(18, 2)] = empty1
    window1[:, pl.ds(1, 2)] = padded1[pl.ds(2 * (row // 2), 6)]
    for w in range(6):
        window1[w, 3 - 3 * core] = packed[w]
        window1[w, 3 * core] = side[10 + w]
    far1[...] = dot(
        lanes([window1[w, pl.ds(k, 2)].reshape(-1, 128) for w in range(6) for k in range(3)]),
        w1[...],
    )

    empty2 = jnp.zeros((2, PROBES, 128), BF)
    padded2[pl.ds(0, 2)] = empty2
    padded2[pl.ds(2, 8)] = level2[...]
    padded2[pl.ds(10, 2)] = empty2
    window2[:, 1] = padded2[pl.ds(2 * (row // 4), 6)]
    for w in range(6):
        window2[w, 2 - 2 * core] = packed[6 + w]
        window2[w, 2 * core] = side[16 + w]
    far2[...] = dot(lanes([window2[w, k] for w in range(6) for k in range(3)]), w2[...])


def lower_kernel(
    side, level3, w3, near_sum, far0, far1, far2, down0, down1, down2, wide, partial, window3
):
    _, _, _, core = places()
    for r in range(4):
        window3[r, 2 * core] = side[22 + r]
        window3[r, 1] = level3[r]
        window3[r, 2 - 2 * core] = jnp.zeros((PROBES, 128), BF)
    far3 = dot(lanes([window3[r, k] for r in range(4) for k in range(3)]), w3[...])
    local2 = (far2[...] + dot(far3.astype(BF), down2[...])).astype(BF)
    spread1 = dot(local2, down1[...])
    spread1 = jnp.concatenate([spread1[:, :128], spread1[:, 128:]], axis=0)
    local1 = (far1[...] + spread1).astype(BF)
    spread0 = dot(local1, down0[...]).reshape(2, PROBES, 512)
    spread0 = jnp.stack([spread0[:, :, :256], spread0[:, :, 256:]], axis=1).reshape(-1, 256)
    local0 = (far0[...] + spread0).astype(BF)
    for e in (0, 1):
        far_sum = dot(local0[:, 128 * e : 128 * e + 128], wide[...]).reshape(4, PROBES, 256)
        for q in range(4):
            for f in (0, 1):
                part = far_sum[q, :, 128 * f : 128 * f + 128]
                partial[e, 2 * q + f] = near_sum[e, 2 * q + f] + part


def share_kernel(block, third, wt, wx, partial, out, parts):
    row, _, _, _ = places()
    parts[...] = dot(block[...], wt[...])

    @pl.when(row == 0)
    def _():
        parts[...] += dot(lanes([third[r] for r in range(4)]), wx[...])

    for node in range(4):
        part = parts[:, RANK * node : RANK * node + RANK].astype(BF)
        packed = lanes([part[: PROBES // 2], part[PROBES // 2 :]])
        for peer in range(4 * node, 4 * node + 4):
            out[peer] = packed


def fourth_kernel(top, partial, top_leaf, out):
    packed = jnp.sum(top[...].astype(F32), axis=0)
    local = jnp.concatenate([packed[:, :RANK], packed[:, RANK:]], axis=0).astype(BF)
    spread = dot(local, top_leaf[...])
    for e in (0, 1):
        for c in range(8):
            at = 128 * (8 * e + c)
            out[e, c] = (partial[e, c] + spread[:, at : at + 128]).astype(BF)


def route(rule, size_x, size_y):
    pairs = []
    for a in range(size_x):
        for b in range(size_y):
            x, y = rule(a, b)
            if 0 <= x < size_x and 0 <= y < size_y:
                pairs.append((a * size_y + b, x * size_y + y))
    return pairs


def across(core):
    return 1 if core else -1


def shards(probes, leaf_basis, up_transfer, down_transfer, coupling, far_ids):
    size_x, size_y = lax.axis_size("gx"), lax.axis_size("gy")
    both = ("gx", "gy")

    def move(value, rule):
        return lax.ppermute(value, both, route(rule, size_x, size_y))

    above = move(probes, lambda a, b: (a + 1, b))
    below = move(probes, lambda a, b: (a - 1, b))

    hbm = pl.BlockSpec(memory_space=pltpu.MemorySpace.HBM)
    whole = pl.BlockSpec(memory_space=pltpu.VMEM)
    block = (PROBES, 128)
    far_inputs = [
        pltpu.with_memory_space_constraint(value, pltpu.MemorySpace.HBM)
        for value in (far_ids, coupling, down_transfer, up_transfer, leaf_basis.T, probes)
    ]
    weight_shapes = [
        array((36 * RANK, 256)), array((36 * RANK, 128)), array((36 * RANK, 128)),
        array((24 * RANK, RANK)), array((9 * 128, 128)), array((128, 512)), array((128, 256)),
        array((RANK, 128)), array((RANK, 16 * 128)), array((2 * RANK, 4 * RANK)),
        array((8 * RANK, 4 * RANK)),
    ]
    build_scratch = [
        pltpu.SMEM(far_ids.shape, jnp.int32), pltpu.VMEM(coupling.shape, BF),
        pltpu.VMEM(down_transfer.shape, BF),
    ]
    wide, up, own, mine, low, *weights = call(
        start_kernel,
        [
            array((128, 256)), array(up_transfer.shape), array(probes.shape),
            array((2, 4) + block), array((2,) + block),
        ]
        + weight_shapes,
        in_specs=[hbm] * 6,
        scratch=build_scratch
        + [
            pltpu.VMEM(leaf_basis.shape[::-1], BF), pltpu.SemaphoreType.DMA((10,)),
            pltpu.SemaphoreType.DMA((3,)),
        ],
    )(*far_inputs)
    rim, sent = call(rim_kernel, [array((4, 4) + block), array((16, 2) + block)])(
        above, below, wide, low
    )
    gathered = lax.all_to_all(sent, "gx", 0, 0)

    pack, level2, level3_own = call(
        strip_kernel,
        [array((24,) + block), array((8,) + block), array((4, PROBES, RANK))],
        scratch=[pltpu.VMEM((20,) + block, BF), pltpu.VMEM((12,) + block, BF)],
    )(gathered, own, mine, above, below, rim, up)
    packed = move(pack, lambda a, b: (a, b ^ 1))
    far_out, side_out, level3 = call(
        second_kernel,
        [array(block), array((26,) + block), array((4,) + block)],
        scratch=[pltpu.VMEM((20,) + block, BF), pltpu.VMEM((12,) + block, BF)],
    )(packed, gathered, level2, level3_own, own, mine, above, below, rim, up)

    chips = size_y // 2
    side = move(side_out, lambda a, b: (a, b + across(b % 2)))
    third = move(level3, lambda a, b: (a, b + 3 - 6 * (b % 2)) if a == 0 else (-1, -1))
    top = move(far_out, lambda a, b: (a, 2 * ((b // 2 + a) % chips) + b % 2))

    count = len(weight_shapes)
    weights = call(
        later_kernel,
        weight_shapes,
        in_specs=[hbm] * 3 + [whole] * (3 + count),
        input_output_aliases={6 + at: at for at in range(count)},
        scratch=build_scratch + [pltpu.SemaphoreType.DMA((10,))],
    )(*far_inputs[:3], wide, up, side, *weights)
    w0, w1, w2, w3, table, down0, down1, down2, top_leaf, wt, wx = weights

    near_sum, far0, far1, far2 = call(
        third_kernel,
        [
            array((2, 8) + block, F32), array((4 * PROBES, 256), F32),
            array((2 * PROBES, 128), F32), array((PROBES, 128), F32),
        ],
        scratch=[
            pltpu.VMEM(lead + block, BF)
            for lead in ((4, 10), (6, 6), (20, 2), (6, 4), (12,), (6, 3))
        ],
    )(own, above, below, mine, packed, rim, gathered, level2, side, w0, w1, w2, table)
    partial = call(
        lower_kernel,
        array((2, 8) + block, F32),
        scratch=[pltpu.VMEM((4, 3) + block, BF)],
    )(side, level3, w3, near_sum, far0, far1, far2, down0, down1, down2, wide)
    shares = call(
        share_kernel,
        array((16, PROBES // 2, 128)),
        scratch=[pltpu.VMEM((PROBES, 4 * RANK), F32)],
    )(top, third, wt, wx, partial)
    top = lax.all_to_all(shares, "gx", 0, 0)

    return call(fourth_kernel, array(probes.shape))(top, partial, top_leaf)


def solution(mesh):
    in_specs = (P("gx", "gy", None, None), P(), P(), P(), P(), P())
    out_specs = P("gx", "gy", None, None)
    return jax.shard_map(shards, mesh=mesh, in_specs=in_specs, out_specs=out_specs, check_vma=False)
```

```python
import jax
import jax.numpy as jnp
from jax import lax
from jax.experimental import pallas as pl
from jax.experimental.pallas import tpu as pltpu
from jax.sharding import PartitionSpec as P

LEAF_ROWS = 8
LEAF_COLS = 16
RANK = 64
PROBES = 32
BF = jnp.bfloat16
F32 = jnp.float32

length_scale = 1.5


def dot(left, right):
    return jnp.dot(left, right, preferred_element_type=F32)


def lanes(parts):
    return jnp.concatenate(parts, axis=-1)


def block_slot(e, f, wr, wc):
    return 6 * wr + wc - 3 * min(max(wr - 1 - e, 0), 3) - (
        min(max(wc - 1 - f, 0), 3) if e + 1 <= wr <= e + 3 else 0
    )


def is_near(e, f, wr, wc):
    return e + 1 <= wr <= e + 3 and f + 1 <= wc <= f + 3


def places():
    row = lax.axis_index("gx")
    col = lax.axis_index("gy")
    return row, col, col // 2, col % 2


def build_weights(
    ids_far, coupling_far, down_far, wide, up,
    w0, w1, w2, w3, table, down0, down1, down2, top_leaf, wt, wx,
    ids, coupling, down, sems,
):
    row, col, _, _ = places()
    first = pltpu.make_async_copy(ids_far, ids, sems.at[8])
    first.start()
    levels = []
    for level in range(8):
        levels.append(
            pltpu.make_async_copy(coupling_far.at[level], coupling.at[level], sems.at[level])
        )
        levels[-1].start()
    other = pltpu.make_async_copy(down_far, down, sems.at[9])
    other.start()

    size = LEAF_ROWS * LEAF_COLS
    theirs = lax.broadcasted_iota(jnp.int32, (size, size), 0)
    ours = lax.broadcasted_iota(jnp.int32, (size, size), 1)
    rows_apart = (theirs // LEAF_COLS - ours // LEAF_COLS).astype(F32)
    cols_apart = (theirs % LEAF_COLS - ours % LEAF_COLS).astype(F32)
    for u in (-1, 0, 1):
        for v in (-1, 0, 1):
            apart_row = rows_apart + float(u * LEAF_ROWS)
            apart_col = cols_apart + float(v * LEAF_COLS)
            scaled = jnp.sqrt(3.0 * (apart_row * apart_row + apart_col * apart_col)) / length_scale
            value = (1.0 + scaled) * jnp.exp(-scaled)
            table[pl.ds((3 * (u + 1) + v + 1) * size, size), :] = value.astype(BF)

    def pair(level, e, wr, wc):
        halves = []
        for f in (0, 1):
            if is_near(e, f, wr, wc):
                halves.append(jnp.zeros((RANK, RANK), BF))
            else:
                halves.append(coupling[level, ids[level, 2 * e + f, block_slot(e, f, wr, wc)]])
        return lanes(halves)

    first.wait()
    levels[0].wait()
    for wr in range(6):
        for wc in range(6):
            at = pl.ds((6 * wr + wc) * RANK, RANK)
            for e in (0, 1):
                w0[at, pl.ds(128 * e, 128)] = pair(0, e, wr, wc)

    for level, out, bit in ((1, w1, row % 2), (2, w2, (row // 2) % 2)):
        levels[level].wait()
        for e in (0, 1):

            @pl.when(bit == e)
            def _(level=level, out=out, e=e):
                for wr in range(6):
                    for wc in range(6):
                        out[pl.ds((6 * wr + wc) * RANK, RANK), :] = pair(level, e, wr, wc)

    def single(level, e, f, wr, wc):
        row_in = jnp.logical_and(wr >= e + 1, wr <= e + 3)
        col_in = jnp.logical_and(wc >= f + 1, wc <= f + 3)
        skipped = 3 * jnp.clip(wr - 1 - e, 0, 3) + jnp.where(row_in, jnp.clip(wc - 1 - f, 0, 3), 0)
        slot = jnp.clip(6 * wr + wc - skipped, 0, 26)
        keep = jnp.where(jnp.logical_and(row_in, col_in), 0.0, 1.0)
        block = coupling[level, ids[level, 2 * e + f, slot]]
        return block * jnp.full((RANK, RANK), keep, F32).astype(BF)

    levels[3].wait()
    e3, f3 = (row // 4) % 2, col % 2
    first3 = 2 - 2 * (row // 8)
    for r in range(4):
        for wc in range(6):
            w3[pl.ds((6 * r + wc) * RANK, RANK), :] = single(3, e3, f3, r + first3, wc)

    @pl.when(row == 0)
    def _():
        for r in range(4):
            for k in (0, 1):
                wc = k + 4 - 4 * f3
                for p in (0, 1):
                    wx[pl.ds((2 * r + k) * RANK, RANK), pl.ds(128 * p, 128)] = lanes(
                        [single(3, e, f3, jnp.int32(r + 2 - 2 * p), wc) for e in (0, 1)]
                    )

    other.wait()
    chip = col // 2
    plane = (chip - row + 16) % 16

    def coupled(level, e, wr, height):
        levels_up = plane // (1 << height), chip // (1 << height)
        f = levels_up[1] % 2
        wc = levels_up[0] - levels_up[1] + 2 + f
        inside = jnp.where(jnp.logical_and(wc >= 0, wc <= 5), 1.0, 0.0)
        block = single(level, e, f, jnp.int32(wr), jnp.clip(wc, 0, 5))
        return block.astype(F32) * jnp.full((RANK, RANK), inside, F32)

    for level in (4, 5, 6, 7):
        levels[level].wait()
    zero = jnp.int32(0)
    inner = coupled(7, zero, 2, 3).astype(BF)
    inner = dot(dot(up[6, (plane // 4) % 2], inner).astype(BF), down[6, (chip // 4) % 2])
    inner = (inner + coupled(6, zero, 2, 2)).astype(BF)
    inner = dot(dot(up[5, (plane // 2) % 2], inner).astype(BF), down[5, (chip // 2) % 2])
    inner = (inner + coupled(5, zero, 2, 1)).astype(BF)
    for source in (0, 1):
        raised = dot(up[4, 2 * source + plane % 2], inner).astype(BF)
        for target in (0, 1):
            local4 = dot(raised, down[4, 2 * target + chip % 2])
            local4 = (local4 + coupled(4, jnp.int32(target), source + 2, 0)).astype(BF)
            nodes = lanes([dot(local4, down[3, 2 * e + f3]).astype(BF) for e in (0, 1)])
            wt[pl.ds(RANK * source, RANK), pl.ds(128 * target, 128)] = nodes

    all0 = lanes([down[0, k] for k in range(4)])
    none0 = jnp.zeros_like(all0)
    down0[...] = jnp.concatenate([lanes([all0, none0]), lanes([none0, all0])], axis=0)
    e1, e2 = row % 2, (row // 2) % 2
    both1 = lanes([down[1, 2 * e1], down[1, 2 * e1 + 1]])
    none1 = jnp.zeros_like(both1)
    down1[...] = jnp.concatenate([lanes([both1, none1]), lanes([none1, both1])], axis=0)
    down2[...] = lanes([down[2, 2 * e2], down[2, 2 * e2 + 1]])

    node1 = dot(down2[...], down1[...]).astype(BF)
    for t in (0, 1):
        node0 = dot(node1[:, 128 * t : 128 * t + 128], down0[...]).astype(BF)
        for q in (0, 1):
            for e in (0, 1):
                at = 256 * q + 128 * e
                leaves = dot(node0[:, at : at + 128], wide[...]).astype(BF)
                top_leaf[:, pl.ds(256 * (4 * e + 2 * t + q), 256)] = leaves


EARLY_PLANES = 7


def start_kernel(
    ids_far, coupling_far, down_far, up_far, basis_far, own_far,
    wide, up, own, mine, low,
    w0, w1, w2, w3, table, down0, down1, down2, top_leaf, wt, wx,
    ids, coupling, down, basis, sems, small_sems,
):
    _, _, chip, _ = places()
    small = [
        pltpu.make_async_copy(source, target, small_sems.at[at])
        for at, (source, target) in enumerate(((basis_far, basis), (own_far, own), (up_far, up)))
    ]
    for copy in small:
        copy.start()
    for copy in small:
        copy.wait()
    blank = jnp.zeros_like(basis)
    wide[...] = jnp.concatenate([lanes([basis[...], blank]), lanes([blank, basis[...]])], axis=0)
    coeffs = leaf_coeffs(own[...], wide[...])
    mine[...] = coeffs
    low[...] = to_pairs(raise_pairs(coeffs, up[0].reshape(4 * RANK, RANK))[0])

    @pl.when(chip < EARLY_PLANES)
    def _():
        build_weights(
            ids_far, coupling_far, down_far, wide, up,
            w0, w1, w2, w3, table, down0, down1, down2, top_leaf, wt, wx,
            ids, coupling, down, sems,
        )


def later_kernel(ids_far, coupling_far, down_far, wide, up, tag, *refs):
    _, _, chip, _ = places()
    weights, scratch = refs[11:22], refs[22:]

    @pl.when(chip >= EARLY_PLANES)
    def _():
        build_weights(ids_far, coupling_far, down_far, wide, up, *weights, *scratch)


def array(shape, kind=BF):
    return jax.ShapeDtypeStruct(shape, kind)


def call(kernel, out_shape, scratch=(), flops=1 << 24, read=1 << 21, **specs):
    return pl.pallas_call(
        kernel,
        out_shape=out_shape,
        **specs,
        scratch_shapes=list(scratch),
        compiler_params=pltpu.CompilerParams(vmem_limit_bytes=16 << 20),
        cost_estimate=pl.CostEstimate(flops=flops, bytes_accessed=read, transcendentals=0),
    )


def leaf_coeffs(tile, wide_basis):
    rows = tile.shape[0]
    split = tile.reshape(rows, 4, 2, PROBES, 128)
    joined = lanes([split[:, :, 0], split[:, :, 1]]).reshape(-1, 256)
    coeffs = lax.dot_general(
        joined, wide_basis, (((1,), (1,)), ((), ())), preferred_element_type=F32
    )
    return coeffs.astype(BF).reshape(rows, 4, PROBES, 128)


def to_pairs(nodes):
    lead = nodes.shape[:-3]
    split = nodes.reshape(lead + (nodes.shape[-3] // 2, 2, PROBES, RANK))
    return lanes([split[..., 0, :, :], split[..., 1, :, :]])


def raise_pairs(pairs, transfer):
    rows, count = pairs.shape[:2]
    split = pairs.reshape(rows // 2, 2, count, PROBES, 128)
    joined = lanes([split[:, 0], split[:, 1]]).reshape(-1, 256)
    return dot(joined, transfer).astype(BF).reshape(rows // 2, count, PROBES, RANK)


def rim_kernel(above, below, wide, low, rim, sent):
    rim[pl.ds(0, 2)] = leaf_coeffs(above[...], wide[...])
    rim[pl.ds(2, 2)] = leaf_coeffs(below[...], wide[...])
    for peer in range(16):
        sent[peer] = low[...]


def strip_kernel(gathered, own, mine, above, below, rim, up, pack, level2, level3, padded1, padded2):
    row, _, _, core = places()
    pairs2 = to_pairs(raise_pairs(gathered[...], up[1].reshape(4 * RANK, RANK)))
    level2[...] = pairs2[:, 0]
    level3[...] = raise_pairs(pairs2, up[2].reshape(4 * RANK, RANK))[:, 0]
    nothing = jnp.zeros((2, PROBES, 128), BF)
    padded1[pl.ds(0, 2)] = nothing
    padded1[pl.ds(18, 2)] = nothing
    padded2[pl.ds(0, 2)] = nothing
    padded2[pl.ds(2, 8)] = level2[...]
    padded2[pl.ds(10, 2)] = nothing
    for r in range(16):
        padded1[r + 2] = gathered[r, 1 - core]
    edge_pair = 3 - 3 * core
    edge_col = 7 - 7 * core
    pack[pl.ds(0, 6)] = padded1[pl.ds(2 * (row // 2), 6)]
    pack[pl.ds(6, 6)] = padded2[pl.ds(2 * (row // 4), 6)]
    pack[12] = lanes([level3[0], level3[1]])
    pack[13] = lanes([level3[2], level3[3]])
    pack[14] = mine[0, edge_pair]
    pack[15] = mine[1, edge_pair]
    pack[16] = own[0, edge_col]
    pack[17] = own[1, edge_col]
    pack[18] = above[1, edge_col]
    pack[19] = below[0, edge_col]
    for r in range(4):
        pack[20 + r] = rim[r, edge_pair]


def second_kernel(
    packed, gathered, level2, level3_own, own, mine, above, below, rim, up,
    far_out, side_out, level3, padded1, padded2,
):
    row, _, _, core = places()
    theirs = []
    for at in (12, 13):
        block = packed[at]
        theirs += [block[:, :RANK], block[:, RANK:]]

    @pl.when(core == 0)
    def _():
        for r in range(4):
            level3[r] = lanes([level3_own[r], theirs[r]])

    @pl.when(core == 1)
    def _():
        for r in range(4):
            level3[r] = lanes([theirs[r], level3_own[r]])

    pairs3 = level3[...]
    nodes4 = raise_pairs(pairs3[:, None], up[3].reshape(4 * RANK, RANK))
    far_out[...] = lanes([nodes4[0, 0], nodes4[1, 0]])

    edge_pair = 3 * core
    edge_col = 7 * core
    nothing = jnp.zeros((2, PROBES, 128), BF)
    padded1[pl.ds(0, 2)] = nothing
    padded1[pl.ds(18, 2)] = nothing
    padded2[pl.ds(0, 2)] = nothing
    padded2[pl.ds(2, 8)] = level2[...]
    padded2[pl.ds(10, 2)] = nothing
    for r in range(16):
        padded1[r + 2] = gathered[r, core]
    side_out[0] = above[1, edge_col]
    side_out[1] = own[0, edge_col]
    side_out[2] = own[1, edge_col]
    side_out[3] = below[0, edge_col]
    side_out[4] = rim[0, edge_pair]
    side_out[5] = rim[1, edge_pair]
    side_out[6] = mine[0, edge_pair]
    side_out[7] = mine[1, edge_pair]
    side_out[8] = rim[2, edge_pair]
    side_out[9] = rim[3, edge_pair]
    side_out[pl.ds(10, 6)] = padded1[pl.ds(2 * (row // 2), 6)]
    side_out[pl.ds(16, 6)] = padded2[pl.ds(2 * (row // 4), 6)]
    side_out[pl.ds(22, 4)] = pairs3


def third_kernel(
    own, above, below, mine, packed, rim, gathered, level2, side, w0, w1, w2, table,
    near_sum, far0, far1, far2,
    near, window0, padded1, window1, padded2, window2,
):
    row, _, _, core = places()

    window0[pl.ds(0, 2), pl.ds(1, 4)] = rim[pl.ds(0, 2)]
    window0[pl.ds(2, 2), pl.ds(1, 4)] = mine[...]
    window0[pl.ds(4, 2), pl.ds(1, 4)] = rim[pl.ds(2, 2)]
    for w in range(6):
        window0[w, 5 * core] = side[4 + w]
    for r in range(2):
        window0[r, 5 - 5 * core] = packed[20 + r]
        window0[2 + r, 5 - 5 * core] = packed[14 + r]
        window0[4 + r, 5 - 5 * core] = packed[22 + r]
    far0[...] = dot(
        lanes([window0[w, pl.ds(k, 4)].reshape(-1, 128) for w in range(6) for k in range(3)]),
        w0[...],
    )

    near[0, pl.ds(1, 8)] = above[1]
    near[1, pl.ds(1, 8)] = own[0]
    near[2, pl.ds(1, 8)] = own[1]
    near[3, pl.ds(1, 8)] = below[0]
    for r in range(4):
        near[r, 9 * core] = side[r]
    near[0, 9 - 9 * core] = packed[18]
    near[1, 9 - 9 * core] = packed[16]
    near[2, 9 - 9 * core] = packed[17]
    near[3, 9 - 9 * core] = packed[19]
    for e in (0, 1):
        joined = lanes([near[e + u, pl.ds(v, 8)].reshape(-1, 128) for u in range(3) for v in range(3)])
        near_sum[e] = dot(joined, table[...]).reshape(8, PROBES, 128)

    empty1 = jnp.zeros((2, 2, PROBES, 128), BF)
    padded1[pl.ds(0, 2)] = empty1
    padded1[pl.ds(2, 16)] = gathered[...]
    padded1[pl.ds(18, 2)] = empty1
    window1[:, pl.ds(1, 2)] = padded1[pl.ds(2 * (row // 2), 6)]
    for w in range(6):
        window1[w, 3 - 3 * core] = packed[w]
        window1[w, 3 * core] = side[10 + w]
    far1[...] = dot(
        lanes([window1[w, pl.ds(k, 2)].reshape(-1, 128) for w in range(6) for k in range(3)]),
        w1[...],
    )

    empty2 = jnp.zeros((2, PROBES, 128), BF)
    padded2[pl.ds(0, 2)] = empty2
    padded2[pl.ds(2, 8)] = level2[...]
    padded2[pl.ds(10, 2)] = empty2
    window2[:, 1] = padded2[pl.ds(2 * (row // 4), 6)]
    for w in range(6):
        window2[w, 2 - 2 * core] = packed[6 + w]
        window2[w, 2 * core] = side[16 + w]
    far2[...] = dot(lanes([window2[w, k] for w in range(6) for k in range(3)]), w2[...])


def lower_kernel(
    side, level3, w3, near_sum, far0, far1, far2, down0, down1, down2, wide, partial, window3
):
    _, _, _, core = places()
    for r in range(4):
        window3[r, 2 * core] = side[22 + r]
        window3[r, 1] = level3[r]
        window3[r, 2 - 2 * core] = jnp.zeros((PROBES, 128), BF)
    far3 = dot(lanes([window3[r, k] for r in range(4) for k in range(3)]), w3[...])
    local2 = (far2[...] + dot(far3.astype(BF), down2[...])).astype(BF)
    spread1 = dot(local2, down1[...])
    spread1 = jnp.concatenate([spread1[:, :128], spread1[:, 128:]], axis=0)
    local1 = (far1[...] + spread1).astype(BF)
    spread0 = dot(local1, down0[...]).reshape(2, PROBES, 512)
    spread0 = jnp.stack([spread0[:, :, :256], spread0[:, :, 256:]], axis=1).reshape(-1, 256)
    local0 = (far0[...] + spread0).astype(BF)
    for e in (0, 1):
        far_sum = dot(local0[:, 128 * e : 128 * e + 128], wide[...]).reshape(4, PROBES, 256)
        for q in range(4):
            for f in (0, 1):
                part = far_sum[q, :, 128 * f : 128 * f + 128]
                partial[e, 2 * q + f] = near_sum[e, 2 * q + f] + part


def arrival_kernel(block, partial, out):
    out[...] = block[...]


def share_kernel(block, third, wt, wx, partial, out, parts):
    row, _, _, _ = places()
    parts[...] = dot(block[...], wt[...])

    @pl.when(row == 0)
    def _():
        parts[...] += dot(lanes([third[r] for r in range(4)]), wx[...])

    for node in range(4):
        part = parts[:, RANK * node : RANK * node + RANK].astype(BF)
        packed = lanes([part[: PROBES // 2], part[PROBES // 2 :]])
        for peer in range(4 * node, 4 * node + 4):
            out[peer] = packed


def fourth_kernel(top, partial, top_leaf, out):
    packed = jnp.sum(top[...].astype(F32), axis=0)
    local = jnp.concatenate([packed[:, :RANK], packed[:, RANK:]], axis=0).astype(BF)
    spread = dot(local, top_leaf[...])
    for e in (0, 1):
        for c in range(8):
            at = 128 * (8 * e + c)
            out[e, c] = (partial[e, c] + spread[:, at : at + 128]).astype(BF)


def route(rule, size_x, size_y):
    pairs = []
    for a in range(size_x):
        for b in range(size_y):
            x, y = rule(a, b)
            if 0 <= x < size_x and 0 <= y < size_y:
                pairs.append((a * size_y + b, x * size_y + y))
    return pairs


def across(core):
    return 1 if core else -1


def shards(probes, leaf_basis, up_transfer, down_transfer, coupling, far_ids):
    size_x, size_y = lax.axis_size("gx"), lax.axis_size("gy")
    both = ("gx", "gy")

    def move(value, rule):
        return lax.ppermute(value, both, route(rule, size_x, size_y))

    above = move(probes, lambda a, b: (a + 1, b))
    below = move(probes, lambda a, b: (a - 1, b))

    hbm = pl.BlockSpec(memory_space=pltpu.MemorySpace.HBM)
    whole = pl.BlockSpec(memory_space=pltpu.VMEM)
    block = (PROBES, 128)
    far_inputs = [
        pltpu.with_memory_space_constraint(value, pltpu.MemorySpace.HBM)
        for value in (far_ids, coupling, down_transfer, up_transfer, leaf_basis.T, probes)
    ]
    weight_shapes = [
        array((36 * RANK, 256)), array((36 * RANK, 128)), array((36 * RANK, 128)),
        array((24 * RANK, RANK)), array((9 * 128, 128)), array((128, 512)), array((128, 256)),
        array((RANK, 128)), array((RANK, 16 * 128)), array((2 * RANK, 4 * RANK)),
        array((8 * RANK, 4 * RANK)),
    ]
    build_scratch = [
        pltpu.SMEM(far_ids.shape, jnp.int32), pltpu.VMEM(coupling.shape, BF),
        pltpu.VMEM(down_transfer.shape, BF),
    ]
    wide, up, own, mine, low, *weights = call(
        start_kernel,
        [
            array((128, 256)), array(up_transfer.shape), array(probes.shape),
            array((2, 4) + block), array((2,) + block),
        ]
        + weight_shapes,
        in_specs=[hbm] * 6,
        scratch=build_scratch
        + [
            pltpu.VMEM(leaf_basis.shape[::-1], BF), pltpu.SemaphoreType.DMA((10,)),
            pltpu.SemaphoreType.DMA((3,)),
        ],
    )(*far_inputs)
    rim, sent = call(rim_kernel, [array((4, 4) + block), array((16, 2) + block)])(
        above, below, wide, low
    )
    gathered = lax.all_to_all(sent, "gx", 0, 0)

    pack, level2, level3_own = call(
        strip_kernel,
        [array((24,) + block), array((8,) + block), array((4, PROBES, RANK))],
        scratch=[pltpu.VMEM((20,) + block, BF), pltpu.VMEM((12,) + block, BF)],
    )(gathered, own, mine, above, below, rim, up)
    packed = move(pack, lambda a, b: (a, b ^ 1))
    far_out, side_out, level3 = call(
        second_kernel,
        [array(block), array((26,) + block), array((4,) + block)],
        scratch=[pltpu.VMEM((20,) + block, BF), pltpu.VMEM((12,) + block, BF)],
    )(packed, gathered, level2, level3_own, own, mine, above, below, rim, up)

    chips = size_y // 2
    side = move(side_out, lambda a, b: (a, b + across(b % 2)))
    third = move(level3, lambda a, b: (a, b + 3 - 6 * (b % 2)) if a == 0 else (-1, -1))
    top = move(far_out, lambda a, b: (a, 2 * ((b // 2 + a) % chips) + b % 2))

    count = len(weight_shapes)
    weights = call(
        later_kernel,
        weight_shapes,
        in_specs=[hbm] * 3 + [whole] * (3 + count),
        input_output_aliases={6 + at: at for at in range(count)},
        scratch=build_scratch + [pltpu.SemaphoreType.DMA((10,))],
    )(*far_inputs[:3], wide, up, side, *weights)
    w0, w1, w2, w3, table, down0, down1, down2, top_leaf, wt, wx = weights

    near_sum, far0, far1, far2 = call(
        third_kernel,
        [
            array((2, 8) + block, F32), array((4 * PROBES, 256), F32),
            array((2 * PROBES, 128), F32), array((PROBES, 128), F32),
        ],
        scratch=[
            pltpu.VMEM(lead + block, BF)
            for lead in ((4, 10), (6, 6), (20, 2), (6, 4), (12,), (6, 3))
        ],
    )(own, above, below, mine, packed, rim, gathered, level2, side, w0, w1, w2, table)
    partial = call(
        lower_kernel,
        array((2, 8) + block, F32),
        scratch=[pltpu.VMEM((4, 3) + block, BF)],
    )(side, level3, w3, near_sum, far0, far1, far2, down0, down1, down2, wide)
    arrived = call(arrival_kernel, array(block), flops=1 << 36)(top, partial)
    shares = call(
        share_kernel,
        array((16, PROBES // 2, 128)),
        scratch=[pltpu.VMEM((PROBES, 4 * RANK), F32)],
    )(arrived, third, wt, wx, partial)
    top = lax.all_to_all(shares, "gx", 0, 0)

    return call(fourth_kernel, array(probes.shape))(top, partial, top_leaf)


def solution(mesh):
    in_specs = (P("gx", "gy", None, None), P(), P(), P(), P(), P())
    out_specs = P("gx", "gy", None, None)
    return jax.shard_map(shards, mesh=mesh, in_specs=in_specs, out_specs=out_specs, check_vma=False)
```

```python
import jax
import jax.numpy as jnp
from jax import lax
from jax.experimental import pallas as pl
from jax.experimental.pallas import tpu as pltpu
from jax.sharding import PartitionSpec as P

LEAF_ROWS = 8
LEAF_COLS = 16
RANK = 64
PROBES = 32
BF = jnp.bfloat16
F32 = jnp.float32

length_scale = 1.5


def dot(left, right):
    return jnp.dot(left, right, preferred_element_type=F32)


def lanes(parts):
    return jnp.concatenate(parts, axis=-1)


def block_slot(e, f, wr, wc):
    return 6 * wr + wc - 3 * min(max(wr - 1 - e, 0), 3) - (
        min(max(wc - 1 - f, 0), 3) if e + 1 <= wr <= e + 3 else 0
    )


def is_near(e, f, wr, wc):
    return e + 1 <= wr <= e + 3 and f + 1 <= wc <= f + 3


def places():
    row = lax.axis_index("gx")
    col = lax.axis_index("gy")
    return row, col, col // 2, col % 2


def build_weights(
    ids_far, coupling_far, down_far, wide, up,
    w0, w1, w2, w3, table, down0, down1, down2, top_leaf, wt, wx,
    ids, coupling, down, sems,
):
    row, col, _, _ = places()
    first = pltpu.make_async_copy(ids_far, ids, sems.at[8])
    first.start()
    levels = []
    for level in range(8):
        levels.append(
            pltpu.make_async_copy(coupling_far.at[level], coupling.at[level], sems.at[level])
        )
        levels[-1].start()
    other = pltpu.make_async_copy(down_far, down, sems.at[9])
    other.start()

    size = LEAF_ROWS * LEAF_COLS
    theirs = lax.broadcasted_iota(jnp.int32, (size, size), 0)
    ours = lax.broadcasted_iota(jnp.int32, (size, size), 1)
    rows_apart = (theirs // LEAF_COLS - ours // LEAF_COLS).astype(F32)
    cols_apart = (theirs % LEAF_COLS - ours % LEAF_COLS).astype(F32)
    for u in (-1, 0, 1):
        for v in (-1, 0, 1):
            apart_row = rows_apart + float(u * LEAF_ROWS)
            apart_col = cols_apart + float(v * LEAF_COLS)
            scaled = jnp.sqrt(3.0 * (apart_row * apart_row + apart_col * apart_col)) / length_scale
            value = (1.0 + scaled) * jnp.exp(-scaled)
            table[pl.ds((3 * (u + 1) + v + 1) * size, size), :] = value.astype(BF)

    def pair(level, e, wr, wc):
        halves = []
        for f in (0, 1):
            if is_near(e, f, wr, wc):
                halves.append(jnp.zeros((RANK, RANK), BF))
            else:
                halves.append(coupling[level, ids[level, 2 * e + f, block_slot(e, f, wr, wc)]])
        return lanes(halves)

    def single(level, e, f, wr, wc):
        row_in = jnp.logical_and(wr >= e + 1, wr <= e + 3)
        col_in = jnp.logical_and(wc >= f + 1, wc <= f + 3)
        skipped = 3 * jnp.clip(wr - 1 - e, 0, 3) + jnp.where(row_in, jnp.clip(wc - 1 - f, 0, 3), 0)
        slot = jnp.clip(6 * wr + wc - skipped, 0, 26)
        keep = jnp.where(jnp.logical_and(row_in, col_in), 0.0, 1.0)
        block = coupling[level, ids[level, 2 * e + f, slot]]
        return block * jnp.full((RANK, RANK), keep, F32).astype(BF)

    e3, f3 = (row // 4) % 2, col % 2
    first.wait()
    levels[0].wait()
    other.wait()
    chip = col // 2
    plane = (chip - row + 16) % 16

    def coupled(level, e, wr, height):
        levels_up = plane // (1 << height), chip // (1 << height)
        f = levels_up[1] % 2
        wc = levels_up[0] - levels_up[1] + 2 + f
        inside = jnp.where(jnp.logical_and(wc >= 0, wc <= 5), 1.0, 0.0)
        block = single(level, e, f, jnp.int32(wr), jnp.clip(wc, 0, 5))
        return block.astype(F32) * jnp.full((RANK, RANK), inside, F32)

    for level in (4, 5, 6, 7):
        levels[level].wait()
    zero = jnp.int32(0)
    inner = coupled(7, zero, 2, 3).astype(BF)
    inner = dot(dot(up[6, (plane // 4) % 2], inner).astype(BF), down[6, (chip // 4) % 2])
    inner = (inner + coupled(6, zero, 2, 2)).astype(BF)
    inner = dot(dot(up[5, (plane // 2) % 2], inner).astype(BF), down[5, (chip // 2) % 2])
    inner = (inner + coupled(5, zero, 2, 1)).astype(BF)
    for source in (0, 1):
        raised = dot(up[4, 2 * source + plane % 2], inner).astype(BF)
        for target in (0, 1):
            local4 = dot(raised, down[4, 2 * target + chip % 2])
            local4 = (local4 + coupled(4, jnp.int32(target), source + 2, 0)).astype(BF)
            nodes = lanes([dot(local4, down[3, 2 * e + f3]).astype(BF) for e in (0, 1)])
            wt[pl.ds(RANK * source, RANK), pl.ds(128 * target, 128)] = nodes

    for wr in range(6):
        for wc in range(6):
            at = pl.ds((6 * wr + wc) * RANK, RANK)
            for e in (0, 1):
                w0[at, pl.ds(128 * e, 128)] = pair(0, e, wr, wc)

    for level, out, bit in ((1, w1, row % 2), (2, w2, (row // 2) % 2)):
        levels[level].wait()
        for e in (0, 1):

            @pl.when(bit == e)
            def _(level=level, out=out, e=e):
                for wr in range(6):
                    for wc in range(6):
                        out[pl.ds((6 * wr + wc) * RANK, RANK), :] = pair(level, e, wr, wc)

    levels[3].wait()
    first3 = 2 - 2 * (row // 8)
    for r in range(4):
        for wc in range(6):
            w3[pl.ds((6 * r + wc) * RANK, RANK), :] = single(3, e3, f3, r + first3, wc)

    @pl.when(row == 0)
    def _():
        for r in range(4):
            for k in (0, 1):
                wc = k + 4 - 4 * f3
                for p in (0, 1):
                    wx[pl.ds((2 * r + k) * RANK, RANK), pl.ds(128 * p, 128)] = lanes(
                        [single(3, e, f3, jnp.int32(r + 2 - 2 * p), wc) for e in (0, 1)]
                    )

    all0 = lanes([down[0, k] for k in range(4)])
    none0 = jnp.zeros_like(all0)
    down0[...] = jnp.concatenate([lanes([all0, none0]), lanes([none0, all0])], axis=0)
    e1, e2 = row % 2, (row // 2) % 2
    both1 = lanes([down[1, 2 * e1], down[1, 2 * e1 + 1]])
    none1 = jnp.zeros_like(both1)
    down1[...] = jnp.concatenate([lanes([both1, none1]), lanes([none1, both1])], axis=0)
    down2[...] = lanes([down[2, 2 * e2], down[2, 2 * e2 + 1]])

    node1 = dot(down2[...], down1[...]).astype(BF)
    for t in (0, 1):
        node0 = dot(node1[:, 128 * t : 128 * t + 128], down0[...]).astype(BF)
        for q in (0, 1):
            for e in (0, 1):
                at = 256 * q + 128 * e
                leaves = dot(node0[:, at : at + 128], wide[...]).astype(BF)
                top_leaf[:, pl.ds(256 * (4 * e + 2 * t + q), 256)] = leaves


EARLY_PLANES = 7


def start_kernel(
    ids_far, coupling_far, down_far, up_far, basis_far, own_far,
    wide, up, own, mine, low,
    w0, w1, w2, w3, table, down0, down1, down2, top_leaf, wt, wx,
    ids, coupling, down, basis, sems, small_sems,
):
    _, _, chip, _ = places()
    small = [
        pltpu.make_async_copy(source, target, small_sems.at[at])
        for at, (source, target) in enumerate(((basis_far, basis), (own_far, own), (up_far, up)))
    ]
    for copy in small:
        copy.start()
    for copy in small:
        copy.wait()
    blank = jnp.zeros_like(basis)
    wide[...] = jnp.concatenate([lanes([basis[...], blank]), lanes([blank, basis[...]])], axis=0)
    coeffs = leaf_coeffs(own[...], wide[...])
    mine[...] = coeffs
    low[...] = to_pairs(raise_pairs(coeffs, up[0].reshape(4 * RANK, RANK))[0])

    @pl.when(chip < EARLY_PLANES)
    def _():
        build_weights(
            ids_far, coupling_far, down_far, wide, up,
            w0, w1, w2, w3, table, down0, down1, down2, top_leaf, wt, wx,
            ids, coupling, down, sems,
        )


def later_kernel(ids_far, coupling_far, down_far, wide, up, tag, *refs):
    _, _, chip, _ = places()
    weights, scratch = refs[11:22], refs[22:]

    @pl.when(chip >= EARLY_PLANES)
    def _():
        build_weights(ids_far, coupling_far, down_far, wide, up, *weights, *scratch)


def array(shape, kind=BF):
    return jax.ShapeDtypeStruct(shape, kind)


def call(kernel, out_shape, scratch=(), flops=1 << 24, read=1 << 21, **specs):
    return pl.pallas_call(
        kernel,
        out_shape=out_shape,
        **specs,
        scratch_shapes=list(scratch),
        compiler_params=pltpu.CompilerParams(vmem_limit_bytes=16 << 20),
        cost_estimate=pl.CostEstimate(flops=flops, bytes_accessed=read, transcendentals=0),
    )


def leaf_coeffs(tile, wide_basis):
    rows = tile.shape[0]
    split = tile.reshape(rows, 4, 2, PROBES, 128)
    joined = lanes([split[:, :, 0], split[:, :, 1]]).reshape(-1, 256)
    coeffs = lax.dot_general(
        joined, wide_basis, (((1,), (1,)), ((), ())), preferred_element_type=F32
    )
    return coeffs.astype(BF).reshape(rows, 4, PROBES, 128)


def to_pairs(nodes):
    lead = nodes.shape[:-3]
    split = nodes.reshape(lead + (nodes.shape[-3] // 2, 2, PROBES, RANK))
    return lanes([split[..., 0, :, :], split[..., 1, :, :]])


def raise_pairs(pairs, transfer):
    rows, count = pairs.shape[:2]
    split = pairs.reshape(rows // 2, 2, count, PROBES, 128)
    joined = lanes([split[:, 0], split[:, 1]]).reshape(-1, 256)
    return dot(joined, transfer).astype(BF).reshape(rows // 2, count, PROBES, RANK)


def rim_kernel(above, below, wide, low, rim, sent):
    rim[pl.ds(0, 2)] = leaf_coeffs(above[...], wide[...])
    rim[pl.ds(2, 2)] = leaf_coeffs(below[...], wide[...])
    for peer in range(16):
        sent[peer] = low[...]


def strip_kernel(gathered, own, mine, above, below, rim, up, pack, level2, level3, padded1, padded2):
    row, _, _, core = places()
    pairs2 = to_pairs(raise_pairs(gathered[...], up[1].reshape(4 * RANK, RANK)))
    level2[...] = pairs2[:, 0]
    level3[...] = raise_pairs(pairs2, up[2].reshape(4 * RANK, RANK))[:, 0]
    nothing = jnp.zeros((2, PROBES, 128), BF)
    padded1[pl.ds(0, 2)] = nothing
    padded1[pl.ds(18, 2)] = nothing
    padded2[pl.ds(0, 2)] = nothing
    padded2[pl.ds(2, 8)] = level2[...]
    padded2[pl.ds(10, 2)] = nothing
    for r in range(16):
        padded1[r + 2] = gathered[r, 1 - core]
    edge_pair = 3 - 3 * core
    edge_col = 7 - 7 * core
    pack[pl.ds(0, 6)] = padded1[pl.ds(2 * (row // 2), 6)]
    pack[pl.ds(6, 6)] = padded2[pl.ds(2 * (row // 4), 6)]
    pack[12] = lanes([level3[0], level3[1]])
    pack[13] = lanes([level3[2], level3[3]])
    pack[14] = mine[0, edge_pair]
    pack[15] = mine[1, edge_pair]
    pack[16] = own[0, edge_col]
    pack[17] = own[1, edge_col]
    pack[18] = above[1, edge_col]
    pack[19] = below[0, edge_col]
    for r in range(4):
        pack[20 + r] = rim[r, edge_pair]


def second_kernel(
    packed, gathered, level2, level3_own, own, mine, above, below, rim, up,
    far_out, side_out, level3, padded1, padded2,
):
    row, _, _, core = places()
    theirs = []
    for at in (12, 13):
        block = packed[at]
        theirs += [block[:, :RANK], block[:, RANK:]]

    @pl.when(core == 0)
    def _():
        for r in range(4):
            level3[r] = lanes([level3_own[r], theirs[r]])

    @pl.when(core == 1)
    def _():
        for r in range(4):
            level3[r] = lanes([theirs[r], level3_own[r]])

    pairs3 = level3[...]
    nodes4 = raise_pairs(pairs3[:, None], up[3].reshape(4 * RANK, RANK))
    far_out[...] = lanes([nodes4[0, 0], nodes4[1, 0]])

    edge_pair = 3 * core
    edge_col = 7 * core
    nothing = jnp.zeros((2, PROBES, 128), BF)
    padded1[pl.ds(0, 2)] = nothing
    padded1[pl.ds(18, 2)] = nothing
    padded2[pl.ds(0, 2)] = nothing
    padded2[pl.ds(2, 8)] = level2[...]
    padded2[pl.ds(10, 2)] = nothing
    for r in range(16):
        padded1[r + 2] = gathered[r, core]
    side_out[0] = above[1, edge_col]
    side_out[1] = own[0, edge_col]
    side_out[2] = own[1, edge_col]
    side_out[3] = below[0, edge_col]
    side_out[4] = rim[0, edge_pair]
    side_out[5] = rim[1, edge_pair]
    side_out[6] = mine[0, edge_pair]
    side_out[7] = mine[1, edge_pair]
    side_out[8] = rim[2, edge_pair]
    side_out[9] = rim[3, edge_pair]
    side_out[pl.ds(10, 6)] = padded1[pl.ds(2 * (row // 2), 6)]
    side_out[pl.ds(16, 6)] = padded2[pl.ds(2 * (row // 4), 6)]
    side_out[pl.ds(22, 4)] = pairs3


def third_kernel(
    own, above, below, mine, packed, rim, gathered, level2, side, w0, w1, w2, table,
    near_sum, far0, far1, far2,
    near, window0, padded1, window1, padded2, window2,
):
    row, _, _, core = places()

    window0[pl.ds(0, 2), pl.ds(1, 4)] = rim[pl.ds(0, 2)]
    window0[pl.ds(2, 2), pl.ds(1, 4)] = mine[...]
    window0[pl.ds(4, 2), pl.ds(1, 4)] = rim[pl.ds(2, 2)]
    for w in range(6):
        window0[w, 5 * core] = side[4 + w]
    for r in range(2):
        window0[r, 5 - 5 * core] = packed[20 + r]
        window0[2 + r, 5 - 5 * core] = packed[14 + r]
        window0[4 + r, 5 - 5 * core] = packed[22 + r]
    far0[...] = dot(
        lanes([window0[w, pl.ds(k, 4)].reshape(-1, 128) for w in range(6) for k in range(3)]),
        w0[...],
    )

    near[0, pl.ds(1, 8)] = above[1]
    near[1, pl.ds(1, 8)] = own[0]
    near[2, pl.ds(1, 8)] = own[1]
    near[3, pl.ds(1, 8)] = below[0]
    for r in range(4):
        near[r, 9 * core] = side[r]
    near[0, 9 - 9 * core] = packed[18]
    near[1, 9 - 9 * core] = packed[16]
    near[2, 9 - 9 * core] = packed[17]
    near[3, 9 - 9 * core] = packed[19]
    for e in (0, 1):
        joined = lanes([near[e + u, pl.ds(v, 8)].reshape(-1, 128) for u in range(3) for v in range(3)])
        near_sum[e] = dot(joined, table[...]).reshape(8, PROBES, 128)

    empty1 = jnp.zeros((2, 2, PROBES, 128), BF)
    padded1[pl.ds(0, 2)] = empty1
    padded1[pl.ds(2, 16)] = gathered[...]
    padded1[pl.ds(18, 2)] = empty1
    window1[:, pl.ds(1, 2)] = padded1[pl.ds(2 * (row // 2), 6)]
    for w in range(6):
        window1[w, 3 - 3 * core] = packed[w]
        window1[w, 3 * core] = side[10 + w]
    far1[...] = dot(
        lanes([window1[w, pl.ds(k, 2)].reshape(-1, 128) for w in range(6) for k in range(3)]),
        w1[...],
    )

    empty2 = jnp.zeros((2, PROBES, 128), BF)
    padded2[pl.ds(0, 2)] = empty2
    padded2[pl.ds(2, 8)] = level2[...]
    padded2[pl.ds(10, 2)] = empty2
    window2[:, 1] = padded2[pl.ds(2 * (row // 4), 6)]
    for w in range(6):
        window2[w, 2 - 2 * core] = packed[6 + w]
        window2[w, 2 * core] = side[16 + w]
    far2[...] = dot(lanes([window2[w, k] for w in range(6) for k in range(3)]), w2[...])


def lower_kernel(
    side, level3, w3, near_sum, far0, far1, far2, down0, down1, down2, wide, partial, window3
):
    _, _, _, core = places()
    for r in range(4):
        window3[r, 2 * core] = side[22 + r]
        window3[r, 1] = level3[r]
        window3[r, 2 - 2 * core] = jnp.zeros((PROBES, 128), BF)
    far3 = dot(lanes([window3[r, k] for r in range(4) for k in range(3)]), w3[...])
    local2 = (far2[...] + dot(far3.astype(BF), down2[...])).astype(BF)
    spread1 = dot(local2, down1[...])
    spread1 = jnp.concatenate([spread1[:, :128], spread1[:, 128:]], axis=0)
    local1 = (far1[...] + spread1).astype(BF)
    spread0 = dot(local1, down0[...]).reshape(2, PROBES, 512)
    spread0 = jnp.stack([spread0[:, :, :256], spread0[:, :, 256:]], axis=1).reshape(-1, 256)
    local0 = (far0[...] + spread0).astype(BF)
    for e in (0, 1):
        far_sum = dot(local0[:, 128 * e : 128 * e + 128], wide[...]).reshape(4, PROBES, 256)
        for q in range(4):
            for f in (0, 1):
                part = far_sum[q, :, 128 * f : 128 * f + 128]
                partial[e, 2 * q + f] = near_sum[e, 2 * q + f] + part


def arrival_kernel(block, partial, out):
    out[...] = block[...]


def share_kernel(block, third, wt, wx, partial, out, parts):
    row, _, _, _ = places()
    parts[...] = dot(block[...], wt[...])

    @pl.when(row == 0)
    def _():
        parts[...] += dot(lanes([third[r] for r in range(4)]), wx[...])

    for node in range(4):
        part = parts[:, RANK * node : RANK * node + RANK].astype(BF)
        packed = lanes([part[: PROBES // 2], part[PROBES // 2 :]])
        for peer in range(4 * node, 4 * node + 4):
            out[peer] = packed


def fourth_kernel(top, partial, top_leaf, out):
    packed = jnp.sum(top[...].astype(F32), axis=0)
    local = jnp.concatenate([packed[:, :RANK], packed[:, RANK:]], axis=0).astype(BF)
    spread = dot(local, top_leaf[...])
    for e in (0, 1):
        for c in range(8):
            at = 128 * (8 * e + c)
            out[e, c] = (partial[e, c] + spread[:, at : at + 128]).astype(BF)


def route(rule, size_x, size_y):
    pairs = []
    for a in range(size_x):
        for b in range(size_y):
            x, y = rule(a, b)
            if 0 <= x < size_x and 0 <= y < size_y:
                pairs.append((a * size_y + b, x * size_y + y))
    return pairs


def across(core):
    return 1 if core else -1


def shards(probes, leaf_basis, up_transfer, down_transfer, coupling, far_ids):
    size_x, size_y = lax.axis_size("gx"), lax.axis_size("gy")
    both = ("gx", "gy")

    def move(value, rule):
        return lax.ppermute(value, both, route(rule, size_x, size_y))

    above = move(probes, lambda a, b: (a + 1, b))
    below = move(probes, lambda a, b: (a - 1, b))

    hbm = pl.BlockSpec(memory_space=pltpu.MemorySpace.HBM)
    whole = pl.BlockSpec(memory_space=pltpu.VMEM)
    block = (PROBES, 128)
    far_inputs = [
        pltpu.with_memory_space_constraint(value, pltpu.MemorySpace.HBM)
        for value in (far_ids, coupling, down_transfer, up_transfer, leaf_basis.T, probes)
    ]
    weight_shapes = [
        array((36 * RANK, 256)), array((36 * RANK, 128)), array((36 * RANK, 128)),
        array((24 * RANK, RANK)), array((9 * 128, 128)), array((128, 512)), array((128, 256)),
        array((RANK, 128)), array((RANK, 16 * 128)), array((2 * RANK, 4 * RANK)),
        array((8 * RANK, 4 * RANK)),
    ]
    build_scratch = [
        pltpu.SMEM(far_ids.shape, jnp.int32), pltpu.VMEM(coupling.shape, BF),
        pltpu.VMEM(down_transfer.shape, BF),
    ]
    wide, up, own, mine, low, *weights = call(
        start_kernel,
        [
            array((128, 256)), array(up_transfer.shape), array(probes.shape),
            array((2, 4) + block), array((2,) + block),
        ]
        + weight_shapes,
        in_specs=[hbm] * 6,
        scratch=build_scratch
        + [
            pltpu.VMEM(leaf_basis.shape[::-1], BF), pltpu.SemaphoreType.DMA((10,)),
            pltpu.SemaphoreType.DMA((3,)),
        ],
    )(*far_inputs)
    rim, sent = call(rim_kernel, [array((4, 4) + block), array((16, 2) + block)])(
        above, below, wide, low
    )
    gathered = lax.all_to_all(sent, "gx", 0, 0)

    pack, level2, level3_own = call(
        strip_kernel,
        [array((24,) + block), array((8,) + block), array((4, PROBES, RANK))],
        scratch=[pltpu.VMEM((20,) + block, BF), pltpu.VMEM((12,) + block, BF)],
    )(gathered, own, mine, above, below, rim, up)
    packed = move(pack, lambda a, b: (a, b ^ 1))
    far_out, side_out, level3 = call(
        second_kernel,
        [array(block), array((26,) + block), array((4,) + block)],
        scratch=[pltpu.VMEM((20,) + block, BF), pltpu.VMEM((12,) + block, BF)],
    )(packed, gathered, level2, level3_own, own, mine, above, below, rim, up)

    chips = size_y // 2
    side = move(side_out, lambda a, b: (a, b + across(b % 2)))
    third = move(level3, lambda a, b: (a, b + 3 - 6 * (b % 2)) if a == 0 else (-1, -1))
    top = move(far_out, lambda a, b: (a, 2 * ((b // 2 + a) % chips) + b % 2))

    count = len(weight_shapes)
    weights = call(
        later_kernel,
        weight_shapes,
        in_specs=[hbm] * 3 + [whole] * (3 + count),
        input_output_aliases={6 + at: at for at in range(count)},
        scratch=build_scratch + [pltpu.SemaphoreType.DMA((10,))],
    )(*far_inputs[:3], wide, up, side, *weights)
    w0, w1, w2, w3, table, down0, down1, down2, top_leaf, wt, wx = weights

    near_sum, far0, far1, far2 = call(
        third_kernel,
        [
            array((2, 8) + block, F32), array((4 * PROBES, 256), F32),
            array((2 * PROBES, 128), F32), array((PROBES, 128), F32),
        ],
        scratch=[
            pltpu.VMEM(lead + block, BF)
            for lead in ((4, 10), (6, 6), (20, 2), (6, 4), (12,), (6, 3))
        ],
    )(own, above, below, mine, packed, rim, gathered, level2, side, w0, w1, w2, table)
    partial = call(
        lower_kernel,
        array((2, 8) + block, F32),
        scratch=[pltpu.VMEM((4, 3) + block, BF)],
    )(side, level3, w3, near_sum, far0, far1, far2, down0, down1, down2, wide)
    arrived = call(arrival_kernel, array(block), flops=1 << 36)(top, partial)
    shares = call(
        share_kernel,
        array((16, PROBES // 2, 128)),
        scratch=[pltpu.VMEM((PROBES, 4 * RANK), F32)],
    )(arrived, third, wt, wx, partial)
    top = lax.all_to_all(shares, "gx", 0, 0)

    return call(fourth_kernel, array(probes.shape))(top, partial, top_leaf)


def solution(mesh):
    in_specs = (P("gx", "gy", None, None), P(), P(), P(), P(), P())
    out_specs = P("gx", "gy", None, None)
    return jax.shard_map(shards, mesh=mesh, in_specs=in_specs, out_specs=out_specs, check_vma=False)
```

```python
import jax
import jax.numpy as jnp
from jax import lax
from jax.experimental import pallas as pl
from jax.experimental.pallas import tpu as pltpu
from jax.sharding import PartitionSpec as P

LEAF_ROWS = 8
LEAF_COLS = 16
RANK = 64
PROBES = 32
BF = jnp.bfloat16
F32 = jnp.float32

length_scale = 1.5


def dot(left, right):
    return jnp.dot(left, right, preferred_element_type=F32)


def lanes(parts):
    return jnp.concatenate(parts, axis=-1)


def block_slot(e, f, wr, wc):
    return 6 * wr + wc - 3 * min(max(wr - 1 - e, 0), 3) - (
        min(max(wc - 1 - f, 0), 3) if e + 1 <= wr <= e + 3 else 0
    )


def is_near(e, f, wr, wc):
    return e + 1 <= wr <= e + 3 and f + 1 <= wc <= f + 3


def places():
    row = lax.axis_index("gx")
    col = lax.axis_index("gy")
    return row, col, col // 2, col % 2


def build_weights(
    ids_far, coupling_far, down_far, wide, up,
    w0, w1, w2, w3, table, down0, down1, down2, top_leaf, wt, wx,
    ids, coupling, down, blocks, sems,
):
    row, col, _, _ = places()
    first = pltpu.make_async_copy(ids_far, ids, sems.at[8])
    first.start()
    levels = []
    for level in range(4):
        levels.append(
            pltpu.make_async_copy(coupling_far.at[level], coupling.at[level], sems.at[level])
        )
        levels[-1].start()
    other = pltpu.make_async_copy(down_far, down, sems.at[9])
    other.start()

    size = LEAF_ROWS * LEAF_COLS
    theirs = lax.broadcasted_iota(jnp.int32, (size, size), 0)
    ours = lax.broadcasted_iota(jnp.int32, (size, size), 1)
    rows_apart = (theirs // LEAF_COLS - ours // LEAF_COLS).astype(F32)
    cols_apart = (theirs % LEAF_COLS - ours % LEAF_COLS).astype(F32)
    for u in (-1, 0, 1):
        for v in (-1, 0, 1):
            apart_row = rows_apart + float(u * LEAF_ROWS)
            apart_col = cols_apart + float(v * LEAF_COLS)
            scaled = jnp.sqrt(3.0 * (apart_row * apart_row + apart_col * apart_col)) / length_scale
            value = (1.0 + scaled) * jnp.exp(-scaled)
            table[pl.ds((3 * (u + 1) + v + 1) * size, size), :] = value.astype(BF)

    def pair(level, e, wr, wc):
        halves = []
        for f in (0, 1):
            if is_near(e, f, wr, wc):
                halves.append(jnp.zeros((RANK, RANK), BF))
            else:
                halves.append(coupling[level, ids[level, 2 * e + f, block_slot(e, f, wr, wc)]])
        return lanes(halves)

    def far_slot(e, f, wr, wc):
        row_in = jnp.logical_and(wr >= e + 1, wr <= e + 3)
        col_in = jnp.logical_and(wc >= f + 1, wc <= f + 3)
        skipped = 3 * jnp.clip(wr - 1 - e, 0, 3) + jnp.where(row_in, jnp.clip(wc - 1 - f, 0, 3), 0)
        slot = jnp.clip(6 * wr + wc - skipped, 0, 26)
        return slot, jnp.where(jnp.logical_and(row_in, col_in), 0.0, 1.0)

    def single(level, e, f, wr, wc):
        slot, keep = far_slot(e, f, wr, wc)
        block = coupling[level, ids[level, 2 * e + f, slot]]
        return block * jnp.full((RANK, RANK), keep, F32).astype(BF)

    first.wait()
    chip = col // 2
    plane = (chip - row + 16) % 16
    fetched, keeps = [], []
    for level, e, wr in ((7, 0, 2), (6, 0, 2), (5, 0, 2), (4, 0, 2), (4, 1, 2), (4, 0, 3), (4, 1, 3)):
        theirs, ours = plane // (1 << (level - 4)), chip // (1 << (level - 4))
        wc = theirs - ours + 2 + ours % 2
        inside = jnp.where(jnp.logical_and(wc >= 0, wc <= 5), 1.0, 0.0)
        slot, keep = far_slot(jnp.int32(e), ours % 2, jnp.int32(wr), jnp.clip(wc, 0, 5))
        at = len(fetched)
        picked = coupling_far.at[level, ids[level, 2 * e + ours % 2, slot]]
        fetched.append(pltpu.make_async_copy(picked, blocks.at[at], sems.at[10 + at]))
        fetched[at].start()
        keeps.append(keep * inside)
    levels[0].wait()
    for wr in range(6):
        for wc in range(6):
            at = pl.ds((6 * wr + wc) * RANK, RANK)
            for e in (0, 1):
                w0[at, pl.ds(128 * e, 128)] = pair(0, e, wr, wc)

    for level, out, bit in ((1, w1, row % 2), (2, w2, (row // 2) % 2)):
        levels[level].wait()
        for e in (0, 1):

            @pl.when(bit == e)
            def _(level=level, out=out, e=e):
                for wr in range(6):
                    for wc in range(6):
                        out[pl.ds((6 * wr + wc) * RANK, RANK), :] = pair(level, e, wr, wc)

    levels[3].wait()
    e3, f3 = (row // 4) % 2, col % 2
    first3 = 2 - 2 * (row // 8)
    for r in range(4):
        for wc in range(6):
            w3[pl.ds((6 * r + wc) * RANK, RANK), :] = single(3, e3, f3, r + first3, wc)

    @pl.when(row == 0)
    def _():
        for r in range(4):
            for k in (0, 1):
                wc = k + 4 - 4 * f3
                for p in (0, 1):
                    wx[pl.ds((2 * r + k) * RANK, RANK), pl.ds(128 * p, 128)] = lanes(
                        [single(3, e, f3, jnp.int32(r + 2 - 2 * p), wc) for e in (0, 1)]
                    )

    other.wait()
    def coupled(at):
        fetched[at].wait()
        return blocks[at].astype(F32) * jnp.full((RANK, RANK), keeps[at], F32)

    inner = coupled(0).astype(BF)
    inner = dot(dot(up[6, (plane // 4) % 2], inner).astype(BF), down[6, (chip // 4) % 2])
    inner = (inner + coupled(1)).astype(BF)
    inner = dot(dot(up[5, (plane // 2) % 2], inner).astype(BF), down[5, (chip // 2) % 2])
    inner = (inner + coupled(2)).astype(BF)
    for source in (0, 1):
        raised = dot(up[4, 2 * source + plane % 2], inner).astype(BF)
        for target in (0, 1):
            local4 = dot(raised, down[4, 2 * target + chip % 2])
            local4 = (local4 + coupled(3 + 2 * source + target)).astype(BF)
            nodes = lanes([dot(local4, down[3, 2 * e + f3]).astype(BF) for e in (0, 1)])
            wt[pl.ds(RANK * source, RANK), pl.ds(128 * target, 128)] = nodes

    all0 = lanes([down[0, k] for k in range(4)])
    none0 = jnp.zeros_like(all0)
    down0[...] = jnp.concatenate([lanes([all0, none0]), lanes([none0, all0])], axis=0)
    e1, e2 = row % 2, (row // 2) % 2
    both1 = lanes([down[1, 2 * e1], down[1, 2 * e1 + 1]])
    none1 = jnp.zeros_like(both1)
    down1[...] = jnp.concatenate([lanes([both1, none1]), lanes([none1, both1])], axis=0)
    down2[...] = lanes([down[2, 2 * e2], down[2, 2 * e2 + 1]])

    node1 = dot(down2[...], down1[...]).astype(BF)
    for t in (0, 1):
        node0 = dot(node1[:, 128 * t : 128 * t + 128], down0[...]).astype(BF)
        for q in (0, 1):
            for e in (0, 1):
                at = 256 * q + 128 * e
                leaves = dot(node0[:, at : at + 128], wide[...]).astype(BF)
                top_leaf[:, pl.ds(256 * (4 * e + 2 * t + q), 256)] = leaves


EARLY_PLANES = 7


def start_kernel(
    ids_far, coupling_far, down_far, up_far, basis_far, own_far,
    wide, up, own, mine, low,
    w0, w1, w2, w3, table, down0, down1, down2, top_leaf, wt, wx,
    ids, coupling, down, blocks, basis, sems, small_sems,
):
    _, _, chip, _ = places()
    small = [
        pltpu.make_async_copy(source, target, small_sems.at[at])
        for at, (source, target) in enumerate(((basis_far, basis), (own_far, own), (up_far, up)))
    ]
    for copy in small:
        copy.start()
    for copy in small:
        copy.wait()
    blank = jnp.zeros_like(basis)
    wide[...] = jnp.concatenate([lanes([basis[...], blank]), lanes([blank, basis[...]])], axis=0)
    coeffs = leaf_coeffs(own[...], wide[...])
    mine[...] = coeffs
    low[...] = to_pairs(raise_pairs(coeffs, up[0].reshape(4 * RANK, RANK))[0])

    @pl.when(chip < EARLY_PLANES)
    def _():
        build_weights(
            ids_far, coupling_far, down_far, wide, up,
            w0, w1, w2, w3, table, down0, down1, down2, top_leaf, wt, wx,
            ids, coupling, down, blocks, sems,
        )


def later_kernel(ids_far, coupling_far, down_far, wide, up, tag, *refs):
    _, _, chip, _ = places()
    weights, scratch = refs[11:22], refs[22:]

    @pl.when(chip >= EARLY_PLANES)
    def _():
        build_weights(ids_far, coupling_far, down_far, wide, up, *weights, *scratch)


def array(shape, kind=BF):
    return jax.ShapeDtypeStruct(shape, kind)


def call(kernel, out_shape, scratch=(), flops=1 << 24, read=1 << 21, **specs):
    return pl.pallas_call(
        kernel,
        out_shape=out_shape,
        **specs,
        scratch_shapes=list(scratch),
        compiler_params=pltpu.CompilerParams(vmem_limit_bytes=16 << 20),
        cost_estimate=pl.CostEstimate(flops=flops, bytes_accessed=read, transcendentals=0),
    )


def leaf_coeffs(tile, wide_basis):
    rows = tile.shape[0]
    split = tile.reshape(rows, 4, 2, PROBES, 128)
    joined = lanes([split[:, :, 0], split[:, :, 1]]).reshape(-1, 256)
    coeffs = lax.dot_general(
        joined, wide_basis, (((1,), (1,)), ((), ())), preferred_element_type=F32
    )
    return coeffs.astype(BF).reshape(rows, 4, PROBES, 128)


def to_pairs(nodes):
    lead = nodes.shape[:-3]
    split = nodes.reshape(lead + (nodes.shape[-3] // 2, 2, PROBES, RANK))
    return lanes([split[..., 0, :, :], split[..., 1, :, :]])


def raise_pairs(pairs, transfer):
    rows, count = pairs.shape[:2]
    split = pairs.reshape(rows // 2, 2, count, PROBES, 128)
    joined = lanes([split[:, 0], split[:, 1]]).reshape(-1, 256)
    return dot(joined, transfer).astype(BF).reshape(rows // 2, count, PROBES, RANK)


def rim_kernel(above, below, wide, low, rim, sent):
    rim[pl.ds(0, 2)] = leaf_coeffs(above[...], wide[...])
    rim[pl.ds(2, 2)] = leaf_coeffs(below[...], wide[...])
    for peer in range(16):
        sent[peer] = low[...]


def strip_kernel(gathered, own, mine, above, below, rim, up, pack, level2, level3, padded1, padded2):
    row, _, _, core = places()
    pairs2 = to_pairs(raise_pairs(gathered[...], up[1].reshape(4 * RANK, RANK)))
    level2[...] = pairs2[:, 0]
    level3[...] = raise_pairs(pairs2, up[2].reshape(4 * RANK, RANK))[:, 0]
    nothing = jnp.zeros((2, PROBES, 128), BF)
    padded1[pl.ds(0, 2)] = nothing
    padded1[pl.ds(18, 2)] = nothing
    padded2[pl.ds(0, 2)] = nothing
    padded2[pl.ds(2, 8)] = level2[...]
    padded2[pl.ds(10, 2)] = nothing
    for r in range(16):
        padded1[r + 2] = gathered[r, 1 - core]
    edge_pair = 3 - 3 * core
    edge_col = 7 - 7 * core
    pack[pl.ds(0, 6)] = padded1[pl.ds(2 * (row // 2), 6)]
    pack[pl.ds(6, 6)] = padded2[pl.ds(2 * (row // 4), 6)]
    pack[12] = lanes([level3[0], level3[1]])
    pack[13] = lanes([level3[2], level3[3]])
    pack[14] = mine[0, edge_pair]
    pack[15] = mine[1, edge_pair]
    pack[16] = own[0, edge_col]
    pack[17] = own[1, edge_col]
    pack[18] = above[1, edge_col]
    pack[19] = below[0, edge_col]
    for r in range(4):
        pack[20 + r] = rim[r, edge_pair]


def second_kernel(
    packed, gathered, level2, level3_own, own, mine, above, below, rim, up,
    far_out, side_out, level3, padded1, padded2,
):
    row, _, _, core = places()
    theirs = []
    for at in (12, 13):
        block = packed[at]
        theirs += [block[:, :RANK], block[:, RANK:]]

    @pl.when(core == 0)
    def _():
        for r in range(4):
            level3[r] = lanes([level3_own[r], theirs[r]])

    @pl.when(core == 1)
    def _():
        for r in range(4):
            level3[r] = lanes([theirs[r], level3_own[r]])

    pairs3 = level3[...]
    nodes4 = raise_pairs(pairs3[:, None], up[3].reshape(4 * RANK, RANK))
    far_out[...] = lanes([nodes4[0, 0], nodes4[1, 0]])

    edge_pair = 3 * core
    edge_col = 7 * core
    nothing = jnp.zeros((2, PROBES, 128), BF)
    padded1[pl.ds(0, 2)] = nothing
    padded1[pl.ds(18, 2)] = nothing
    padded2[pl.ds(0, 2)] = nothing
    padded2[pl.ds(2, 8)] = level2[...]
    padded2[pl.ds(10, 2)] = nothing
    for r in range(16):
        padded1[r + 2] = gathered[r, core]
    side_out[0] = above[1, edge_col]
    side_out[1] = own[0, edge_col]
    side_out[2] = own[1, edge_col]
    side_out[3] = below[0, edge_col]
    side_out[4] = rim[0, edge_pair]
    side_out[5] = rim[1, edge_pair]
    side_out[6] = mine[0, edge_pair]
    side_out[7] = mine[1, edge_pair]
    side_out[8] = rim[2, edge_pair]
    side_out[9] = rim[3, edge_pair]
    side_out[pl.ds(10, 6)] = padded1[pl.ds(2 * (row // 2), 6)]
    side_out[pl.ds(16, 6)] = padded2[pl.ds(2 * (row // 4), 6)]
    side_out[pl.ds(22, 4)] = pairs3


def third_kernel(
    own, above, below, mine, packed, rim, gathered, level2, side, w0, w1, w2, table,
    near_sum, far0, far1, far2,
    near, window0, padded1, window1, padded2, window2,
):
    row, _, _, core = places()

    window0[pl.ds(0, 2), pl.ds(1, 4)] = rim[pl.ds(0, 2)]
    window0[pl.ds(2, 2), pl.ds(1, 4)] = mine[...]
    window0[pl.ds(4, 2), pl.ds(1, 4)] = rim[pl.ds(2, 2)]
    for w in range(6):
        window0[w, 5 * core] = side[4 + w]
    for r in range(2):
        window0[r, 5 - 5 * core] = packed[20 + r]
        window0[2 + r, 5 - 5 * core] = packed[14 + r]
        window0[4 + r, 5 - 5 * core] = packed[22 + r]
    far0[...] = dot(
        lanes([window0[w, pl.ds(k, 4)].reshape(-1, 128) for w in range(6) for k in range(3)]),
        w0[...],
    )

    near[0, pl.ds(1, 8)] = above[1]
    near[1, pl.ds(1, 8)] = own[0]
    near[2, pl.ds(1, 8)] = own[1]
    near[3, pl.ds(1, 8)] = below[0]
    for r in range(4):
        near[r, 9 * core] = side[r]
    near[0, 9 - 9 * core] = packed[18]
    near[1, 9 - 9 * core] = packed[16]
    near[2, 9 - 9 * core] = packed[17]
    near[3, 9 - 9 * core] = packed[19]
    for e in (0, 1):
        joined = lanes([near[e + u, pl.ds(v, 8)].reshape(-1, 128) for u in range(3) for v in range(3)])
        near_sum[e] = dot(joined, table[...]).reshape(8, PROBES, 128)

    empty1 = jnp.zeros((2, 2, PROBES, 128), BF)
    padded1[pl.ds(0, 2)] = empty1
    padded1[pl.ds(2, 16)] = gathered[...]
    padded1[pl.ds(18, 2)] = empty1
    window1[:, pl.ds(1, 2)] = padded1[pl.ds(2 * (row // 2), 6)]
    for w in range(6):
        window1[w, 3 - 3 * core] = packed[w]
        window1[w, 3 * core] = side[10 + w]
    far1[...] = dot(
        lanes([window1[w, pl.ds(k, 2)].reshape(-1, 128) for w in range(6) for k in range(3)]),
        w1[...],
    )

    empty2 = jnp.zeros((2, PROBES, 128), BF)
    padded2[pl.ds(0, 2)] = empty2
    padded2[pl.ds(2, 8)] = level2[...]
    padded2[pl.ds(10, 2)] = empty2
    window2[:, 1] = padded2[pl.ds(2 * (row // 4), 6)]
    for w in range(6):
        window2[w, 2 - 2 * core] = packed[6 + w]
        window2[w, 2 * core] = side[16 + w]
    far2[...] = dot(lanes([window2[w, k] for w in range(6) for k in range(3)]), w2[...])


def lower_kernel(
    side, level3, w3, near_sum, far0, far1, far2, down0, down1, down2, wide, partial, window3
):
    _, _, _, core = places()
    for r in range(4):
        window3[r, 2 * core] = side[22 + r]
        window3[r, 1] = level3[r]
        window3[r, 2 - 2 * core] = jnp.zeros((PROBES, 128), BF)
    far3 = dot(lanes([window3[r, k] for r in range(4) for k in range(3)]), w3[...])
    local2 = (far2[...] + dot(far3.astype(BF), down2[...])).astype(BF)
    spread1 = dot(local2, down1[...])
    spread1 = jnp.concatenate([spread1[:, :128], spread1[:, 128:]], axis=0)
    local1 = (far1[...] + spread1).astype(BF)
    spread0 = dot(local1, down0[...]).reshape(2, PROBES, 512)
    spread0 = jnp.stack([spread0[:, :, :256], spread0[:, :, 256:]], axis=1).reshape(-1, 256)
    local0 = (far0[...] + spread0).astype(BF)
    for e in (0, 1):
        far_sum = dot(local0[:, 128 * e : 128 * e + 128], wide[...]).reshape(4, PROBES, 256)
        for q in range(4):
            for f in (0, 1):
                part = far_sum[q, :, 128 * f : 128 * f + 128]
                partial[e, 2 * q + f] = near_sum[e, 2 * q + f] + part


def arrival_kernel(block, partial, out):
    out[...] = block[...]


def share_kernel(block, third, wt, wx, partial, out, parts):
    row, _, _, _ = places()
    parts[...] = dot(block[...], wt[...])

    @pl.when(row == 0)
    def _():
        parts[...] += dot(lanes([third[r] for r in range(4)]), wx[...])

    for node in range(4):
        part = parts[:, RANK * node : RANK * node + RANK].astype(BF)
        packed = lanes([part[: PROBES // 2], part[PROBES // 2 :]])
        for peer in range(4 * node, 4 * node + 4):
            out[peer] = packed


def fourth_kernel(top, partial, top_leaf, out):
    packed = jnp.sum(top[...].astype(F32), axis=0)
    local = jnp.concatenate([packed[:, :RANK], packed[:, RANK:]], axis=0).astype(BF)
    spread = dot(local, top_leaf[...])
    for e in (0, 1):
        for c in range(8):
            at = 128 * (8 * e + c)
            out[e, c] = (partial[e, c] + spread[:, at : at + 128]).astype(BF)


def route(rule, size_x, size_y):
    pairs = []
    for a in range(size_x):
        for b in range(size_y):
            x, y = rule(a, b)
            if 0 <= x < size_x and 0 <= y < size_y:
                pairs.append((a * size_y + b, x * size_y + y))
    return pairs


def across(core):
    return 1 if core else -1


def shards(probes, leaf_basis, up_transfer, down_transfer, coupling, far_ids):
    size_x, size_y = lax.axis_size("gx"), lax.axis_size("gy")
    both = ("gx", "gy")

    def move(value, rule):
        return lax.ppermute(value, both, route(rule, size_x, size_y))

    above = move(probes, lambda a, b: (a + 1, b))
    below = move(probes, lambda a, b: (a - 1, b))

    hbm = pl.BlockSpec(memory_space=pltpu.MemorySpace.HBM)
    whole = pl.BlockSpec(memory_space=pltpu.VMEM)
    block = (PROBES, 128)
    far_inputs = [
        pltpu.with_memory_space_constraint(value, pltpu.MemorySpace.HBM)
        for value in (far_ids, coupling, down_transfer, up_transfer, leaf_basis.T, probes)
    ]
    weight_shapes = [
        array((36 * RANK, 256)), array((36 * RANK, 128)), array((36 * RANK, 128)),
        array((24 * RANK, RANK)), array((9 * 128, 128)), array((128, 512)), array((128, 256)),
        array((RANK, 128)), array((RANK, 16 * 128)), array((2 * RANK, 4 * RANK)),
        array((8 * RANK, 4 * RANK)),
    ]
    build_scratch = [
        pltpu.SMEM(far_ids.shape, jnp.int32), pltpu.VMEM((4,) + coupling.shape[1:], BF),
        pltpu.VMEM(down_transfer.shape, BF), pltpu.VMEM((7, RANK, RANK), BF),
    ]
    wide, up, own, mine, low, *weights = call(
        start_kernel,
        [
            array((128, 256)), array(up_transfer.shape), array(probes.shape),
            array((2, 4) + block), array((2,) + block),
        ]
        + weight_shapes,
        in_specs=[hbm] * 6,
        scratch=build_scratch
        + [
            pltpu.VMEM(leaf_basis.shape[::-1], BF), pltpu.SemaphoreType.DMA((17,)),
            pltpu.SemaphoreType.DMA((3,)),
        ],
    )(*far_inputs)
    rim, sent = call(rim_kernel, [array((4, 4) + block), array((16, 2) + block)])(
        above, below, wide, low
    )
    gathered = lax.all_to_all(sent, "gx", 0, 0)

    pack, level2, level3_own = call(
        strip_kernel,
        [array((24,) + block), array((8,) + block), array((4, PROBES, RANK))],
        scratch=[pltpu.VMEM((20,) + block, BF), pltpu.VMEM((12,) + block, BF)],
    )(gathered, own, mine, above, below, rim, up)
    packed = move(pack, lambda a, b: (a, b ^ 1))
    far_out, side_out, level3 = call(
        second_kernel,
        [array(block), array((26,) + block), array((4,) + block)],
        scratch=[pltpu.VMEM((20,) + block, BF), pltpu.VMEM((12,) + block, BF)],
    )(packed, gathered, level2, level3_own, own, mine, above, below, rim, up)

    chips = size_y // 2
    side = move(side_out, lambda a, b: (a, b + across(b % 2)))
    third = move(level3, lambda a, b: (a, b + 3 - 6 * (b % 2)) if a == 0 else (-1, -1))
    top = move(far_out, lambda a, b: (a, 2 * ((b // 2 + a) % chips) + b % 2))

    count = len(weight_shapes)
    weights = call(
        later_kernel,
        weight_shapes,
        in_specs=[hbm] * 3 + [whole] * (3 + count),
        input_output_aliases={6 + at: at for at in range(count)},
        scratch=build_scratch + [pltpu.SemaphoreType.DMA((17,))],
    )(*far_inputs[:3], wide, up, side, *weights)
    w0, w1, w2, w3, table, down0, down1, down2, top_leaf, wt, wx = weights

    near_sum, far0, far1, far2 = call(
        third_kernel,
        [
            array((2, 8) + block, F32), array((4 * PROBES, 256), F32),
            array((2 * PROBES, 128), F32), array((PROBES, 128), F32),
        ],
        scratch=[
            pltpu.VMEM(lead + block, BF)
            for lead in ((4, 10), (6, 6), (20, 2), (6, 4), (12,), (6, 3))
        ],
    )(own, above, below, mine, packed, rim, gathered, level2, side, w0, w1, w2, table)
    partial = call(
        lower_kernel,
        array((2, 8) + block, F32),
        scratch=[pltpu.VMEM((4, 3) + block, BF)],
    )(side, level3, w3, near_sum, far0, far1, far2, down0, down1, down2, wide)
    arrived = call(arrival_kernel, array(block), flops=1 << 36)(top, partial)
    shares = call(
        share_kernel,
        array((16, PROBES // 2, 128)),
        scratch=[pltpu.VMEM((PROBES, 4 * RANK), F32)],
    )(arrived, third, wt, wx, partial)
    top = lax.all_to_all(shares, "gx", 0, 0)

    return call(fourth_kernel, array(probes.shape))(top, partial, top_leaf)


def solution(mesh):
    in_specs = (P("gx", "gy", None, None), P(), P(), P(), P(), P())
    out_specs = P("gx", "gy", None, None)
    return jax.shard_map(shards, mesh=mesh, in_specs=in_specs, out_specs=out_specs, check_vma=False)
```
